128 devices in a mesh: dp: 2 (over core), context: 16 (over y, x), tensor: 4 (over z).
Axes of the slice: x: 4, y: 4, z: 4, core: 2. Of those that a mesh axis runs over, the one named last changes fastest.
Arguments:
- ids: int32 [16384], P(('dp', 'context', 'tensor')), parts along dimension 0, may hold values from 65 to 84, as said below
- block_order: int32 [64], P('dp'), parts along dimension 0, may hold values from 0 to 31, each once
- embed: bfloat16 [512, 4096], replicated, may hold values from -6 to 6
- mix_gain: float32 [4096], replicated, may hold values from 0.5 to 2
- in_proj: bfloat16 [3, 4096, 2048], P(None, None, 'tensor'), may hold values from -0.09375 to 0.09375
- short_filter: float32 [3, 3, 2048], P(None, None, 'tensor'), may hold values from -1 to 1
- long_filter: float32 [128, 128], P('tensor'), as said below
- conv_skip: float32 [2048], P('tensor'), may hold values from -1 to 1
- hyena_out: bfloat16 [2048, 4096], P('tensor'), may hold values from -0.125 to 0.125
- attn_gain: float32 [4096], replicated, may hold values from 0.5 to 2
- qkv_proj: bfloat16 [3, 4096, 2048], P(None, None, 'tensor'), as said below
- attn_out: bfloat16 [2048, 4096], P('tensor'), may hold values from -0.5 to 0.5
Outputs:
- stream_out: float32 [16384, 4096], P(('dp', 'context', 'tensor')), parts along dimension 0
The draws below stay inside these ranges and needn't reach their ends.
There are 2 independent parts, one for each index of `dp`. The reference program is written for one: setup_inputs(seed, part) draws one part's arguments, and reference() takes and returns one part's arrays. A program takes and returns all parts, laid end to end along the dimension named above; an argument that names none is the same for every part. Nothing has to cross between parts.
Inputs may be any that keep to these rules, and one draw needn't show every extreme that they name: `ids`: every id is the code of a base: 65, 67, 71 or 84. `block_order`: every block lies in exactly one slot. `long_filter`: real-valued filter taps. `qkv_proj`: real-valued projection weights.
All inputs are finite; a program needn't handle non-finite values.
Results may differ from the reference program's by a relative error of at most 0.01.
Values may be sent and summed in bfloat16 or wider, within the bound.
A program may use at most 192 MiB of HBM per device.

```python
import math
import jax
import jax.numpy as jnp
from jax import lax

D = 4096
VOCAB = 512
HEADS = 16
HD = 128
CH = 2048
GROUP_CH = 16
FILT = 128
SHORT = 3
BLK = 256
BLOCKS = 32
SEQ = 8192
GROUPS = 128


def draw_ids(key, part):
    codes = jnp.array([65, 67, 71, 84], dtype=jnp.int32)
    picks = jax.random.randint(key, (SEQ,), 0, 4)
    slots = jnp.arange(SEQ, dtype=jnp.int32)
    picks = jnp.where(slots < 2, slots * 3, picks)
    return jnp.take(codes, picks)


def draw_long_filter(key, part):
    rate_key, tap_key = jax.random.split(key, 2)
    low_rate, high_rate = (0.001, 0.05)
    rates = jnp.exp(jax.random.uniform(rate_key, (GROUPS, 1), jnp.float32, math.log(low_rate), math.log(high_rate)))
    taps = jnp.arange(FILT, dtype=jnp.float32)[None, :]
    scaling = jnp.sqrt((1.0 - jnp.exp(-2.0 * rates)) / (1.0 - jnp.exp(-2.0 * rates * FILT)))
    rough = jnp.clip(jax.random.normal(tap_key, (GROUPS, FILT), jnp.float32), -4.0, 4.0)
    return rough * jnp.exp(-rates * taps) * scaling


def draw_qkv_proj(key, part):
    base = jnp.clip(jax.random.normal(key, (3, D, HEADS * HD), jnp.float32), -5.0, 5.0) / math.sqrt(D)
    queries = 1.6 * base[0]
    keys = base[1]
    return jnp.stack([queries, keys, base[2]]).astype(jnp.bfloat16)


def block_levels(key, dims, cuts, low, largest):
    def one(dim, parts):
        steps = jax.random.uniform(jax.random.fold_in(jax.random.fold_in(key, 6), dim), (parts,), jnp.float32, low / len(cuts), largest / len(cuts))
        return jnp.repeat(jnp.exp(steps), dims[dim] // parts).reshape((-1,) + (1,) * (len(dims) - dim - 1))

    loudness = one(*cuts[0])
    for cut in cuts[1:]:
        loudness = loudness * one(*cut)
    return loudness


def noise(stream_key, shape, deviation, bound, shards=(), held_as=jnp.bfloat16):
    values = jax.random.normal(stream_key, shape, jnp.float32) * deviation
    if len(shards) > 0:
        values = block_levels(stream_key, shape, shards, -0.22, 0.18) * values
    return jnp.clip(values, min=-bound, max=bound).astype(held_as)


def setup_inputs(seed: int = 0, part: int = 0) -> dict:
    key_list = jax.random.split(jax.random.key(seed), 13)
    part_splits = jax.random.split(jax.random.fold_in(key_list[12], part), 13)
    return {
        "ids": draw_ids(jax.random.fold_in(jax.random.fold_in(key_list[12], part), 71), part),
        "block_order": jax.random.permutation(part_splits[1], BLOCKS).astype(jnp.int32),
        "embed": noise(key_list[2], (VOCAB, D), 1.0, 6.0),
        "mix_gain": jnp.clip(jnp.exp(jax.random.uniform(key_list[3], (D,), jnp.float32, math.log(0.5), math.log(2.0))), 0.5, 2.0),
        "in_proj": noise(key_list[4], (3, D, CH), D ** -0.5, 0.09375, ((2, 4),)),
        "short_filter": jnp.clip(jax.random.uniform(key_list[5], (3, SHORT, CH), jnp.float32, -1.0, 1.0) * block_levels(key_list[5], (3, SHORT, CH), ((2, 4),), -0.4, 0.0), -1.0, 1.0),
        "long_filter": draw_long_filter(jax.random.fold_in(key_list[12], 71), part),
        "conv_skip": jnp.clip(jax.random.uniform(key_list[7], (CH,), jnp.float32, -1.0, 1.0) * block_levels(key_list[7], (CH,), ((0, 4),), -0.4, 0.0), -1.0, 1.0),
        "hyena_out": noise(key_list[8], (CH, D), CH ** -0.5, 0.125, ((0, 4),)),
        "attn_gain": jnp.clip(jnp.exp(jax.random.uniform(key_list[9], (D,), jnp.float32, math.log(0.5), math.log(2.0))), 0.5, 2.0),
        "qkv_proj": draw_qkv_proj(jax.random.fold_in(key_list[12], 71), part),
        "attn_out": noise(key_list[11], (HEADS * HD, D), HD ** -0.5, 0.5, ((0, 4),)),
    }


EPS = 1e-06
THETA = 1000000.0
NEG_FILL = -1e+30

def rms_scale(row_data, gain_vec):
    values = row_data.astype(jnp.float32)
    factor = lax.rsqrt(lax.optimization_barrier(jnp.mean(values * values, axis=-1, keepdims=True)) + EPS)
    return (values * factor * gain_vec).astype(jnp.bfloat16)

def toeplitz(long_filter):
    filter_len = long_filter.shape[1]
    tap_lag = jnp.arange(filter_len, dtype=jnp.int32)[:, None] - jnp.arange(filter_len, dtype=jnp.int32)[None, :]
    near_taps = jnp.take(long_filter, jnp.clip(tap_lag, 0, filter_len - 1), axis=1)
    far_taps = jnp.take(long_filter, jnp.clip(tap_lag + filter_len, 0, filter_len - 1), axis=1)
    near_taps = jnp.where(tap_lag[None] >= 0, near_taps, jnp.zeros_like(near_taps))
    far_taps = jnp.where(tap_lag[None] < 0, far_taps, jnp.zeros_like(far_taps))
    return (near_taps, far_taps)

def long_conv(padded, long_filter, group_width):
    filter_len = long_filter.shape[1]
    near_taps, far_taps = toeplitz(long_filter)
    row_total = padded.shape[0]
    chan_total = padded.shape[1]
    blocks = padded.reshape(row_total // filter_len, filter_len, chan_total // group_width, group_width)
    current_part = jnp.einsum('grs,bsgc->brgc', near_taps, blocks[1:], precision=lax.Precision.HIGHEST)
    before = jnp.einsum('grs,bsgc->brgc', far_taps, blocks[:-1], precision=lax.Precision.HIGHEST)
    return (current_part + before).reshape(row_total - filter_len, chan_total)

def short_conv(padded_rows, short_filter, out_len):
    taps = short_filter.shape[1]
    result = jnp.zeros((padded_rows.shape[0], out_len, padded_rows.shape[2]), jnp.float32)
    for tap_at in range(taps):
        offset = taps - 1 - tap_at
        result = result + short_filter[:, tap_at][:, None, :] * padded_rows[:, offset:offset + out_len]
    return result

def rotate(values, positions, head_dim):
    half_dim = head_dim // 2
    inverse_freq = THETA ** (-(2.0 * jnp.arange(half_dim, dtype=jnp.float32)) / head_dim)
    angles = positions.astype(jnp.float32)[:, None] * inverse_freq[None, :]
    cosine_part = jnp.cos(angles)[:, None, :]
    sine_part = jnp.sin(angles)[:, None, :]
    lower_half = values[..., :half_dim]
    upper_half = values[..., half_dim:]
    return jnp.concatenate([lower_half * cosine_part - upper_half * sine_part, upper_half * cosine_part + lower_half * sine_part], axis=-1)

def reference(ids, block_order, embed, mix_gain, in_proj, short_filter, long_filter, conv_skip, hyena_out, attn_gain, qkv_proj, attn_out):
    row_index = jnp.arange(SEQ, dtype=jnp.int32)
    positions = (block_order[row_index // BLK] * BLK + row_index % BLK).astype(jnp.int32)
    ids_true = jnp.zeros((SEQ,), jnp.int32).at[positions].set(ids)
    embedded = embed[ids_true]
    mixed_in = rms_scale(embedded, mix_gain)
    projected = jnp.stack([jnp.dot(mixed_in, in_proj[part_at], preferred_element_type=jnp.float32) for part_at in range(3)]).astype(jnp.bfloat16)
    padded_rows = jnp.concatenate([jnp.zeros((3, SHORT - 1, CH), jnp.float32), projected.astype(jnp.float32)], axis=1)
    filtered = short_conv(padded_rows, short_filter, SEQ)
    gated = filtered[1] * filtered[2]
    padded = jnp.concatenate([jnp.zeros((FILT, CH), jnp.float32), gated], axis=0)
    long_mix = long_conv(padded, long_filter, GROUP_CH)
    hyena_mix = (filtered[0] * (long_mix + conv_skip * gated)).astype(jnp.bfloat16)
    hyena_branch = jnp.dot(hyena_mix, hyena_out, preferred_element_type=jnp.float32)
    stream_mid = embedded.astype(jnp.float32) + hyena_branch
    attn_in = rms_scale(stream_mid, attn_gain)
    projections = [jnp.dot(attn_in, qkv_proj[part_at], preferred_element_type=jnp.float32).reshape(SEQ, HEADS, HD) for part_at in range(3)]
    queries = rotate(projections[0], row_index, HD).astype(jnp.bfloat16)
    keys = rotate(projections[1], row_index, HD).astype(jnp.bfloat16)
    values = projections[2].astype(jnp.bfloat16)

    def head_attend(operands):
        head_q, head_k, head_v = operands
        keys_wide = head_k.astype(jnp.float32)

        def block_attend(row_start):
            query_rows = lax.dynamic_slice_in_dim(head_q, row_start, BLK, 0).astype(jnp.float32)
            scores = jnp.dot(query_rows, keys_wide.T, preferred_element_type=jnp.float32) * HD ** (-0.5)
            query_pos = row_start + jnp.arange(BLK, dtype=jnp.int32)
            visible = jnp.arange(SEQ, dtype=jnp.int32)[None, :] <= query_pos[:, None]
            scores = jnp.where(visible, scores, NEG_FILL)
            top_score = lax.optimization_barrier(jnp.max(scores, axis=-1, keepdims=True))
            weights = jnp.where(visible, jnp.exp(scores - top_score), 0.0)
            totals = lax.optimization_barrier(jnp.sum(weights, axis=-1, keepdims=True))
            mixed = jnp.dot(weights.astype(jnp.bfloat16), head_v, preferred_element_type=jnp.float32)
            return (mixed / totals).astype(jnp.bfloat16)
        starts = jnp.arange(SEQ // BLK, dtype=jnp.int32) * BLK
        return lax.map(block_attend, starts).reshape(SEQ, HD)
    attended = lax.map(head_attend, (queries.transpose(1, 0, 2), keys.transpose(1, 0, 2), values.transpose(1, 0, 2)))
    attended = attended.transpose(1, 0, 2).reshape(SEQ, HEADS * HD)
    attn_branch = jnp.dot(attended, attn_out, preferred_element_type=jnp.float32)
    stream_true = stream_mid + attn_branch
    return stream_true[positions]
```

```python
import functools
import math

import jax
import jax.numpy as jnp
from jax import lax
from jax.experimental import pallas as pl
from jax.experimental.pallas import tpu as pltpu
from jax.sharding import PartitionSpec as P

HD = 128
EPS = 1e-06
THETA = 1000000.0
NEG_FILL = -1e30
CODES = (65, 67, 71, 84)
MESH_ID = pl.DeviceIdType.MESH
F32 = jnp.float32
BF16 = jnp.bfloat16
ANY = pl.BlockSpec(memory_space=pl.ANY)


def coords():
    dp = lax.axis_index("dp")
    ctx = lax.axis_index("context")
    t = lax.axis_index("tensor")
    return dp, ctx // 4, ctx % 4, t


def pick(dp, first, second):
    return first + dp * (second - first)


def remote(src, dst, send, recv, where):
    return pltpu.make_async_remote_copy(
        src_ref=src, dst_ref=dst, send_sem=send, recv_sem=recv, device_id=where, device_id_type=MESH_ID
    )


ZKINDS = ((3, 0), (3, 1), (1, 0), (1, 1), (2, 0), (2, 1))


class WeightGather:
    def __init__(self, w_in, w_out, send, recv, local_sem):
        self.w_in, self.w_out, self.send, self.recv, self.local_sem = w_in, w_out, send, recv, local_sem
        dp, y, x, t = coords()
        self.dp, self.t = dp, t
        u, w = pick(dp, x, y), pick(dp, y, x)
        self.q = (u + 2 * w) % 4
        self.sib_q = (w + 2 * u) % 4
        self.shard = w_in.shape[0]
        self.piece = self.shard // 16
        xp, xm, yp, ym = (x + 1) % 4, (x + 3) % 4, (y + 1) % 4, (y + 3) % 4
        self.up = {"context": pick(dp, y * 4 + xp, yp * 4 + x)}
        self.um = {"context": pick(dp, y * 4 + xm, ym * 4 + x)}
        self.wp = {"context": pick(dp, yp * 4 + x, y * 4 + xp)}
        self.wm = {"context": pick(dp, ym * 4 + x, y * 4 + xm)}
        self.zp = {"tensor": (t + 1) % 4}
        self.zm = {"tensor": (t + 3) % 4}
        self.sib = {"dp": 1 - dp}
        self.pending = []

    def unit(self, z, dp, q, h):
        start = z * self.shard + dp * (self.shard // 2) + q * (2 * self.piece) + h * self.piece
        return self.w_out.at[pl.ds(pl.multiple_of(start, self.piece), self.piece), :]

    def own(self, h):
        start = self.dp * (self.shard // 2) + self.q * (2 * self.piece) + h * self.piece
        return self.w_in.at[pl.ds(pl.multiple_of(start, self.piece), self.piece), :]

    def go(self, src, dst, recv_at, where):
        at = len(self.pending)
        copy = remote(src, dst, self.send.at[at], self.recv.at[recv_at], where)
        copy.start()
        self.pending.append(copy)

    def arrived(self, dst, recv_at):
        remote(dst, dst, self.send.at[0], self.recv.at[recv_at], self.sib).wait_recv()

    def start(self):
        row = pl.multiple_of(self.t * self.shard, self.shard)
        self.local = pltpu.make_async_copy(self.w_in, self.w_out.at[pl.ds(row, self.shard), :], self.local_sem)
        self.local.start()
        for h in (0, 1):
            dst = self.unit(self.t, self.dp, self.q, h)
            first, second = ((self.zp, 0 + h), (self.zm, 2 + h))
            if h == 0:
                self.go(self.own(h), dst, first[1], first[0])
                self.go(self.own(1), self.unit(self.t, self.dp, self.q, 1), 3, self.zm)
            else:
                self.go(self.own(1), dst, 1, self.zp)
                self.go(self.own(0), self.unit(self.t, self.dp, self.q, 0), 2, self.zm)

    def z_step(self, kind):
        zoff, h = ZKINDS[kind]
        ref = self.unit((self.t + zoff) % 4, self.dp, self.q, h)
        self.arrived(ref, kind)
        if kind == 0:
            self.go(ref, ref, 4, self.zp)
        if kind == 3:
            self.go(ref, ref, 5, self.zm)
        self.go(ref, ref, 6 + kind, self.up)
        self.go(ref, ref, 12 + kind, self.um)
        self.go(ref, ref, 18 + kind, self.wp if h == 0 else self.wm)
        self.go(ref, ref, 24 + kind, self.sib)

    def plane_ref(self, side, kind, dp, q):
        zoff, h = ZKINDS[kind]
        qoff = (3, 1, 2)[side]
        return self.unit((self.t + zoff) % 4, dp, (q + qoff) % 4, h)

    def plane_step(self, side, kind):
        at = 6 + 6 * side + kind
        ref = self.plane_ref(side, kind, self.dp, self.q)
        self.arrived(ref, at)
        self.go(ref, ref, 24 + at, self.sib)

    def finish(self):
        for kind in range(6):
            zoff, h = ZKINDS[kind]
            self.arrived(self.unit((self.t + zoff) % 4, 1 - self.dp, self.sib_q, h), 24 + kind)
            for side in range(3):
                self.arrived(self.plane_ref(side, kind, 1 - self.dp, self.sib_q), 30 + 6 * side + kind)
        for copy in self.pending:
            copy.wait_send()
        self.local.wait()


KIND_ORDER = (0, 3, 1, 2, 4, 5)
N_SENDS = 6 + 18 + 24


def gather_kernel(ids_ref, pack_ref, wh_ref, wa_ref, ids_out, pack_out, wh_out, wa_out,
                  sh, rh, sa, ra, s_ids, r_ids, s_pack, r_pack, loc):
    dp, y, x, t = coords()
    ctx = y * 4 + x
    barrier = pltpu.get_barrier_semaphore()
    partners = (
        [{"tensor": (t + d) % 4} for d in (1, 2, 3)]
        + [{"context": y * 4 + (x + d) % 4} for d in (1, 2, 3)]
        + [{"context": ((y + d) % 4) * 4 + x} for d in (1, 2, 3)]
        + [{"dp": 1 - dp}]
    )
    for where in partners:
        pl.semaphore_signal(barrier, inc=1, device_id=where, device_id_type=MESH_ID)
    pl.semaphore_wait(barrier, len(partners))

    small = []
    mine = ctx * 4 + t
    keep_ids = pltpu.make_async_copy(ids_ref, ids_out.at[pl.ds(mine, 1)], loc.at[2])
    keep_ids.start()
    keep_pack = pltpu.make_async_copy(pack_ref, pack_out.at[t], loc.at[3])
    keep_pack.start()
    for d in (1, 2, 3):
        c = remote(ids_ref, ids_out.at[pl.ds(mine, 1)], s_ids.at[d - 1], r_ids.at[d - 1], partners[d - 1])
        c.start()
        small.append(c)
        c = remote(pack_ref, pack_out.at[t], s_pack.at[d - 1], r_pack.at[d - 1], partners[d - 1])
        c.start()
        small.append(c)
    gh = WeightGather(wh_ref, wh_out, sh, rh, loc.at[0])
    ga = WeightGather(wa_ref, wa_out, sa, ra, loc.at[1])
    gh.start()
    keep_ids.wait()
    for d in (1, 2, 3):
        ref = ids_out.at[pl.ds(ctx * 4 + (t + 4 - d) % 4, 1)]
        remote(ref, ref, s_ids.at[0], r_ids.at[d - 1], partners[0]).wait_recv()
    row = ids_out.at[pl.ds(ctx * 4, 4)]
    for d in (1, 2, 3):
        c = remote(row, row, s_ids.at[2 + d], r_ids.at[2 + d], partners[2 + d])
        c.start()
        small.append(c)
    for d in (1, 2, 3):
        ref = ids_out.at[pl.ds((y * 4 + (x + 4 - d) % 4) * 4, 4)]
        remote(ref, ref, s_ids.at[0], r_ids.at[2 + d], partners[0]).wait_recv()
    row = ids_out.at[pl.ds(y * 16, 16)]
    for d in (1, 2, 3):
        c = remote(row, row, s_ids.at[5 + d], r_ids.at[5 + d], partners[5 + d])
        c.start()
        small.append(c)
    for k in KIND_ORDER:
        gh.z_step(k)
    ga.start()
    for k in KIND_ORDER:
        for side in range(3):
            gh.plane_step(side, k)
    for k in KIND_ORDER:
        ga.z_step(k)
    gh.finish()
    for k in KIND_ORDER:
        for side in range(3):
            ga.plane_step(side, k)
    ga.finish()
    for d in (1, 2, 3):
        ref = ids_out.at[pl.ds(((y + 4 - d) % 4) * 16, 16)]
        remote(ref, ref, s_ids.at[0], r_ids.at[5 + d], partners[0]).wait_recv()
        ref = pack_out.at[(t + 4 - d) % 4]
        remote(ref, ref, s_ids.at[0], r_pack.at[d - 1], partners[0]).wait_recv()
    for c in small:
        c.wait_send()
    keep_pack.wait()


def gather_all(ids, pack, wh, wa):
    dma = pltpu.SemaphoreType.DMA
    return pl.pallas_call(
        gather_kernel,
        out_shape=(
            jax.ShapeDtypeStruct((64, 1, 128), jnp.int32),
            jax.ShapeDtypeStruct((4,) + pack.shape, F32),
            jax.ShapeDtypeStruct((2048, 4096), BF16),
            jax.ShapeDtypeStruct((2048, 4096), BF16),
        ),
        in_specs=[ANY] * 4,
        out_specs=(ANY,) * 4,
        scratch_shapes=[
            dma((N_SENDS,)), dma((48,)), dma((N_SENDS,)), dma((48,)),
            dma((9,)), dma((9,)), dma((3,)), dma((3,)), dma((4,)),
        ],
        compiler_params=pltpu.CompilerParams(collective_id=0, has_side_effects=True),
        name="gather_all",
    )(ids, pack, wh, wa)


def mix_kernel(onehot_ref, tab_ref, taps_ref, skip_ref, out_ref):
    table = jnp.concatenate([tab_ref[0], tab_ref[1], tab_ref[2]], axis=1)
    high = table.astype(BF16)
    low = (table - high.astype(F32)).astype(BF16)
    both = jnp.concatenate([high, low], axis=0)
    filtered = jnp.dot(onehot_ref[...], both, preferred_element_type=F32)
    gated = filtered[:, 128:256] * filtered[:, 256:384]
    g16 = gated.astype(BF16)
    window = jnp.concatenate(
        [g16[b * 384 + s * 128 : b * 384 + s * 128 + 256] for b in range(2) for s in range(2)], axis=1
    )
    lane_group = (lax.broadcasted_iota(jnp.int32, window.shape, 1) % 128) // 16
    total = jnp.zeros((128, 512), F32)
    for g in range(8):
        base = jnp.broadcast_to(taps_ref[g : g + 1, :], (128, 256))
        toep = pltpu.roll(base, 0, 1, stride=1, stride_axis=0).astype(BF16)
        masked = jnp.where(lane_group == g, window, jnp.zeros_like(window))
        total = total + jnp.dot(toep, masked, preferred_element_type=F32)
    for b in range(2):
        for s in range(2):
            at = b * 384 + 128 + s * 128
            part = total[:, (2 * b + s) * 128 : (2 * b + s + 1) * 128]
            mixed = filtered[at : at + 128, 0:128] * (part + skip_ref[...] * gated[at : at + 128])
            out_ref[b * 256 + s * 128 : b * 256 + (s + 1) * 128, :] = mixed.astype(BF16)


def hyena_mix(onehot, tab, taps, skip):
    return pl.pallas_call(
        mix_kernel,
        out_shape=jax.ShapeDtypeStruct((512, 2048), BF16),
        grid=(16,),
        in_specs=[
            pl.BlockSpec((768, 32), lambda i: (0, 0)),
            pl.BlockSpec((3, 16, 128), lambda i: (0, 0, i)),
            pl.BlockSpec((8, 256), lambda i: (i, 0)),
            pl.BlockSpec((1, 128), lambda i: (0, i)),
        ],
        out_specs=pl.BlockSpec((512, 128), lambda i: (0, i)),
        compiler_params=pltpu.CompilerParams(vmem_limit_bytes=40 * 2**20),
        name="hyena_mix",
    )(onehot, tab, taps, skip)


def proj_kernel(t_ref, mix_ref, wh_ref, code_ref, emb_ref, gain_ref, wq_ref, cos_ref, sin_ref,
                own_ref, qkv_ref, attn_in, chunk, squares):
    i = pl.program_id(0)

    @pl.when(i < 8)
    def _():
        vals = jnp.dot(mix_ref[...], wh_ref[...], preferred_element_type=F32)
        vals = vals + jnp.dot(code_ref[...], emb_ref[...], preferred_element_type=F32)
        chunk[...] = vals
        part = jnp.sum(vals * vals, axis=1, keepdims=True)

        @pl.when(i == 0)
        def _():
            squares[...] = jnp.zeros_like(squares)

        squares[...] += jnp.broadcast_to(part, squares.shape)
        attn_in[:, pl.ds(pl.multiple_of(i * 512, 512), 512)] = (vals * gain_ref[...]).astype(BF16)
        own_ref[...] = chunk[pl.ds(pl.multiple_of(t_ref[0] * 128, 128), 128), :]

    @pl.when(i >= 8)
    def _():
        k = i - 8
        j = k // 2
        factor = lax.rsqrt(squares[...] / 4096.0 + EPS)
        factor = factor * jnp.where(j == 0, HD**-0.5 * math.log2(math.e), 1.0).astype(F32)
        rotated = j < 2
        cos = jnp.where(rotated, cos_ref[...], 1.0) * factor
        sin = jnp.where(rotated, sin_ref[...], 0.0) * factor
        vals = jnp.dot(attn_in[...], wq_ref[0], preferred_element_type=F32)
        for hh in range(2):
            head = vals[:, hh * 128 : (hh + 1) * 128]
            turned = head * cos + pltpu.roll(head, 64, 1) * sin
            qkv_ref[2 * (k % 2) + hh, j] = turned.astype(BF16).reshape(2, 4, 64, 128)


def stream_qkv(t_arr, mix, wh, code_hot, emb4, gain, wq, cos, sin):
    def whi(i, t):
        return (0, jnp.minimum(i, 7))

    def wqi(i, t):
        k = jnp.maximum(i - 8, 0)
        return (k // 2, 0, k % 2)

    def whole(*shape):
        return pl.BlockSpec(shape, lambda i, t: (0,) * len(shape))

    return pl.pallas_call(
        proj_kernel,
        out_shape=(
            jax.ShapeDtypeStruct((128, 4096), F32),
            jax.ShapeDtypeStruct((4, 3, 2, 4, 64, 128), BF16),
        ),
        grid_spec=pltpu.PrefetchScalarGridSpec(
            num_scalar_prefetch=1,
            grid=(14,),
            in_specs=[
                whole(512, 2048),
                pl.BlockSpec((2048, 512), whi),
                whole(512, 16),
                pl.BlockSpec((16, 512), whi),
                pl.BlockSpec((1, 512), whi),
                pl.BlockSpec((1, 4096, 256), wqi),
                whole(512, 128),
                whole(512, 128),
            ],
            out_specs=(
                pl.BlockSpec((128, 512), whi),
                whole(4, 3, 2, 4, 64, 128),
            ),
            scratch_shapes=[
                pltpu.VMEM((512, 4096), BF16),
                pltpu.VMEM((512, 512), F32),
                pltpu.VMEM((512, 128), F32),
            ],
        ),
        compiler_params=pltpu.CompilerParams(vmem_limit_bytes=48 * 2**20),
        name="stream_qkv",
    )(t_arr, mix, wh, code_hot, emb4, gain, wq, cos, sin)


def ab_of(dp, y, x):
    return pick(dp, y, x), pick(dp, x, y)


def ctx_of(dp, a, b):
    return pick(dp, a * 4 + b, b * 4 + a)


def exchange_kernel(qkv_ref, q_out, kv_out, sq, rq, s1, r1, s2, r2, s3, r3, loc):
    dp, y, x, t = coords()
    ctx = y * 4 + x
    a, b = ab_of(dp, y, x)
    barrier = pltpu.get_barrier_semaphore()
    others = [{"context": (ctx + d) % 16} for d in range(1, 16)]
    for where in others:
        pl.semaphore_signal(barrier, inc=1, device_id=where, device_id_type=MESH_ID)
    pl.semaphore_wait(barrier, 15)
    sent = []
    keep_kv = pltpu.make_async_copy(qkv_ref.at[a, pl.ds(1, 2)], kv_out.at[ctx], loc.at[0])
    keep_kv.start()
    bp = {"context": ctx_of(dp, a, (b + 1) % 4)}
    bm = {"context": ctx_of(dp, a, (b + 3) % 4)}

    def spread(src, k, src_ctx):
        for side, where in ((0, bp), (1, bm)):
            c = remote(src, kv_out.at[src_ctx], s2.at[side * 4 + k], r2.at[side * 4 + k], where)
            c.start()
            sent.append(c)

    for d in (1, 3, 2):
        h = (a + d) % 4
        c = remote(qkv_ref.at[h, pl.ds(1, 2)], kv_out.at[ctx], s1.at[d - 1], r1.at[d - 1], {"context": ctx_of(dp, h, b)})
        c.start()
        sent.append(c)
    spread(qkv_ref.at[a, pl.ds(1, 2)], 0, ctx)
    for d in range(1, 16):
        to = (ctx + d) % 16
        h, s = ab_of(dp, to // 4, to % 4)
        c = remote(qkv_ref.at[h, 0, :, s], q_out.at[ctx], sq.at[d - 1], rq.at[d - 1], others[d - 1])
        c.start()
        sent.append(c)
    keep_q = pltpu.make_async_copy(qkv_ref.at[a, 0, :, b], q_out.at[ctx], loc.at[1])
    keep_q.start()
    for d in (1, 3, 2):
        from_ctx = ctx_of(dp, (a + 4 - d) % 4, b)
        ref = kv_out.at[from_ctx]
        remote(ref, ref, s1.at[0], r1.at[d - 1], bp).wait_recv()
        spread(ref, d, from_ctx)
    for k in (0, 1, 3, 2):
        ua = (a + 4 - k) % 4
        ref = kv_out.at[ctx_of(dp, ua, (b + 3) % 4)]
        remote(ref, ref, s1.at[0], r2.at[k], bp).wait_recv()
        c = remote(ref.at[0], ref.at[0], s3.at[k], r3.at[k], bp)
        c.start()
        sent.append(c)
        ref = kv_out.at[ctx_of(dp, ua, (b + 1) % 4)]
        remote(ref, ref, s1.at[0], r2.at[4 + k], bp).wait_recv()
        c = remote(ref.at[1], ref.at[1], s3.at[4 + k], r3.at[4 + k], bm)
        c.start()
        sent.append(c)
    for k in (0, 1, 3, 2):
        ref = kv_out.at[ctx_of(dp, (a + 4 - k) % 4, (b + 2) % 4)]
        for part in (0, 1):
            remote(ref.at[part], ref.at[part], s1.at[0], r3.at[4 * part + k], bp).wait_recv()
    for d in range(1, 16):
        ref = q_out.at[(ctx + 16 - d) % 16]
        remote(ref, ref, s1.at[0], rq.at[d - 1], bp).wait_recv()
    for c in sent:
        c.wait_send()
    keep_q.wait()
    keep_kv.wait()


def exchange(qkv):
    dma = pltpu.SemaphoreType.DMA
    return pl.pallas_call(
        exchange_kernel,
        out_shape=(
            jax.ShapeDtypeStruct((16, 2, 64, 128), BF16),
            jax.ShapeDtypeStruct((16, 2, 2, 4, 64, 128), BF16),
        ),
        in_specs=[ANY],
        out_specs=(ANY,) * 2,
        scratch_shapes=[dma((15,)), dma((15,)), dma((3,)), dma((3,)), dma((8,)), dma((8,)), dma((8,)), dma((8,)), dma((2,))],
        compiler_params=pltpu.CompilerParams(collective_id=1, has_side_effects=True),
        name="exchange",
    )(qkv)


KEYS = 1024


def attend_kernel(slot_ref, q_hbm, kv_hbm, o_hbm, q_s, k_s, v_s, o_s, sem, osem):
    b = slot_ref[32]

    def load(p, _):
        slot = slot_ref[p]
        c, i = slot // 2, slot % 2
        pltpu.make_async_copy(q_hbm.at[c, i], q_s.at[pl.ds(pl.multiple_of(p * 64, 64), 64)], sem.at[0, p]).start()
        rows = pl.ds(pl.multiple_of(p * 256, 256), 256)
        pltpu.make_async_copy(kv_hbm.at[c, 0, i], k_s.at[rows], sem.at[1, p]).start()
        pltpu.make_async_copy(kv_hbm.at[c, 1, i], v_s.at[rows], sem.at[2, p]).start()
        return 0

    lax.fori_loop(0, 32, load, 0)

    for j in range(8):
        for p in range(4 * j, 4 * j + 4):
            pltpu.make_async_copy(q_hbm.at[0, 0], q_s.at[pl.ds(p * 64, 64)], sem.at[0, p]).wait()
            pltpu.make_async_copy(kv_hbm.at[0, 0, 0], k_s.at[pl.ds(p * 256, 256)], sem.at[1, p]).wait()
            pltpu.make_async_copy(kv_hbm.at[0, 1, 0], v_s.at[pl.ds(p * 256, 256)], sem.at[2, p]).wait()
        q = q_s[pl.ds(j * 256, 256), :]

        def step(start, carry, masked):
            top, tot, acc = carry
            keys = k_s[pl.ds(start, KEYS), :]
            scores = lax.dot_general(q, keys, (((1,), (1,)), ((), ())), preferred_element_type=F32)
            if masked:
                r = lax.broadcasted_iota(jnp.int32, scores.shape, 0)
                col = lax.broadcasted_iota(jnp.int32, scores.shape, 1)
                qpos = (r // 64) * 256 + b * 64 + r % 64
                scores = jnp.where(col <= qpos, scores, NEG_FILL)
            new = jnp.maximum(top, jnp.max(scores, axis=1, keepdims=True))
            w = jnp.exp2(scores - new)
            shrink = jnp.exp2(top - new)
            tot = tot * shrink + jnp.sum(w, axis=1, keepdims=True)
            acc = acc * shrink + jnp.dot(w.astype(BF16), v_s[pl.ds(start, KEYS), :], preferred_element_type=F32)
            return new, tot, acc

        first = (jnp.full((256, 1), NEG_FILL, F32), jnp.zeros((256, 1), F32), jnp.zeros((256, 128), F32))
        carry = step(j * KEYS, first, True)
        if j:
            carry = lax.fori_loop(0, j, lambda kc, c: step(pl.multiple_of(kc * KEYS, KEYS), c, False), carry)
        top, tot, acc = carry
        o_s[pl.ds(j * 256, 256), :] = (acc / tot).astype(BF16)
        for p in range(4 * j, 4 * j + 4):
            pltpu.make_async_copy(o_s.at[pl.ds(p * 64, 64)], o_hbm.at[slot_ref[p]], osem.at[p]).start()
    for p in range(32):
        pltpu.make_async_copy(o_s.at[pl.ds(p * 64, 64)], o_hbm.at[0], osem.at[p]).wait()


def attend(slots, q_all, kv_all):
    dma = pltpu.SemaphoreType.DMA
    return pl.pallas_call(
        attend_kernel,
        out_shape=jax.ShapeDtypeStruct((32, 64, 128), BF16),
        in_specs=[pl.BlockSpec(memory_space=pltpu.SMEM), ANY, ANY],
        out_specs=ANY,
        scratch_shapes=[
            pltpu.VMEM((2048, 128), BF16),
            pltpu.VMEM((8192, 128), BF16),
            pltpu.VMEM((8192, 128), BF16),
            pltpu.VMEM((2048, 128), BF16),
            dma((3, 32)),
            dma((32,)),
        ],
        compiler_params=pltpu.CompilerParams(vmem_limit_bytes=48 * 2**20),
        name="attend",
    )(slots, q_all, kv_all)


def return_kernel(o_ref, att_out, send, recv, loc):
    dp, y, x, t = coords()
    ctx = y * 4 + x
    a, b = ab_of(dp, y, x)
    barrier = pltpu.get_barrier_semaphore()

    def source(n):
        st, sa, r = n // 8, (n // 2) % 4, n % 2
        return st, ctx_of(dp, sa, 2 * (t % 2) + r)

    def dest(n):
        return 2 * (n % 2) + b // 2, n // 2

    def hello(n, _):
        st, sc = source(n)

        @pl.when(jnp.logical_or(st != t, sc != ctx))
        def _():
            pl.semaphore_signal(barrier, inc=1, device_id={"context": sc, "tensor": st}, device_id_type=MESH_ID)

        return 0

    lax.fori_loop(0, 32, hello, 0)
    has_self = (b // 2 == t % 2).astype(jnp.int32)
    pl.semaphore_wait(barrier, 32 - has_self)
    mine = (t * 4 + a) * 2 + b % 2

    def out_copy(n):
        dt, dc = dest(n)
        return remote(o_ref.at[n], att_out.at[mine], send.at[n], recv.at[mine], {"context": dc, "tensor": dt}), dt, dc

    def start(k, _):
        n = (k + 2 * ctx) % 32
        copy, dt, dc = out_copy(n)
        self_copy = jnp.logical_and(dt == t, dc == ctx)

        @pl.when(jnp.logical_not(self_copy))
        def _():
            copy.start()

        @pl.when(self_copy)
        def _():
            pltpu.make_async_copy(o_ref.at[n], att_out.at[mine], loc).start()

        return 0

    lax.fori_loop(0, 32, start, 0)

    def finish(n, _):
        st, sc = source(n)

        @pl.when(jnp.logical_or(st != t, sc != ctx))
        def _():
            ref = att_out.at[n]
            remote(ref, ref, send.at[0], recv.at[n], {"dp": 1 - dp}).wait_recv()

        copy, dt, dc = out_copy(n)
        self_copy = jnp.logical_and(dt == t, dc == ctx)

        @pl.when(jnp.logical_not(self_copy))
        def _():
            copy.wait_send()

        @pl.when(self_copy)
        def _():
            pltpu.make_async_copy(o_ref.at[n], att_out.at[mine], loc).wait()

        return 0

    lax.fori_loop(0, 32, finish, 0)


def give_back(o):
    dma = pltpu.SemaphoreType.DMA
    return pl.pallas_call(
        return_kernel,
        out_shape=jax.ShapeDtypeStruct((32, 64, 128), BF16),
        in_specs=[ANY],
        out_specs=ANY,
        scratch_shapes=[dma((32,)), dma((32,)), dma],
        compiler_params=pltpu.CompilerParams(collective_id=2, has_side_effects=True),
        name="give_back",
    )(o)


def body(ids, block_order, embed, mix_gain, in_proj, short_filter, long_filter, conv_skip,
         hyena_out, attn_gain, qkv_proj, attn_out):
    dp, y, x, t = coords()
    ctx = y * 4 + x
    codes = jnp.array(CODES, jnp.int32)
    emb4 = jnp.concatenate([embed[c : c + 1] for c in CODES] + [jnp.zeros((12, embed.shape[1]), BF16)], axis=0)
    wide = emb4.astype(F32)
    normed = (wide * lax.rsqrt(jnp.mean(wide * wide, axis=-1, keepdims=True) + EPS) * mix_gain).astype(BF16)
    projected = jnp.einsum("rd,jdc->jrc", normed, in_proj, preferred_element_type=F32).astype(BF16)[:, :4]
    table = short_filter[:, :, None, :] * projected.astype(F32)[:, None]
    pack = jnp.concatenate(
        [table.reshape(-1), long_filter.reshape(-1), conv_skip.reshape(-1)]
    ).reshape(-1, 128)
    ids_all, packs, wh, wa = gather_all(ids.reshape(1, 1, 128), pack, hyena_out, attn_out)

    packs = packs.reshape(4, -1)
    n_tab = 36 * 512
    tab = packs[:, :n_tab].reshape(4, 3, 12, 512).transpose(1, 2, 0, 3).reshape(3, 12, 2048)
    tab = jnp.concatenate([tab, jnp.zeros((3, 4, 2048), F32)], axis=1)
    lf = packs[:, n_tab : n_tab + 4096].reshape(128, 128)
    skip = packs[:, n_tab + 4096 :].reshape(1, 2048)
    taps = jnp.concatenate([jnp.zeros((128, 1), F32), lf[:, ::-1], jnp.zeros((128, 127), F32)], axis=1)

    ids_blocks = ids_all.reshape(32, 256)
    slot_ids = jnp.arange(32, dtype=jnp.int32)
    pair = 2 * ctx + jnp.arange(2, dtype=jnp.int32)
    owned = jnp.sum(jnp.where(slot_ids[None] == pair[:, None], block_order[None], 0), axis=1)
    own_ids = lax.dynamic_slice_in_dim(ids_blocks, 2 * ctx, 2, 0)
    hit = block_order[None, :] == owned[:, None] - 1
    prev_ids = jnp.sum(jnp.where(hit[:, :, None], ids_blocks[None, :, 126:], 0), axis=1)
    ext = jnp.concatenate([prev_ids, own_ids], axis=1)
    hots = [
        (ext[:, 2 - tap : 2 - tap + 384, None] == codes).astype(BF16) for tap in range(3)
    ]
    hot16 = jnp.concatenate(hots + [jnp.zeros((2, 384, 4), BF16)], axis=-1).reshape(768, 16)
    hot32 = jnp.concatenate([hot16, hot16], axis=1)
    code_hot = jnp.concatenate(
        [(own_ids.reshape(512, 1) == codes).astype(BF16), jnp.zeros((512, 12), BF16)], axis=1
    )
    mix = hyena_mix(hot32, tab, taps, skip)

    local_pos = (owned[:, None] * 256 + jnp.arange(256, dtype=jnp.int32)[None]).reshape(512)
    inverse_freq = THETA ** (-(2.0 * jnp.arange(64, dtype=F32)) / HD)
    angles = local_pos.astype(F32)[:, None] * inverse_freq[None, :]
    cos, sin = jnp.cos(angles), jnp.sin(angles)
    cos = jnp.concatenate([cos, cos], axis=1)
    sin = jnp.concatenate([-sin, sin], axis=1)
    stream_own, qkv = stream_qkv(
        t.astype(jnp.int32).reshape(1), mix, wh, code_hot, emb4, attn_gain.reshape(1, -1), qkv_proj, cos, sin
    )
    q_all, kv_all = exchange(qkv)
    slot_of = jnp.sum(jnp.where(block_order[None, :] == slot_ids[:, None], slot_ids[None, :], 0), axis=1)
    _, b = ab_of(dp, y, x)
    slots = jnp.concatenate([slot_of, b.astype(jnp.int32).reshape(1)])
    att = attend(slots, q_all, kv_all.reshape(16, 2, 2, 256, 128))
    att = give_back(att)
    att = att.reshape(16, 128, 128).transpose(1, 0, 2).reshape(128, 2048)
    return stream_own + jnp.dot(att, wa, preferred_element_type=F32)


def solution(mesh):
    placed = (
        P(("dp", "context", "tensor")),
        P("dp"),
        P(),
        P(),
        P(None, None, "tensor"),
        P(None, None, "tensor"),
        P("tensor", None),
        P("tensor"),
        P("tensor", None),
        P(),
        P(None, None, "tensor"),
        P("tensor", None),
    )
    return jax.shard_map(
        body,
        mesh=mesh,
        in_specs=placed,
        out_specs=P(("dp", "context", "tensor"), None),
        check_vma=False,
    )
```

```python
import functools
import math

import jax
import jax.numpy as jnp
from jax import lax
from jax.experimental import pallas as pl
from jax.experimental.pallas import tpu as pltpu
from jax.sharding import PartitionSpec as P

HD = 128
EPS = 1e-06
THETA = 1000000.0
NEG_FILL = -1e30
CODES = (65, 67, 71, 84)
MESH_ID = pl.DeviceIdType.MESH
F32 = jnp.float32
BF16 = jnp.bfloat16
ANY = pl.BlockSpec(memory_space=pl.ANY)


def coords():
    dp = lax.axis_index("dp")
    ctx = lax.axis_index("context")
    t = lax.axis_index("tensor")
    return dp, ctx // 4, ctx % 4, t


def pick(dp, first, second):
    return first + dp * (second - first)


def remote(src, dst, send, recv, where):
    return pltpu.make_async_remote_copy(
        src_ref=src, dst_ref=dst, send_sem=send, recv_sem=recv, device_id=where, device_id_type=MESH_ID
    )


ZKINDS = ((3, 0), (3, 1), (1, 0), (1, 1), (2, 0), (2, 1))


class WeightGather:
    def __init__(self, w_in, w_out, send, recv, hold, local_sem):
        self.w_in, self.w_out, self.send, self.recv = w_in, w_out, send, recv
        self.hold, self.local_sem = hold, local_sem
        dp, y, x, t = coords()
        self.dp, self.t = dp, t
        u, w = pick(dp, x, y), pick(dp, y, x)
        self.q = (u + 2 * w) % 4
        self.sib_q = (w + 2 * u) % 4
        self.shard = w_in.shape[0]
        self.piece = self.shard // 16
        xp, xm, yp, ym = (x + 1) % 4, (x + 3) % 4, (y + 1) % 4, (y + 3) % 4
        self.up = {"context": pick(dp, y * 4 + xp, yp * 4 + x)}
        self.um = {"context": pick(dp, y * 4 + xm, ym * 4 + x)}
        self.wp = {"context": pick(dp, yp * 4 + x, y * 4 + xp)}
        self.wm = {"context": pick(dp, ym * 4 + x, y * 4 + xm)}
        self.zp = {"tensor": (t + 1) % 4}
        self.zm = {"tensor": (t + 3) % 4}
        self.sib = {"dp": 1 - dp}
        self.pending = []

    def unit(self, z, dp, q, h):
        start = z * self.shard + dp * (self.shard // 2) + q * (2 * self.piece) + h * self.piece
        return self.w_out.at[pl.ds(pl.multiple_of(start, self.piece), self.piece), :]

    def own(self, h):
        start = self.dp * (self.shard // 2) + self.q * (2 * self.piece) + h * self.piece
        return self.w_in.at[pl.ds(pl.multiple_of(start, self.piece), self.piece), :]

    def go(self, src, dst, recv_at, where):
        at = len(self.pending)
        copy = remote(src, dst, self.send.at[at], self.recv.at[recv_at], where)
        copy.start()
        self.pending.append(copy)

    def arrived(self, dst, recv_at):
        remote(dst, dst, self.send.at[0], self.recv.at[recv_at], self.sib).wait_recv()

    def start(self):
        self.load = pltpu.make_async_copy(self.w_in, self.hold, self.local_sem.at[0])
        self.load.start()
        for h in (0, 1):
            dst = self.unit(self.t, self.dp, self.q, h)
            first, second = ((self.zp, 0 + h), (self.zm, 2 + h))
            if h == 0:
                self.go(self.own(h), dst, first[1], first[0])
                self.go(self.own(1), self.unit(self.t, self.dp, self.q, 1), 3, self.zm)
            else:
                self.go(self.own(1), dst, 1, self.zp)
                self.go(self.own(0), self.unit(self.t, self.dp, self.q, 0), 2, self.zm)

    def keep(self):
        row = pl.multiple_of(self.t * self.shard, self.shard)
        self.load.wait()
        self.local = pltpu.make_async_copy(self.hold, self.w_out.at[pl.ds(row, self.shard), :], self.local_sem.at[1])
        self.local.start()

    def z_step(self, kind):
        zoff, h = ZKINDS[kind]
        ref = self.unit((self.t + zoff) % 4, self.dp, self.q, h)
        self.arrived(ref, kind)
        if kind == 0:
            self.go(ref, ref, 4, self.zp)
        if kind == 3:
            self.go(ref, ref, 5, self.zm)
        self.go(ref, ref, 6 + kind, self.up)
        self.go(ref, ref, 12 + kind, self.um)
        self.go(ref, ref, 18 + kind, self.wp if h == 0 else self.wm)
        self.go(ref, ref, 24 + kind, self.sib)

    def plane_ref(self, side, kind, dp, q):
        zoff, h = ZKINDS[kind]
        qoff = (3, 1, 2)[side]
        return self.unit((self.t + zoff) % 4, dp, (q + qoff) % 4, h)

    def plane_step(self, side, kind):
        at = 6 + 6 * side + kind
        ref = self.plane_ref(side, kind, self.dp, self.q)
        self.arrived(ref, at)
        self.go(ref, ref, 24 + at, self.sib)

    def finish(self):
        for kind in range(6):
            zoff, h = ZKINDS[kind]
            self.arrived(self.unit((self.t + zoff) % 4, 1 - self.dp, self.sib_q, h), 24 + kind)
            for side in range(3):
                self.arrived(self.plane_ref(side, kind, 1 - self.dp, self.sib_q), 30 + 6 * side + kind)
        for copy in self.pending:
            copy.wait_send()
        self.local.wait()


KIND_ORDER = (0, 3, 1, 2, 4, 5)
N_SENDS = 6 + 18 + 24


def gather_kernel(ids_ref, pack_ref, wh_ref, wa_ref, ids_out, pack_out, wh_out,
                  sh, rh, sa, ra, s_ids, r_ids, s_pack, r_pack, hold_h, hold_a, loc_h, loc_a, loc):
    dp, y, x, t = coords()
    ctx = y * 4 + x
    barrier = pltpu.get_barrier_semaphore()
    partners = (
        [{"tensor": (t + d) % 4} for d in (1, 2, 3)]
        + [{"context": y * 4 + (x + d) % 4} for d in (1, 2, 3)]
        + [{"context": ((y + d) % 4) * 4 + x} for d in (1, 2, 3)]
        + [{"dp": 1 - dp}]
    )
    for where in partners:
        pl.semaphore_signal(barrier, inc=1, device_id=where, device_id_type=MESH_ID)
    pl.semaphore_wait(barrier, len(partners))

    small = []
    mine = ctx * 4 + t
    keep_ids = pltpu.make_async_copy(ids_ref, ids_out.at[pl.ds(mine, 1)], loc.at[0])
    keep_ids.start()
    keep_pack = pltpu.make_async_copy(pack_ref, pack_out.at[t], loc.at[1])
    keep_pack.start()
    for d in (1, 2, 3):
        c = remote(ids_ref, ids_out.at[pl.ds(mine, 1)], s_ids.at[d - 1], r_ids.at[d - 1], partners[d - 1])
        c.start()
        small.append(c)
        c = remote(pack_ref, pack_out.at[t], s_pack.at[d - 1], r_pack.at[d - 1], partners[d - 1])
        c.start()
        small.append(c)
    gh = WeightGather(wh_ref, wh_out, sh, rh, hold_h, loc_h)
    gh.start()
    keep_ids.wait()
    for d in (1, 2, 3):
        ref = ids_out.at[pl.ds(ctx * 4 + (t + 4 - d) % 4, 1)]
        remote(ref, ref, s_ids.at[0], r_ids.at[d - 1], partners[0]).wait_recv()
    row = ids_out.at[pl.ds(ctx * 4, 4)]
    for d in (1, 2, 3):
        c = remote(row, row, s_ids.at[2 + d], r_ids.at[2 + d], partners[2 + d])
        c.start()
        small.append(c)
    for d in (1, 2, 3):
        ref = ids_out.at[pl.ds((y * 4 + (x + 4 - d) % 4) * 4, 4)]
        remote(ref, ref, s_ids.at[0], r_ids.at[2 + d], partners[0]).wait_recv()
    row = ids_out.at[pl.ds(y * 16, 16)]
    for d in (1, 2, 3):
        c = remote(row, row, s_ids.at[5 + d], r_ids.at[5 + d], partners[5 + d])
        c.start()
        small.append(c)
    for k in KIND_ORDER:
        gh.z_step(k)
    gh.keep()
    for k in KIND_ORDER:
        for side in range(3):
            gh.plane_step(side, k)
    gh.finish()
    for d in (1, 2, 3):
        ref = ids_out.at[pl.ds(((y + 4 - d) % 4) * 16, 16)]
        remote(ref, ref, s_ids.at[0], r_ids.at[5 + d], partners[0]).wait_recv()
        ref = pack_out.at[(t + 4 - d) % 4]
        remote(ref, ref, s_ids.at[0], r_pack.at[d - 1], partners[0]).wait_recv()
    for c in small:
        c.wait_send()
    keep_pack.wait()


def gather_all(ids, pack, wh, wa):
    dma = pltpu.SemaphoreType.DMA
    return pl.pallas_call(
        gather_kernel,
        out_shape=(
            jax.ShapeDtypeStruct((64, 1, 128), jnp.int32),
            jax.ShapeDtypeStruct((4,) + pack.shape, F32),
            jax.ShapeDtypeStruct((2048, 4096), BF16),
        ),
        in_specs=[ANY] * 4,
        out_specs=(ANY,) * 3,
        scratch_shapes=[
            dma((N_SENDS,)), dma((48,)), dma((N_SENDS,)), dma((48,)),
            dma((9,)), dma((9,)), dma((3,)), dma((3,)),
            pltpu.VMEM(wh.shape, BF16), pltpu.VMEM(wa.shape, BF16), dma((2,)), dma((2,)), dma((2,)),
        ],
        compiler_params=pltpu.CompilerParams(
            collective_id=0, has_side_effects=True, vmem_limit_bytes=32 * 2**20
        ),
        name="gather_all",
    )(ids, pack, wh, wa)


def mix_kernel(onehot_ref, tab_ref, taps_ref, skip_ref, out_ref):
    table = jnp.concatenate([tab_ref[0], tab_ref[1], tab_ref[2]], axis=1)
    high = table.astype(BF16)
    low = (table - high.astype(F32)).astype(BF16)
    both = jnp.concatenate([high, low], axis=0)
    filtered = jnp.dot(onehot_ref[...], both, preferred_element_type=F32)
    gated = filtered[:, 128:256] * filtered[:, 256:384]
    g16 = gated.astype(BF16)
    window = jnp.concatenate(
        [g16[b * 384 + s * 128 : b * 384 + s * 128 + 256] for b in range(2) for s in range(2)], axis=1
    )
    lane_group = (lax.broadcasted_iota(jnp.int32, window.shape, 1) % 128) // 16
    total = jnp.zeros((128, 512), F32)
    for g in range(8):
        base = jnp.broadcast_to(taps_ref[g : g + 1, :], (128, 256))
        toep = pltpu.roll(base, 0, 1, stride=1, stride_axis=0).astype(BF16)
        masked = jnp.where(lane_group == g, window, jnp.zeros_like(window))
        total = total + jnp.dot(toep, masked, preferred_element_type=F32)
    for b in range(2):
        for s in range(2):
            at = b * 384 + 128 + s * 128
            part = total[:, (2 * b + s) * 128 : (2 * b + s + 1) * 128]
            mixed = filtered[at : at + 128, 0:128] * (part + skip_ref[...] * gated[at : at + 128])
            out_ref[b * 256 + s * 128 : b * 256 + (s + 1) * 128, :] = mixed.astype(BF16)


def hyena_mix(onehot, tab, taps, skip):
    return pl.pallas_call(
        mix_kernel,
        out_shape=jax.ShapeDtypeStruct((512, 2048), BF16),
        grid=(16,),
        in_specs=[
            pl.BlockSpec((768, 32), lambda i: (0, 0)),
            pl.BlockSpec((3, 16, 128), lambda i: (0, 0, i)),
            pl.BlockSpec((8, 256), lambda i: (i, 0)),
            pl.BlockSpec((1, 128), lambda i: (0, i)),
        ],
        out_specs=pl.BlockSpec((512, 128), lambda i: (0, i)),
        compiler_params=pltpu.CompilerParams(vmem_limit_bytes=40 * 2**20),
        name="hyena_mix",
    )(onehot, tab, taps, skip)


def proj_kernel(t_ref, mix_ref, wh_ref, code_ref, emb_ref, gain_ref, wq_ref, cos_ref, sin_ref,
                own_ref, qkv_ref, attn_in, chunk, squares):
    i = pl.program_id(0)

    @pl.when(i < 8)
    def _():
        vals = jnp.dot(mix_ref[...], wh_ref[...], preferred_element_type=F32)
        vals = vals + jnp.dot(code_ref[...], emb_ref[...], preferred_element_type=F32)
        chunk[...] = vals
        part = jnp.sum(vals * vals, axis=1, keepdims=True)

        @pl.when(i == 0)
        def _():
            squares[...] = jnp.zeros_like(squares)

        squares[...] += jnp.broadcast_to(part, squares.shape)
        attn_in[:, pl.ds(pl.multiple_of(i * 512, 512), 512)] = (vals * gain_ref[...]).astype(BF16)
        own_ref[...] = chunk[pl.ds(pl.multiple_of(t_ref[0] * 128, 128), 128), :]

    @pl.when(i >= 8)
    def _():
        k = i - 8
        j = k // 2
        factor = lax.rsqrt(squares[...] / 4096.0 + EPS)
        factor = factor * jnp.where(j == 0, HD**-0.5 * math.log2(math.e), 1.0).astype(F32)
        rotated = j < 2
        cos = jnp.where(rotated, cos_ref[...], 1.0) * factor
        sin = jnp.where(rotated, sin_ref[...], 0.0) * factor
        vals = jnp.dot(attn_in[...], wq_ref[0], preferred_element_type=F32)
        for hh in range(2):
            head = vals[:, hh * 128 : (hh + 1) * 128]
            turned = head * cos + pltpu.roll(head, 64, 1) * sin
            qkv_ref[2 * (k % 2) + hh, j] = turned.astype(BF16).reshape(2, 4, 64, 128)


def stream_qkv(t_arr, mix, wh, code_hot, emb4, gain, wq, cos, sin):
    def whi(i, t):
        return (0, jnp.minimum(i, 7))

    def wqi(i, t):
        k = jnp.maximum(i - 8, 0)
        return (k // 2, 0, k % 2)

    def whole(*shape):
        return pl.BlockSpec(shape, lambda i, t: (0,) * len(shape))

    return pl.pallas_call(
        proj_kernel,
        out_shape=(
            jax.ShapeDtypeStruct((128, 4096), F32),
            jax.ShapeDtypeStruct((4, 3, 2, 4, 64, 128), BF16),
        ),
        grid_spec=pltpu.PrefetchScalarGridSpec(
            num_scalar_prefetch=1,
            grid=(14,),
            in_specs=[
                whole(512, 2048),
                pl.BlockSpec((2048, 512), whi),
                whole(512, 16),
                pl.BlockSpec((16, 512), whi),
                pl.BlockSpec((1, 512), whi),
                pl.BlockSpec((1, 4096, 256), wqi),
                whole(512, 128),
                whole(512, 128),
            ],
            out_specs=(
                pl.BlockSpec((128, 512), whi),
                whole(4, 3, 2, 4, 64, 128),
            ),
            scratch_shapes=[
                pltpu.VMEM((512, 4096), BF16),
                pltpu.VMEM((512, 512), F32),
                pltpu.VMEM((512, 128), F32),
            ],
        ),
        compiler_params=pltpu.CompilerParams(vmem_limit_bytes=48 * 2**20),
        name="stream_qkv",
    )(t_arr, mix, wh, code_hot, emb4, gain, wq, cos, sin)


def ab_of(dp, y, x):
    return pick(dp, y, x), pick(dp, x, y)


def ctx_of(dp, a, b):
    return pick(dp, a * 4 + b, b * 4 + a)


def exchange_kernel(qkv_ref, q_out, kv_out, sq, rq, s1, r1, s2, r2, s3, r3, loc):
    dp, y, x, t = coords()
    ctx = y * 4 + x
    a, b = ab_of(dp, y, x)
    barrier = pltpu.get_barrier_semaphore()
    others = [{"context": (ctx + d) % 16} for d in range(1, 16)]
    for where in others:
        pl.semaphore_signal(barrier, inc=1, device_id=where, device_id_type=MESH_ID)
    pl.semaphore_wait(barrier, 15)
    sent = []
    keep_kv = pltpu.make_async_copy(qkv_ref.at[a, pl.ds(1, 2)], kv_out.at[ctx], loc.at[0])
    keep_kv.start()
    bp = {"context": ctx_of(dp, a, (b + 1) % 4)}
    bm = {"context": ctx_of(dp, a, (b + 3) % 4)}

    def spread(src, k, src_ctx):
        for side, where in ((0, bp), (1, bm)):
            c = remote(src, kv_out.at[src_ctx], s2.at[side * 4 + k], r2.at[side * 4 + k], where)
            c.start()
            sent.append(c)

    for d in (1, 3, 2):
        h = (a + d) % 4
        c = remote(qkv_ref.at[h, pl.ds(1, 2)], kv_out.at[ctx], s1.at[d - 1], r1.at[d - 1], {"context": ctx_of(dp, h, b)})
        c.start()
        sent.append(c)
    spread(qkv_ref.at[a, pl.ds(1, 2)], 0, ctx)
    for d in range(1, 16):
        to = (ctx + d) % 16
        h, s = ab_of(dp, to // 4, to % 4)
        c = remote(qkv_ref.at[h, 0, :, s], q_out.at[ctx], sq.at[d - 1], rq.at[d - 1], others[d - 1])
        c.start()
        sent.append(c)
    keep_q = pltpu.make_async_copy(qkv_ref.at[a, 0, :, b], q_out.at[ctx], loc.at[1])
    keep_q.start()
    for d in (1, 3, 2):
        from_ctx = ctx_of(dp, (a + 4 - d) % 4, b)
        ref = kv_out.at[from_ctx]
        remote(ref, ref, s1.at[0], r1.at[d - 1], bp).wait_recv()
        spread(ref, d, from_ctx)
    for k in (0, 1, 3, 2):
        ua = (a + 4 - k) % 4
        ref = kv_out.at[ctx_of(dp, ua, (b + 3) % 4)]
        remote(ref, ref, s1.at[0], r2.at[k], bp).wait_recv()
        c = remote(ref.at[0], ref.at[0], s3.at[k], r3.at[k], bp)
        c.start()
        sent.append(c)
        ref = kv_out.at[ctx_of(dp, ua, (b + 1) % 4)]
        remote(ref, ref, s1.at[0], r2.at[4 + k], bp).wait_recv()
        c = remote(ref.at[1], ref.at[1], s3.at[4 + k], r3.at[4 + k], bm)
        c.start()
        sent.append(c)
    for k in (0, 1, 3, 2):
        ref = kv_out.at[ctx_of(dp, (a + 4 - k) % 4, (b + 2) % 4)]
        for part in (0, 1):
            remote(ref.at[part], ref.at[part], s1.at[0], r3.at[4 * part + k], bp).wait_recv()
    for d in range(1, 16):
        ref = q_out.at[(ctx + 16 - d) % 16]
        remote(ref, ref, s1.at[0], rq.at[d - 1], bp).wait_recv()
    for c in sent:
        c.wait_send()
    keep_q.wait()
    keep_kv.wait()


def exchange(qkv):
    dma = pltpu.SemaphoreType.DMA
    return pl.pallas_call(
        exchange_kernel,
        out_shape=(
            jax.ShapeDtypeStruct((16, 2, 64, 128), BF16),
            jax.ShapeDtypeStruct((16, 2, 2, 4, 64, 128), BF16),
        ),
        in_specs=[ANY],
        out_specs=(ANY,) * 2,
        scratch_shapes=[dma((15,)), dma((15,)), dma((3,)), dma((3,)), dma((8,)), dma((8,)), dma((8,)), dma((8,)), dma((2,))],
        compiler_params=pltpu.CompilerParams(collective_id=1, has_side_effects=True),
        name="exchange",
    )(qkv)


KEYS = 1024


def attend_kernel(slot_ref, q_hbm, kv_hbm, o_hbm, q_s, k_s, v_s, o_s, sem, osem):
    b = slot_ref[32]

    def load(p, _):
        slot = slot_ref[p]
        c, i = slot // 2, slot % 2
        pltpu.make_async_copy(q_hbm.at[c, i], q_s.at[pl.ds(pl.multiple_of(p * 64, 64), 64)], sem.at[0, p]).start()
        rows = pl.ds(pl.multiple_of(p * 256, 256), 256)
        pltpu.make_async_copy(kv_hbm.at[c, 0, i], k_s.at[rows], sem.at[1, p]).start()
        pltpu.make_async_copy(kv_hbm.at[c, 1, i], v_s.at[rows], sem.at[2, p]).start()
        return 0

    lax.fori_loop(0, 32, load, 0)

    for j in range(8):
        for p in range(4 * j, 4 * j + 4):
            pltpu.make_async_copy(q_hbm.at[0, 0], q_s.at[pl.ds(p * 64, 64)], sem.at[0, p]).wait()
            pltpu.make_async_copy(kv_hbm.at[0, 0, 0], k_s.at[pl.ds(p * 256, 256)], sem.at[1, p]).wait()
            pltpu.make_async_copy(kv_hbm.at[0, 1, 0], v_s.at[pl.ds(p * 256, 256)], sem.at[2, p]).wait()
        q = q_s[pl.ds(j * 256, 256), :]

        def step(start, carry, masked):
            top, tot, acc = carry
            keys = k_s[pl.ds(start, KEYS), :]
            scores = lax.dot_general(q, keys, (((1,), (1,)), ((), ())), preferred_element_type=F32)
            if masked:
                r = lax.broadcasted_iota(jnp.int32, scores.shape, 0)
                col = lax.broadcasted_iota(jnp.int32, scores.shape, 1)
                qpos = (r // 64) * 256 + b * 64 + r % 64
                scores = jnp.where(col <= qpos, scores, NEG_FILL)
            new = jnp.maximum(top, jnp.max(scores, axis=1, keepdims=True))
            w = jnp.exp2(scores - new)
            shrink = jnp.exp2(top - new)
            tot = tot * shrink + jnp.sum(w, axis=1, keepdims=True)
            acc = acc * shrink + jnp.dot(w.astype(BF16), v_s[pl.ds(start, KEYS), :], preferred_element_type=F32)
            return new, tot, acc

        first = (jnp.full((256, 1), NEG_FILL, F32), jnp.zeros((256, 1), F32), jnp.zeros((256, 128), F32))
        carry = step(j * KEYS, first, True)
        if j:
            carry = lax.fori_loop(0, j, lambda kc, c: step(pl.multiple_of(kc * KEYS, KEYS), c, False), carry)
        top, tot, acc = carry
        o_s[pl.ds(j * 256, 256), :] = (acc / tot).astype(BF16)
        for p in range(4 * j, 4 * j + 4):
            pltpu.make_async_copy(o_s.at[pl.ds(p * 64, 64)], o_hbm.at[slot_ref[p]], osem.at[p]).start()
    for p in range(32):
        pltpu.make_async_copy(o_s.at[pl.ds(p * 64, 64)], o_hbm.at[0], osem.at[p]).wait()


def attend(slots, q_all, kv_all):
    dma = pltpu.SemaphoreType.DMA
    return pl.pallas_call(
        attend_kernel,
        out_shape=jax.ShapeDtypeStruct((32, 64, 128), BF16),
        in_specs=[pl.BlockSpec(memory_space=pltpu.SMEM), ANY, ANY],
        out_specs=ANY,
        scratch_shapes=[
            pltpu.VMEM((2048, 128), BF16),
            pltpu.VMEM((8192, 128), BF16),
            pltpu.VMEM((8192, 128), BF16),
            pltpu.VMEM((2048, 128), BF16),
            dma((3, 32)),
            dma((32,)),
        ],
        compiler_params=pltpu.CompilerParams(vmem_limit_bytes=48 * 2**20),
        name="attend",
    )(slots, q_all, kv_all)


def return_kernel(o_ref, att_out, send, recv, loc):
    dp, y, x, t = coords()
    ctx = y * 4 + x
    a, b = ab_of(dp, y, x)
    barrier = pltpu.get_barrier_semaphore()

    def source(n):
        st, sa, r = n // 8, (n // 2) % 4, n % 2
        return st, ctx_of(dp, sa, 2 * (t % 2) + r)

    def dest(n):
        return 2 * (n % 2) + b // 2, n // 2

    def hello(n, _):
        st, sc = source(n)

        @pl.when(jnp.logical_or(st != t, sc != ctx))
        def _():
            pl.semaphore_signal(barrier, inc=1, device_id={"context": sc, "tensor": st}, device_id_type=MESH_ID)

        return 0

    lax.fori_loop(0, 32, hello, 0)
    has_self = (b // 2 == t % 2).astype(jnp.int32)
    pl.semaphore_wait(barrier, 32 - has_self)
    mine = (t * 4 + a) * 2 + b % 2

    def out_copy(n):
        dt, dc = dest(n)
        return remote(o_ref.at[n], att_out.at[mine], send.at[n], recv.at[mine], {"context": dc, "tensor": dt}), dt, dc

    def start(k, _):
        n = (k + 2 * ctx) % 32
        copy, dt, dc = out_copy(n)
        self_copy = jnp.logical_and(dt == t, dc == ctx)

        @pl.when(jnp.logical_not(self_copy))
        def _():
            copy.start()

        @pl.when(self_copy)
        def _():
            pltpu.make_async_copy(o_ref.at[n], att_out.at[mine], loc).start()

        return 0

    lax.fori_loop(0, 32, start, 0)

    def finish(n, _):
        st, sc = source(n)

        @pl.when(jnp.logical_or(st != t, sc != ctx))
        def _():
            ref = att_out.at[n]
            remote(ref, ref, send.at[0], recv.at[n], {"dp": 1 - dp}).wait_recv()

        copy, dt, dc = out_copy(n)
        self_copy = jnp.logical_and(dt == t, dc == ctx)

        @pl.when(jnp.logical_not(self_copy))
        def _():
            copy.wait_send()

        @pl.when(self_copy)
        def _():
            pltpu.make_async_copy(o_ref.at[n], att_out.at[mine], loc).wait()

        return 0

    lax.fori_loop(0, 32, finish, 0)


def give_back(o):
    dma = pltpu.SemaphoreType.DMA
    return pl.pallas_call(
        return_kernel,
        out_shape=jax.ShapeDtypeStruct((32, 64, 128), BF16),
        in_specs=[ANY],
        out_specs=ANY,
        scratch_shapes=[dma((32,)), dma((32,)), dma],
        compiler_params=pltpu.CompilerParams(collective_id=2, has_side_effects=True),
        name="give_back",
    )(o)


def body(ids, block_order, embed, mix_gain, in_proj, short_filter, long_filter, conv_skip,
         hyena_out, attn_gain, qkv_proj, attn_out):
    dp, y, x, t = coords()
    ctx = y * 4 + x
    codes = jnp.array(CODES, jnp.int32)
    emb4 = jnp.concatenate([embed[c : c + 1] for c in CODES] + [jnp.zeros((12, embed.shape[1]), BF16)], axis=0)
    wide = emb4.astype(F32)
    normed = (wide * lax.rsqrt(jnp.mean(wide * wide, axis=-1, keepdims=True) + EPS) * mix_gain).astype(BF16)
    projected = jnp.einsum("rd,jdc->jrc", normed, in_proj, preferred_element_type=F32).astype(BF16)[:, :4]
    table = short_filter[:, :, None, :] * projected.astype(F32)[:, None]
    pack = jnp.concatenate(
        [table.reshape(-1), long_filter.reshape(-1), conv_skip.reshape(-1)]
    ).reshape(-1, 128)
    ids_all, packs, wh = gather_all(ids.reshape(1, 1, 128), pack, hyena_out, attn_out)
    wa = lax.all_gather(lax.dynamic_slice_in_dim(attn_out, (dp * 16 + ctx) * 16, 16, 0), ("tensor", "dp", "context"), axis=0, tiled=True)

    packs = packs.reshape(4, -1)
    n_tab = 36 * 512
    tab = packs[:, :n_tab].reshape(4, 3, 12, 512).transpose(1, 2, 0, 3).reshape(3, 12, 2048)
    tab = jnp.concatenate([tab, jnp.zeros((3, 4, 2048), F32)], axis=1)
    lf = packs[:, n_tab : n_tab + 4096].reshape(128, 128)
    skip = packs[:, n_tab + 4096 :].reshape(1, 2048)
    taps = jnp.concatenate([jnp.zeros((128, 1), F32), lf[:, ::-1], jnp.zeros((128, 127), F32)], axis=1)

    ids_blocks = ids_all.reshape(32, 256)
    slot_ids = jnp.arange(32, dtype=jnp.int32)
    pair = 2 * ctx + jnp.arange(2, dtype=jnp.int32)
    owned = jnp.sum(jnp.where(slot_ids[None] == pair[:, None], block_order[None], 0), axis=1)
    own_ids = lax.dynamic_slice_in_dim(ids_blocks, 2 * ctx, 2, 0)
    hit = block_order[None, :] == owned[:, None] - 1
    prev_ids = jnp.sum(jnp.where(hit[:, :, None], ids_blocks[None, :, 126:], 0), axis=1)
    ext = jnp.concatenate([prev_ids, own_ids], axis=1)
    hots = [
        (ext[:, 2 - tap : 2 - tap + 384, None] == codes).astype(BF16) for tap in range(3)
    ]
    hot16 = jnp.concatenate(hots + [jnp.zeros((2, 384, 4), BF16)], axis=-1).reshape(768, 16)
    hot32 = jnp.concatenate([hot16, hot16], axis=1)
    code_hot = jnp.concatenate(
        [(own_ids.reshape(512, 1) == codes).astype(BF16), jnp.zeros((512, 12), BF16)], axis=1
    )
    mix = hyena_mix(hot32, tab, taps, skip)

    local_pos = (owned[:, None] * 256 + jnp.arange(256, dtype=jnp.int32)[None]).reshape(512)
    inverse_freq = THETA ** (-(2.0 * jnp.arange(64, dtype=F32)) / HD)
    angles = local_pos.astype(F32)[:, None] * inverse_freq[None, :]
    cos, sin = jnp.cos(angles), jnp.sin(angles)
    cos = jnp.concatenate([cos, cos], axis=1)
    sin = jnp.concatenate([-sin, sin], axis=1)
    stream_own, qkv = stream_qkv(
        t.astype(jnp.int32).reshape(1), mix, wh, code_hot, emb4, attn_gain.reshape(1, -1), qkv_proj, cos, sin
    )
    q_all, kv_all = exchange(qkv)
    slot_of = jnp.sum(jnp.where(block_order[None, :] == slot_ids[:, None], slot_ids[None, :], 0), axis=1)
    _, b = ab_of(dp, y, x)
    slots = jnp.concatenate([slot_of, b.astype(jnp.int32).reshape(1)])
    att = attend(slots, q_all, kv_all.reshape(16, 2, 2, 256, 128))
    att = give_back(att)
    att = att.reshape(16, 128, 128).transpose(1, 0, 2).reshape(128, 2048)
    return stream_own + jnp.dot(att, wa, preferred_element_type=F32)


def solution(mesh):
    placed = (
        P(("dp", "context", "tensor")),
        P("dp"),
        P(),
        P(),
        P(None, None, "tensor"),
        P(None, None, "tensor"),
        P("tensor", None),
        P("tensor"),
        P("tensor", None),
        P(),
        P(None, None, "tensor"),
        P("tensor", None),
    )
    return jax.shard_map(
        body,
        mesh=mesh,
        in_specs=placed,
        out_specs=P(("dp", "context", "tensor"), None),
        check_vma=False,
    )
```

```python
import functools
import math

import jax
import jax.numpy as jnp
from jax import lax
from jax.experimental import pallas as pl
from jax.experimental.pallas import tpu as pltpu
from jax.sharding import PartitionSpec as P

HD = 128
EPS = 1e-06
THETA = 1000000.0
NEG_FILL = -1e30
CODES = (65, 67, 71, 84)
MESH_ID = pl.DeviceIdType.MESH
F32 = jnp.float32
BF16 = jnp.bfloat16
ANY = pl.BlockSpec(memory_space=pl.ANY)


def coords():
    dp = lax.axis_index("dp")
    ctx = lax.axis_index("context")
    t = lax.axis_index("tensor")
    return dp, ctx // 4, ctx % 4, t


def pick(dp, first, second):
    return first + dp * (second - first)


def remote(src, dst, send, recv, where):
    return pltpu.make_async_remote_copy(
        src_ref=src, dst_ref=dst, send_sem=send, recv_sem=recv, device_id=where, device_id_type=MESH_ID
    )


ZKINDS = ((3, 0), (3, 1), (1, 0), (1, 1), (2, 0), (2, 1))


class WeightGather:
    def __init__(self, w_in, w_out, send, recv, hold, local_sem):
        self.w_in, self.w_out, self.send, self.recv = w_in, w_out, send, recv
        self.hold, self.local_sem = hold, local_sem
        dp, y, x, t = coords()
        self.dp, self.t = dp, t
        u, w = pick(dp, x, y), pick(dp, y, x)
        self.q = (u + 2 * w) % 4
        self.sib_q = (w + 2 * u) % 4
        self.shard = w_in.shape[0]
        self.piece = self.shard // 16
        xp, xm, yp, ym = (x + 1) % 4, (x + 3) % 4, (y + 1) % 4, (y + 3) % 4
        self.up = {"context": pick(dp, y * 4 + xp, yp * 4 + x)}
        self.um = {"context": pick(dp, y * 4 + xm, ym * 4 + x)}
        self.wp = {"context": pick(dp, yp * 4 + x, y * 4 + xp)}
        self.wm = {"context": pick(dp, ym * 4 + x, y * 4 + xm)}
        self.zp = {"tensor": (t + 1) % 4}
        self.zm = {"tensor": (t + 3) % 4}
        self.sib = {"dp": 1 - dp}
        self.pending = []

    def unit(self, z, dp, q, h):
        start = z * self.shard + dp * (self.shard // 2) + q * (2 * self.piece) + h * self.piece
        return self.w_out.at[pl.ds(pl.multiple_of(start, self.piece), self.piece), :]

    def own(self, h):
        start = self.dp * (self.shard // 2) + self.q * (2 * self.piece) + h * self.piece
        return self.w_in.at[pl.ds(pl.multiple_of(start, self.piece), self.piece), :]

    def go(self, src, dst, recv_at, where):
        at = len(self.pending)
        copy = remote(src, dst, self.send.at[at], self.recv.at[recv_at], where)
        copy.start()
        self.pending.append(copy)

    def arrived(self, dst, recv_at):
        remote(dst, dst, self.send.at[0], self.recv.at[recv_at], self.sib).wait_recv()

    def start(self):
        self.load = pltpu.make_async_copy(self.w_in, self.hold, self.local_sem.at[0])
        self.load.start()
        for h in (0, 1):
            dst = self.unit(self.t, self.dp, self.q, h)
            first, second = ((self.zp, 0 + h), (self.zm, 2 + h))
            if h == 0:
                self.go(self.own(h), dst, first[1], first[0])
                self.go(self.own(1), self.unit(self.t, self.dp, self.q, 1), 3, self.zm)
            else:
                self.go(self.own(1), dst, 1, self.zp)
                self.go(self.own(0), self.unit(self.t, self.dp, self.q, 0), 2, self.zm)

    def keep(self):
        row = pl.multiple_of(self.t * self.shard, self.shard)
        self.load.wait()
        self.local = pltpu.make_async_copy(self.hold, self.w_out.at[pl.ds(row, self.shard), :], self.local_sem.at[1])
        self.local.start()

    def z_step(self, kind):
        zoff, h = ZKINDS[kind]
        ref = self.unit((self.t + zoff) % 4, self.dp, self.q, h)
        self.arrived(ref, kind)
        if kind == 0:
            self.go(ref, ref, 4, self.zp)
        if kind == 3:
            self.go(ref, ref, 5, self.zm)
        self.go(ref, ref, 6 + kind, self.up)
        self.go(ref, ref, 12 + kind, self.um)
        self.go(ref, ref, 18 + kind, self.wp if h == 0 else self.wm)
        self.go(ref, ref, 24 + kind, self.sib)

    def plane_ref(self, side, kind, dp, q):
        zoff, h = ZKINDS[kind]
        qoff = (3, 1, 2)[side]
        return self.unit((self.t + zoff) % 4, dp, (q + qoff) % 4, h)

    def plane_step(self, side, kind):
        at = 6 + 6 * side + kind
        ref = self.plane_ref(side, kind, self.dp, self.q)
        self.arrived(ref, at)
        self.go(ref, ref, 24 + at, self.sib)

    def finish(self):
        for kind in range(6):
            zoff, h = ZKINDS[kind]
            self.arrived(self.unit((self.t + zoff) % 4, 1 - self.dp, self.sib_q, h), 24 + kind)
            for side in range(3):
                self.arrived(self.plane_ref(side, kind, 1 - self.dp, self.sib_q), 30 + 6 * side + kind)
        for copy in self.pending:
            copy.wait_send()
        self.local.wait()


KIND_ORDER = (0, 3, 1, 2, 4, 5)
N_SENDS = 6 + 18 + 24


def code_rows(shape):
    k = lax.broadcasted_iota(jnp.int32, shape, 0) % 4
    return jnp.where(k < 2, jnp.where(k == 0, CODES[0], CODES[1]), jnp.where(k == 2, CODES[2], CODES[3]))


def hyena_kernel(ids_ref, hit_ref, emb_ref, gain_ref, proj_ref, short_ref, taps_ref, skip_ref, wh_ref,
                 mix_ref, hot_out, wh_out,
                 ids_all, tab_all, taps_all, hots, proj_s, hold,
                 s_w, r_w, loc_w, s_ids, r_ids, s_tab, r_tab, s_taps, r_taps, p_sem):
    dp, y, x, t = coords()
    ctx = y * 4 + x
    loads = [pltpu.make_async_copy(proj_ref.at[j], proj_s.at[j], p_sem.at[j]) for j in range(3)]
    for c in loads:
        c.start()
    barrier = pltpu.get_barrier_semaphore()
    zs = [{"tensor": (t + d) % 4} for d in (1, 2, 3)]
    xs = [{"context": y * 4 + (x + d) % 4} for d in (1, 2, 3)]
    ys = [{"context": ((y + d) % 4) * 4 + x} for d in (1, 2, 3)]
    partners = zs + xs + ys + [{"dp": 1 - dp}]
    for where in partners:
        pl.semaphore_signal(barrier, inc=1, device_id=where, device_id_type=MESH_ID)
    mine = ctx * 4 + t
    ids_all[mine] = ids_ref[...]
    trow = pl.ds(pl.multiple_of(t * 32, 32), 32)
    taps_all[trow, :] = taps_ref[...]
    pl.semaphore_wait(barrier, len(partners))

    small = []

    def go(src, send, recv, where):
        c = remote(src, src, send, recv, where)
        c.start()
        small.append(c)

    def landed(ref, recv):
        remote(ref, ref, s_ids.at[0], recv, zs[0]).wait_recv()

    gh = WeightGather(wh_ref, wh_out, s_w, r_w, hold, loc_w)
    for d in (0, 1, 2):
        go(ids_all.at[pl.ds(mine, 1)], s_ids.at[d], r_ids.at[d], zs[d])
    gh.start()
    for d in (0, 1, 2):
        go(taps_all.at[trow, :], s_taps.at[d], r_taps.at[d], zs[d])

    wide = emb_ref[...].astype(F32)
    square = jnp.sum(wide * wide, axis=1, keepdims=True)
    normed = (wide * lax.rsqrt(square / 4096.0 + EPS) * gain_ref[...]).astype(BF16)
    cols = pl.ds(pl.multiple_of(t * 512, 512), 512)
    for j in range(3):
        loads[j].wait()
        rows = jnp.dot(normed, proj_s[j], preferred_element_type=F32).astype(BF16).astype(F32)[0:4]
        last = jnp.broadcast_to(skip_ref[...], (4, 512))
        tab_all[j, :, cols] = jnp.concatenate([short_ref[j, tap : tap + 1, :] * rows for tap in range(3)] + [last], axis=0)
    for d in (0, 1, 2):
        go(tab_all.at[:, :, cols], s_tab.at[d], r_tab.at[d], zs[d])
    for d in (0, 1, 2):
        landed(ids_all.at[pl.ds(ctx * 4 + (t + 3 - d) % 4, 1)], r_ids.at[d])
    for d in (0, 1, 2):
        go(ids_all.at[pl.ds(ctx * 4, 4)], s_ids.at[3 + d], r_ids.at[3 + d], xs[d])
    gh.z_step(0)
    gh.z_step(3)
    for d in (0, 1, 2):
        landed(ids_all.at[pl.ds((y * 4 + (x + 3 - d) % 4) * 4, 4)], r_ids.at[3 + d])
    for d in (0, 1, 2):
        go(ids_all.at[pl.ds(y * 16, 16)], s_ids.at[6 + d], r_ids.at[6 + d], ys[d])
    gh.z_step(1)
    gh.z_step(2)
    gh.keep()
    for d in (0, 1, 2):
        landed(ids_all.at[pl.ds(((y + 3 - d) % 4) * 16, 16)], r_ids.at[6 + d])
        zrow = pl.ds(pl.multiple_of(((t + 3 - d) % 4) * 32, 32), 32)
        landed(taps_all.at[zrow, :], r_taps.at[d])
        landed(tab_all.at[:, :, pl.ds(pl.multiple_of(((t + 3 - d) % 4) * 512, 512), 512)], r_tab.at[d])

    row8 = lax.broadcasted_iota(jnp.int32, (8, 384), 0)
    code8 = code_rows((8, 384))
    for b in range(2):
        prev = [jnp.zeros((8, 128), jnp.int32) for _ in range(2)]
        for slot in range(32):
            hit = hit_ref[b * 32 + slot]
            for half in range(2):
                prev[half] = prev[half] + hit * ids_all[2 * slot + half]
        own = [ids_all[ctx * 4 + 2 * b + half] for half in range(2)]
        line = jnp.concatenate(prev + own, axis=1)
        back = [line[:, 128:]] + [pltpu.roll(line, tap, 1)[:, 128:] for tap in (1, 2)]
        top = jnp.where(jnp.where(row8 < 4, back[0], back[1]) == code8, 1.0, 0.0)
        low = jnp.where(row8 < 4, jnp.where(back[2] == code8, 1.0, 0.0), 0.0)
        hots[b * 384 : (b + 1) * 384, :] = jnp.concatenate([top, low, top, low], axis=0).T.astype(BF16)
        hot_out[b * 256 : (b + 1) * 256, :] = hots[b * 384 + 128 : (b + 1) * 384, :]

    def chunk(i, _):
        lanes = pl.ds(pl.multiple_of(i * 128, 128), 128)
        table = jnp.concatenate([tab_all[j, :, lanes] for j in range(3)], axis=1)
        high = table.astype(BF16)
        low = (table - high.astype(F32)).astype(BF16)
        both = jnp.concatenate([high, low], axis=0)
        filtered = jnp.dot(hots[...], both, preferred_element_type=F32)
        gated = filtered[:, 128:256] * filtered[:, 256:384]
        g16 = gated.astype(BF16)
        window = jnp.concatenate(
            [g16[b * 384 + s * 128 : b * 384 + s * 128 + 256] for b in range(2) for s in range(2)], axis=1
        )
        lane_group = (lax.broadcasted_iota(jnp.int32, window.shape, 1) % 128) // 16
        taps = taps_all[pl.ds(pl.multiple_of(i * 8, 8), 8), :]
        total = jnp.zeros((128, 512), F32)
        for g in range(8):
            base = jnp.broadcast_to(taps[g : g + 1, :], (128, 256))
            toep = pltpu.roll(base, 0, 1, stride=1, stride_axis=0).astype(BF16)
            masked = jnp.where(lane_group == g, window, jnp.zeros_like(window))
            total = total + jnp.dot(toep, masked, preferred_element_type=F32)
        skip = tab_all[0, 12:13, lanes]
        for b in range(2):
            for s in range(2):
                at = b * 384 + 128 + s * 128
                part = total[:, (2 * b + s) * 128 : (2 * b + s + 1) * 128]
                mixed = filtered[at : at + 128, 0:128] * (part + skip * gated[at : at + 128])
                mix_ref[b * 256 + s * 128 : b * 256 + (s + 1) * 128, lanes] = mixed.astype(BF16)
        return 0

    lax.fori_loop(0, 4, chunk, 0)
    gh.z_step(4)
    gh.z_step(5)
    for n, k in enumerate(KIND_ORDER):
        lax.fori_loop(4 + 2 * n, 6 + 2 * n, chunk, 0)
        for side in range(3):
            gh.plane_step(side, k)
    gh.finish()
    for c in small:
        c.wait_send()


def hyena(ids8, hit, emb4, gain, in_proj, short, taps, skip, wh):
    dma = pltpu.SemaphoreType.DMA
    vmem = pl.BlockSpec(memory_space=pltpu.VMEM)
    return pl.pallas_call(
        hyena_kernel,
        out_shape=(
            jax.ShapeDtypeStruct((512, 2048), BF16),
            jax.ShapeDtypeStruct((512, 32), BF16),
            jax.ShapeDtypeStruct((2048, 4096), BF16),
        ),
        in_specs=[vmem, pl.BlockSpec(memory_space=pltpu.SMEM), vmem, vmem, ANY, vmem, vmem, vmem, ANY],
        out_specs=(vmem, vmem, ANY),
        scratch_shapes=[
            pltpu.VMEM((64, 8, 128), jnp.int32),
            pltpu.VMEM((3, 16, 2048), F32),
            pltpu.VMEM((128, 256), F32),
            pltpu.VMEM((768, 32), BF16),
            pltpu.VMEM(in_proj.shape, BF16),
            pltpu.VMEM(wh.shape, BF16),
            dma((N_SENDS,)), dma((48,)), dma((2,)),
            dma((9,)), dma((9,)), dma((3,)), dma((3,)), dma((3,)), dma((3,)), dma((3,)),
        ],
        compiler_params=pltpu.CompilerParams(
            collective_id=0, has_side_effects=True, vmem_limit_bytes=48 * 2**20
        ),
        name="hyena",
    )(ids8, hit, emb4, gain, in_proj, short, taps, skip, wh)


def proj_kernel(t_ref, mix_ref, wh_ref, code_ref, emb_ref, gain_ref, wq_ref, cos_ref, sin_ref,
                own_ref, qkv_ref, attn_in, chunk, squares):
    i = pl.program_id(0)

    @pl.when(i < 8)
    def _():
        vals = jnp.dot(mix_ref[...], wh_ref[...], preferred_element_type=F32)
        vals = vals + jnp.dot(code_ref[...], emb_ref[...], preferred_element_type=F32)
        chunk[...] = vals
        part = jnp.sum(vals * vals, axis=1, keepdims=True)

        @pl.when(i == 0)
        def _():
            squares[...] = jnp.zeros_like(squares)

        squares[...] += jnp.broadcast_to(part, squares.shape)
        attn_in[:, pl.ds(pl.multiple_of(i * 512, 512), 512)] = (vals * gain_ref[...]).astype(BF16)
        own_ref[...] = chunk[pl.ds(pl.multiple_of(t_ref[0] * 128, 128), 128), :]

    @pl.when(i >= 8)
    def _():
        k = i - 8
        j = k // 2
        factor = lax.rsqrt(squares[...] / 4096.0 + EPS)
        factor = factor * jnp.where(j == 0, HD**-0.5 * math.log2(math.e), 1.0).astype(F32)
        rotated = j < 2
        cos = jnp.where(rotated, cos_ref[...], 1.0) * factor
        sin = jnp.where(rotated, sin_ref[...], 0.0) * factor
        vals = jnp.dot(attn_in[...], wq_ref[0], preferred_element_type=F32)
        for hh in range(2):
            head = vals[:, hh * 128 : (hh + 1) * 128]
            turned = head * cos + pltpu.roll(head, 64, 1) * sin
            qkv_ref[2 * (k % 2) + hh, j] = turned.astype(BF16).reshape(2, 4, 64, 128)


def stream_qkv(t_arr, mix, wh, code_hot, emb4, gain, wq, cos, sin):
    def whi(i, t):
        return (0, jnp.minimum(i, 7))

    def wqi(i, t):
        k = jnp.maximum(i - 8, 0)
        return (k // 2, 0, k % 2)

    def whole(*shape):
        return pl.BlockSpec(shape, lambda i, t: (0,) * len(shape))

    return pl.pallas_call(
        proj_kernel,
        out_shape=(
            jax.ShapeDtypeStruct((128, 4096), F32),
            jax.ShapeDtypeStruct((4, 3, 2, 4, 64, 128), BF16),
        ),
        grid_spec=pltpu.PrefetchScalarGridSpec(
            num_scalar_prefetch=1,
            grid=(14,),
            in_specs=[
                whole(512, 2048),
                pl.BlockSpec((2048, 512), whi),
                whole(512, 32),
                pl.BlockSpec((32, 512), whi),
                pl.BlockSpec((1, 512), whi),
                pl.BlockSpec((1, 4096, 256), wqi),
                whole(512, 128),
                whole(512, 128),
            ],
            out_specs=(
                pl.BlockSpec((128, 512), whi),
                whole(4, 3, 2, 4, 64, 128),
            ),
            scratch_shapes=[
                pltpu.VMEM((512, 4096), BF16),
                pltpu.VMEM((512, 512), F32),
                pltpu.VMEM((512, 128), F32),
            ],
        ),
        compiler_params=pltpu.CompilerParams(vmem_limit_bytes=48 * 2**20),
        name="stream_qkv",
    )(t_arr, mix, wh, code_hot, emb4, gain, wq, cos, sin)


def ab_of(dp, y, x):
    return pick(dp, y, x), pick(dp, x, y)


def ctx_of(dp, a, b):
    return pick(dp, a * 4 + b, b * 4 + a)


def exchange_kernel(qkv_ref, q_out, kv_out, sq, rq, s1, r1, s2, r2, s3, r3, loc):
    dp, y, x, t = coords()
    ctx = y * 4 + x
    a, b = ab_of(dp, y, x)
    barrier = pltpu.get_barrier_semaphore()
    others = [{"context": (ctx + d) % 16} for d in range(1, 16)]
    for where in others:
        pl.semaphore_signal(barrier, inc=1, device_id=where, device_id_type=MESH_ID)
    pl.semaphore_wait(barrier, 15)
    sent = []
    keep_kv = pltpu.make_async_copy(qkv_ref.at[a, pl.ds(1, 2)], kv_out.at[ctx], loc.at[0])
    keep_kv.start()
    bp = {"context": ctx_of(dp, a, (b + 1) % 4)}
    bm = {"context": ctx_of(dp, a, (b + 3) % 4)}

    def spread(src, k, src_ctx):
        for side, where in ((0, bp), (1, bm)):
            c = remote(src, kv_out.at[src_ctx], s2.at[side * 4 + k], r2.at[side * 4 + k], where)
            c.start()
            sent.append(c)

    for d in (1, 3, 2):
        h = (a + d) % 4
        c = remote(qkv_ref.at[h, pl.ds(1, 2)], kv_out.at[ctx], s1.at[d - 1], r1.at[d - 1], {"context": ctx_of(dp, h, b)})
        c.start()
        sent.append(c)
    spread(qkv_ref.at[a, pl.ds(1, 2)], 0, ctx)
    for d in range(1, 16):
        to = (ctx + d) % 16
        h, s = ab_of(dp, to // 4, to % 4)
        c = remote(qkv_ref.at[h, 0, :, s], q_out.at[ctx], sq.at[d - 1], rq.at[d - 1], others[d - 1])
        c.start()
        sent.append(c)
    keep_q = pltpu.make_async_copy(qkv_ref.at[a, 0, :, b], q_out.at[ctx], loc.at[1])
    keep_q.start()
    for d in (1, 3, 2):
        from_ctx = ctx_of(dp, (a + 4 - d) % 4, b)
        ref = kv_out.at[from_ctx]
        remote(ref, ref, s1.at[0], r1.at[d - 1], bp).wait_recv()
        spread(ref, d, from_ctx)
    for k in (0, 1, 3, 2):
        ua = (a + 4 - k) % 4
        ref = kv_out.at[ctx_of(dp, ua, (b + 3) % 4)]
        remote(ref, ref, s1.at[0], r2.at[k], bp).wait_recv()
        c = remote(ref.at[0], ref.at[0], s3.at[k], r3.at[k], bp)
        c.start()
        sent.append(c)
        ref = kv_out.at[ctx_of(dp, ua, (b + 1) % 4)]
        remote(ref, ref, s1.at[0], r2.at[4 + k], bp).wait_recv()
        c = remote(ref.at[1], ref.at[1], s3.at[4 + k], r3.at[4 + k], bm)
        c.start()
        sent.append(c)
    for k in (0, 1, 3, 2):
        ref = kv_out.at[ctx_of(dp, (a + 4 - k) % 4, (b + 2) % 4)]
        for part in (0, 1):
            remote(ref.at[part], ref.at[part], s1.at[0], r3.at[4 * part + k], bp).wait_recv()
    for d in range(1, 16):
        ref = q_out.at[(ctx + 16 - d) % 16]
        remote(ref, ref, s1.at[0], rq.at[d - 1], bp).wait_recv()
    for c in sent:
        c.wait_send()
    keep_q.wait()
    keep_kv.wait()


def exchange(qkv):
    dma = pltpu.SemaphoreType.DMA
    return pl.pallas_call(
        exchange_kernel,
        out_shape=(
            jax.ShapeDtypeStruct((16, 2, 64, 128), BF16),
            jax.ShapeDtypeStruct((16, 2, 2, 4, 64, 128), BF16),
        ),
        in_specs=[ANY],
        out_specs=(ANY,) * 2,
        scratch_shapes=[dma((15,)), dma((15,)), dma((3,)), dma((3,)), dma((8,)), dma((8,)), dma((8,)), dma((8,)), dma((2,))],
        compiler_params=pltpu.CompilerParams(collective_id=1, has_side_effects=True),
        name="exchange",
    )(qkv)


def attend_kernel(slot_ref, q_ref, kv_ref, o_ref):
    b = slot_ref[32]

    def q_tile(tile):
        parts = []
        for p in range(4 * tile, 4 * tile + 4):
            slot = slot_ref[p]
            parts.append(q_ref[slot // 2, slot % 2])
        return jnp.concatenate(parts, axis=0)

    def step(queries, carries, block, masked):
        slots = [slot_ref[block + n] for n in range(4)]
        keys = [kv_ref[s // 2, 0, s % 2] for s in slots]
        vals = [kv_ref[s // 2, 1, s % 2] for s in slots]
        scores = [
            [lax.dot_general(q, k, (((1,), (1,)), ((), ())), preferred_element_type=F32) for k in keys] for q in queries
        ]
        done = []
        for (top, tot, acc), score in zip(carries, scores):
            if masked:
                for n in range(4):
                    r = lax.broadcasted_iota(jnp.int32, (256, 256), 0)
                    col = lax.broadcasted_iota(jnp.int32, (256, 256), 1) + n * 256
                    score[n] = jnp.where(col <= (r // 64) * 256 + b * 64 + r % 64, score[n], NEG_FILL)
            most = functools.reduce(jnp.maximum, score)
            new = jnp.maximum(top, jnp.max(most, axis=1, keepdims=True))
            shrink = jnp.exp2(top - new)
            weights = [jnp.exp2(s - new) for s in score]
            tot = tot * shrink + jnp.sum(functools.reduce(jnp.add, weights), axis=1, keepdims=True)
            for n, (w, v) in enumerate(zip(weights, vals)):
                part = jnp.dot(w.astype(BF16), v, preferred_element_type=F32)
                add = part if n == 0 else add + part
            done.append((new, tot, acc * shrink + add))
        return tuple(done)

    start = (jnp.full((256, 1), NEG_FILL, F32), jnp.zeros((256, 1), F32), jnp.zeros((256, 128), F32))
    for j in range(0, 8, 2):
        q0, q1 = q_tile(j), q_tile(j + 1)
        c0 = step([q0], [start], 4 * j, True)[0]
        c1 = step([q1], [start], 4 * j + 4, True)[0]
        c1 = step([q1], [c1], 4 * j, False)[0]
        carries = (c0, c1)
        if j:
            carries = lax.fori_loop(0, j, lambda n, c: step([q0, q1], c, 4 * n, False), carries, unroll=2)
        for tile in range(2):
            _, tot, acc = carries[tile]
            out = (acc / tot).astype(BF16)
            for n in range(4):
                o_ref[slot_ref[4 * (j + tile) + n]] = out[n * 64 : (n + 1) * 64]


def attend(slots, q_all, kv_all):
    vmem = pl.BlockSpec(memory_space=pltpu.VMEM)
    return pl.pallas_call(
        attend_kernel,
        out_shape=jax.ShapeDtypeStruct((32, 64, 128), BF16),
        in_specs=[pl.BlockSpec(memory_space=pltpu.SMEM), vmem, vmem],
        out_specs=vmem,
        compiler_params=pltpu.CompilerParams(vmem_limit_bytes=48 * 2**20),
        name="attend",
    )(slots, q_all, kv_all)


def return_kernel(o_ref, att_out, send, recv, loc):
    dp, y, x, t = coords()
    ctx = y * 4 + x
    a, b = ab_of(dp, y, x)
    barrier = pltpu.get_barrier_semaphore()

    def source(n):
        st, sa, r = n // 8, (n // 2) % 4, n % 2
        return st, ctx_of(dp, sa, 2 * (t % 2) + r)

    def dest(n):
        return 2 * (n % 2) + b // 2, n // 2

    def hello(n, _):
        st, sc = source(n)

        @pl.when(jnp.logical_or(st != t, sc != ctx))
        def _():
            pl.semaphore_signal(barrier, inc=1, device_id={"context": sc, "tensor": st}, device_id_type=MESH_ID)

        return 0

    lax.fori_loop(0, 32, hello, 0)
    has_self = (b // 2 == t % 2).astype(jnp.int32)
    pl.semaphore_wait(barrier, 32 - has_self)
    mine = (t * 4 + a) * 2 + b % 2

    def out_copy(n):
        dt, dc = dest(n)
        return remote(o_ref.at[n], att_out.at[mine], send.at[n], recv.at[mine], {"context": dc, "tensor": dt}), dt, dc

    def start(k, _):
        n = (k + 2 * ctx) % 32
        copy, dt, dc = out_copy(n)
        self_copy = jnp.logical_and(dt == t, dc == ctx)

        @pl.when(jnp.logical_not(self_copy))
        def _():
            copy.start()

        @pl.when(self_copy)
        def _():
            pltpu.make_async_copy(o_ref.at[n], att_out.at[mine], loc).start()

        return 0

    lax.fori_loop(0, 32, start, 0)

    def finish(n, _):
        st, sc = source(n)

        @pl.when(jnp.logical_or(st != t, sc != ctx))
        def _():
            ref = att_out.at[n]
            remote(ref, ref, send.at[0], recv.at[n], {"dp": 1 - dp}).wait_recv()

        copy, dt, dc = out_copy(n)
        self_copy = jnp.logical_and(dt == t, dc == ctx)

        @pl.when(jnp.logical_not(self_copy))
        def _():
            copy.wait_send()

        @pl.when(self_copy)
        def _():
            pltpu.make_async_copy(o_ref.at[n], att_out.at[mine], loc).wait()

        return 0

    lax.fori_loop(0, 32, finish, 0)


def give_back(o):
    dma = pltpu.SemaphoreType.DMA
    return pl.pallas_call(
        return_kernel,
        out_shape=jax.ShapeDtypeStruct((32, 64, 128), BF16),
        in_specs=[ANY],
        out_specs=ANY,
        scratch_shapes=[dma((32,)), dma((32,)), dma],
        compiler_params=pltpu.CompilerParams(collective_id=2, has_side_effects=True),
        name="give_back",
    )(o)


def body(ids, block_order, embed, mix_gain, in_proj, short_filter, long_filter, conv_skip,
         hyena_out, attn_gain, qkv_proj, attn_out):
    dp, y, x, t = coords()
    ctx = y * 4 + x
    emb4 = jnp.concatenate([embed[c : c + 1] for c in CODES] + [jnp.zeros((28, embed.shape[1]), BF16)], axis=0)
    taps = jnp.concatenate(
        [jnp.zeros((32, 1), F32), long_filter[:, ::-1], jnp.zeros((32, 127), F32)], axis=1
    )
    slot_ids = jnp.arange(32, dtype=jnp.int32)
    pair = 2 * ctx + jnp.arange(2, dtype=jnp.int32)
    owned = jnp.sum(jnp.where(slot_ids[None] == pair[:, None], block_order[None], 0), axis=1)
    hit = (block_order[None, :] == owned[:, None] - 1).astype(jnp.int32).reshape(64)
    ids8 = jnp.broadcast_to(ids.reshape(1, 128), (8, 128))
    mix, code_hot, wh = hyena(
        ids8, hit, emb4, mix_gain.reshape(1, -1), in_proj, short_filter, taps, conv_skip.reshape(1, -1), hyena_out
    )
    wa = lax.all_gather(
        lax.dynamic_slice_in_dim(attn_out, (dp * 16 + ctx) * 16, 16, 0), ("tensor", "dp", "context"), axis=0, tiled=True
    )

    local_pos = (owned[:, None] * 256 + jnp.arange(256, dtype=jnp.int32)[None]).reshape(512)
    inverse_freq = THETA ** (-(2.0 * jnp.arange(64, dtype=F32)) / HD)
    angles = local_pos.astype(F32)[:, None] * inverse_freq[None, :]
    cos, sin = jnp.cos(angles), jnp.sin(angles)
    cos = jnp.concatenate([cos, cos], axis=1)
    sin = jnp.concatenate([-sin, sin], axis=1)
    stream_own, qkv = stream_qkv(
        t.astype(jnp.int32).reshape(1), mix, wh, code_hot, emb4, attn_gain.reshape(1, -1), qkv_proj, cos, sin
    )
    q_all, kv_all = exchange(qkv)
    slot_of = jnp.sum(jnp.where(block_order[None, :] == slot_ids[:, None], slot_ids[None, :], 0), axis=1)
    _, b = ab_of(dp, y, x)
    slots = jnp.concatenate([slot_of, b.astype(jnp.int32).reshape(1)])
    att = attend(slots, q_all, kv_all.reshape(16, 2, 2, 256, 128))
    att = give_back(att)
    att = att.reshape(16, 128, 128).transpose(1, 0, 2).reshape(128, 2048)
    return stream_own + jnp.dot(att, wa, preferred_element_type=F32)


def solution(mesh):
    placed = (
        P(("dp", "context", "tensor")),
        P("dp"),
        P(),
        P(),
        P(None, None, "tensor"),
        P(None, None, "tensor"),
        P("tensor", None),
        P("tensor"),
        P("tensor", None),
        P(),
        P(None, None, "tensor"),
        P("tensor", None),
    )
    return jax.shard_map(
        body,
        mesh=mesh,
        in_specs=placed,
        out_specs=P(("dp", "context", "tensor"), None),
        check_vma=False,
    )
```

```python
import functools
import math

import jax
import jax.numpy as jnp
from jax import lax
from jax.experimental import pallas as pl
from jax.experimental.pallas import tpu as pltpu
from jax.sharding import PartitionSpec as P

HD = 128
EPS = 1e-06
THETA = 1000000.0
NEG_FILL = -1e30
CODES = (65, 67, 71, 84)
MESH_ID = pl.DeviceIdType.MESH
F32 = jnp.float32
BF16 = jnp.bfloat16
ANY = pl.BlockSpec(memory_space=pl.ANY)


def coords():
    dp = lax.axis_index("dp")
    ctx = lax.axis_index("context")
    t = lax.axis_index("tensor")
    return dp, ctx // 4, ctx % 4, t


def pick(dp, first, second):
    return first + dp * (second - first)


def remote(src, dst, send, recv, where):
    return pltpu.make_async_remote_copy(
        src_ref=src, dst_ref=dst, send_sem=send, recv_sem=recv, device_id=where, device_id_type=MESH_ID
    )


ZKINDS = ((3, 0), (3, 1), (1, 0), (1, 1), (2, 0), (2, 1))


class WeightGather:
    def __init__(self, w_in, w_out, send, recv, hold, local_sem):
        self.w_in, self.w_out, self.send, self.recv = w_in, w_out, send, recv
        self.hold, self.local_sem = hold, local_sem
        dp, y, x, t = coords()
        self.dp, self.t = dp, t
        u, w = pick(dp, x, y), pick(dp, y, x)
        self.q = (u + 2 * w) % 4
        self.sib_q = (w + 2 * u) % 4
        self.shard = w_in.shape[0]
        self.piece = self.shard // 16
        xp, xm, yp, ym = (x + 1) % 4, (x + 3) % 4, (y + 1) % 4, (y + 3) % 4
        self.up = {"context": pick(dp, y * 4 + xp, yp * 4 + x)}
        self.um = {"context": pick(dp, y * 4 + xm, ym * 4 + x)}
        self.wp = {"context": pick(dp, yp * 4 + x, y * 4 + xp)}
        self.wm = {"context": pick(dp, ym * 4 + x, y * 4 + xm)}
        self.zp = {"tensor": (t + 1) % 4}
        self.zm = {"tensor": (t + 3) % 4}
        self.sib = {"dp": 1 - dp}
        self.pending = []

    def unit(self, z, dp, q, h):
        start = z * self.shard + dp * (self.shard // 2) + q * (2 * self.piece) + h * self.piece
        return self.w_out.at[pl.ds(pl.multiple_of(start, self.piece), self.piece), :]

    def own(self, h):
        start = self.dp * (self.shard // 2) + self.q * (2 * self.piece) + h * self.piece
        return self.w_in.at[pl.ds(pl.multiple_of(start, self.piece), self.piece), :]

    def go(self, src, dst, recv_at, where):
        at = len(self.pending)
        copy = remote(src, dst, self.send.at[at], self.recv.at[recv_at], where)
        copy.start()
        self.pending.append(copy)

    def arrived(self, dst, recv_at):
        remote(dst, dst, self.send.at[0], self.recv.at[recv_at], self.sib).wait_recv()

    def start(self):
        self.load = pltpu.make_async_copy(self.w_in, self.hold, self.local_sem.at[0])
        self.load.start()
        for h in (0, 1):
            dst = self.unit(self.t, self.dp, self.q, h)
            first, second = ((self.zp, 0 + h), (self.zm, 2 + h))
            if h == 0:
                self.go(self.own(h), dst, first[1], first[0])
                self.go(self.own(1), self.unit(self.t, self.dp, self.q, 1), 3, self.zm)
            else:
                self.go(self.own(1), dst, 1, self.zp)
                self.go(self.own(0), self.unit(self.t, self.dp, self.q, 0), 2, self.zm)

    def keep(self):
        row = pl.multiple_of(self.t * self.shard, self.shard)
        self.load.wait()
        self.local = pltpu.make_async_copy(self.hold, self.w_out.at[pl.ds(row, self.shard), :], self.local_sem.at[1])
        self.local.start()

    def z_step(self, kind):
        zoff, h = ZKINDS[kind]
        ref = self.unit((self.t + zoff) % 4, self.dp, self.q, h)
        self.arrived(ref, kind)
        if kind == 0:
            self.go(ref, ref, 4, self.zp)
        if kind == 3:
            self.go(ref, ref, 5, self.zm)
        self.go(ref, ref, 6 + kind, self.up)
        self.go(ref, ref, 12 + kind, self.um)
        self.go(ref, ref, 18 + kind, self.wp if h == 0 else self.wm)
        self.go(ref, ref, 24 + kind, self.sib)

    def plane_ref(self, side, kind, dp, q):
        zoff, h = ZKINDS[kind]
        qoff = (3, 1, 2)[side]
        return self.unit((self.t + zoff) % 4, dp, (q + qoff) % 4, h)

    def plane_step(self, side, kind):
        at = 6 + 6 * side + kind
        ref = self.plane_ref(side, kind, self.dp, self.q)
        self.arrived(ref, at)
        self.go(ref, ref, 24 + at, self.sib)

    def finish(self):
        for kind in range(6):
            zoff, h = ZKINDS[kind]
            self.arrived(self.unit((self.t + zoff) % 4, 1 - self.dp, self.sib_q, h), 24 + kind)
            for side in range(3):
                self.arrived(self.plane_ref(side, kind, 1 - self.dp, self.sib_q), 30 + 6 * side + kind)
        for copy in self.pending:
            copy.wait_send()
        self.local.wait()


KIND_ORDER = (0, 3, 1, 2, 4, 5)
N_SENDS = 6 + 18 + 24


def code_rows(shape):
    k = lax.broadcasted_iota(jnp.int32, shape, 0) % 4
    return jnp.where(k < 2, jnp.where(k == 0, CODES[0], CODES[1]), jnp.where(k == 2, CODES[2], CODES[3]))


def hyena_kernel(ids_ref, hit_ref, emb_ref, gain_ref, proj_ref, short_ref, taps_ref, skip_ref, wh_ref,
                 mix_ref, hot_out, wh_out,
                 ids_all, tab_all, taps_all, hots, proj_s, hold,
                 s_w, r_w, loc_w, s_ids, r_ids, s_tab, r_tab, s_taps, r_taps, p_sem):
    dp, y, x, t = coords()
    ctx = y * 4 + x
    loads = [pltpu.make_async_copy(proj_ref.at[j], proj_s.at[j], p_sem.at[j]) for j in range(3)]
    for c in loads:
        c.start()
    barrier = pltpu.get_barrier_semaphore()
    zs = [{"tensor": (t + d) % 4} for d in (1, 2, 3)]
    xs = [{"context": y * 4 + (x + d) % 4} for d in (1, 2, 3)]
    ys = [{"context": ((y + d) % 4) * 4 + x} for d in (1, 2, 3)]
    partners = zs + xs + ys + [{"dp": 1 - dp}]
    for where in partners:
        pl.semaphore_signal(barrier, inc=1, device_id=where, device_id_type=MESH_ID)
    mine = ctx * 4 + t
    ids_all[mine] = ids_ref[...]
    trow = pl.ds(pl.multiple_of(t * 32, 32), 32)
    taps_all[trow, :] = taps_ref[...]
    pl.semaphore_wait(barrier, len(partners))

    small = []

    def go(src, send, recv, where):
        c = remote(src, src, send, recv, where)
        c.start()
        small.append(c)

    def landed(ref, recv):
        remote(ref, ref, s_ids.at[0], recv, zs[0]).wait_recv()

    gh = WeightGather(wh_ref, wh_out, s_w, r_w, hold, loc_w)
    for d in (0, 1, 2):
        go(ids_all.at[pl.ds(mine, 1)], s_ids.at[d], r_ids.at[d], zs[d])
    gh.start()
    for d in (0, 1, 2):
        go(taps_all.at[trow, :], s_taps.at[d], r_taps.at[d], zs[d])

    wide = emb_ref[...].astype(F32)
    square = jnp.sum(wide * wide, axis=1, keepdims=True)
    normed = (wide * lax.rsqrt(square / 4096.0 + EPS) * gain_ref[...]).astype(BF16)
    cols = pl.ds(pl.multiple_of(t * 512, 512), 512)
    for j in range(3):
        loads[j].wait()
        rows = jnp.dot(normed, proj_s[j], preferred_element_type=F32).astype(BF16).astype(F32)[0:4]
        last = jnp.broadcast_to(skip_ref[...], (4, 512))
        tab_all[j, :, cols] = jnp.concatenate([short_ref[j, tap : tap + 1, :] * rows for tap in range(3)] + [last], axis=0)
    for d in (0, 1, 2):
        go(tab_all.at[:, :, cols], s_tab.at[d], r_tab.at[d], zs[d])
    for d in (0, 1, 2):
        landed(ids_all.at[pl.ds(ctx * 4 + (t + 3 - d) % 4, 1)], r_ids.at[d])
    for d in (0, 1, 2):
        go(ids_all.at[pl.ds(ctx * 4, 4)], s_ids.at[3 + d], r_ids.at[3 + d], xs[d])
    gh.z_step(0)
    gh.z_step(3)
    for d in (0, 1, 2):
        landed(ids_all.at[pl.ds((y * 4 + (x + 3 - d) % 4) * 4, 4)], r_ids.at[3 + d])
    for d in (0, 1, 2):
        go(ids_all.at[pl.ds(y * 16, 16)], s_ids.at[6 + d], r_ids.at[6 + d], ys[d])
    gh.z_step(1)
    gh.z_step(2)
    gh.keep()
    for d in (0, 1, 2):
        landed(ids_all.at[pl.ds(((y + 3 - d) % 4) * 16, 16)], r_ids.at[6 + d])
        zrow = pl.ds(pl.multiple_of(((t + 3 - d) % 4) * 32, 32), 32)
        landed(taps_all.at[zrow, :], r_taps.at[d])
        landed(tab_all.at[:, :, pl.ds(pl.multiple_of(((t + 3 - d) % 4) * 512, 512), 512)], r_tab.at[d])

    row8 = lax.broadcasted_iota(jnp.int32, (8, 384), 0)
    code8 = code_rows((8, 384))
    for b in range(2):
        prev = [jnp.zeros((8, 128), jnp.int32) for _ in range(2)]
        for slot in range(32):
            hit = hit_ref[b * 32 + slot]
            for half in range(2):
                prev[half] = prev[half] + hit * ids_all[2 * slot + half]
        own = [ids_all[ctx * 4 + 2 * b + half] for half in range(2)]
        line = jnp.concatenate(prev + own, axis=1)
        back = [line[:, 128:]] + [pltpu.roll(line, tap, 1)[:, 128:] for tap in (1, 2)]
        top = jnp.where(jnp.where(row8 < 4, back[0], back[1]) == code8, 1.0, 0.0)
        low = jnp.where(row8 < 4, jnp.where(back[2] == code8, 1.0, 0.0), 0.0)
        hots[b * 384 : (b + 1) * 384, :] = jnp.concatenate([top, low, top, low], axis=0).T.astype(BF16)
        hot_out[b * 256 : (b + 1) * 256, :] = hots[b * 384 + 128 : (b + 1) * 384, :]

    def chunk(i, _):
        lanes = pl.ds(pl.multiple_of(i * 128, 128), 128)
        table = jnp.concatenate([tab_all[j, :, lanes] for j in range(3)], axis=1)
        high = table.astype(BF16)
        low = (table - high.astype(F32)).astype(BF16)
        both = jnp.concatenate([high, low], axis=0)
        filtered = jnp.dot(hots[...], both, preferred_element_type=F32)
        gated = filtered[:, 128:256] * filtered[:, 256:384]
        g16 = gated.astype(BF16)
        window = jnp.concatenate(
            [g16[b * 384 + s * 128 : b * 384 + s * 128 + 256] for b in range(2) for s in range(2)], axis=1
        )
        lane_group = (lax.broadcasted_iota(jnp.int32, window.shape, 1) % 128) // 16
        taps = taps_all[pl.ds(pl.multiple_of(i * 8, 8), 8), :]
        total = jnp.zeros((128, 512), F32)
        for g in range(8):
            base = jnp.broadcast_to(taps[g : g + 1, :], (128, 256))
            toep = pltpu.roll(base, 0, 1, stride=1, stride_axis=0).astype(BF16)
            masked = jnp.where(lane_group == g, window, jnp.zeros_like(window))
            total = total + jnp.dot(toep, masked, preferred_element_type=F32)
        skip = tab_all[0, 12:13, lanes]
        for b in range(2):
            for s in range(2):
                at = b * 384 + 128 + s * 128
                part = total[:, (2 * b + s) * 128 : (2 * b + s + 1) * 128]
                mixed = filtered[at : at + 128, 0:128] * (part + skip * gated[at : at + 128])
                mix_ref[b * 256 + s * 128 : b * 256 + (s + 1) * 128, lanes] = mixed.astype(BF16)
        return 0

    lax.fori_loop(0, 4, chunk, 0)
    gh.z_step(4)
    gh.z_step(5)
    for n, k in enumerate(KIND_ORDER):
        lax.fori_loop(4 + 2 * n, 6 + 2 * n, chunk, 0)
        for side in range(3):
            gh.plane_step(side, k)
    gh.finish()
    for c in small:
        c.wait_send()


def hyena(ids8, hit, emb4, gain, in_proj, short, taps, skip, wh):
    dma = pltpu.SemaphoreType.DMA
    vmem = pl.BlockSpec(memory_space=pltpu.VMEM)
    return pl.pallas_call(
        hyena_kernel,
        out_shape=(
            jax.ShapeDtypeStruct((512, 2048), BF16),
            jax.ShapeDtypeStruct((512, 32), BF16),
            jax.ShapeDtypeStruct((2048, 4096), BF16),
        ),
        in_specs=[vmem, pl.BlockSpec(memory_space=pltpu.SMEM), vmem, vmem, ANY, vmem, vmem, vmem, ANY],
        out_specs=(vmem, vmem, ANY),
        scratch_shapes=[
            pltpu.VMEM((64, 8, 128), jnp.int32),
            pltpu.VMEM((3, 16, 2048), F32),
            pltpu.VMEM((128, 256), F32),
            pltpu.VMEM((768, 32), BF16),
            pltpu.VMEM(in_proj.shape, BF16),
            pltpu.VMEM(wh.shape, BF16),
            dma((N_SENDS,)), dma((48,)), dma((2,)),
            dma((9,)), dma((9,)), dma((3,)), dma((3,)), dma((3,)), dma((3,)), dma((3,)),
        ],
        compiler_params=pltpu.CompilerParams(
            collective_id=0, has_side_effects=True, vmem_limit_bytes=48 * 2**20
        ),
        name="hyena",
    )(ids8, hit, emb4, gain, in_proj, short, taps, skip, wh)


def ab_of(dp, y, x):
    return pick(dp, y, x), pick(dp, x, y)


def ctx_of(dp, a, b):
    return pick(dp, a * 4 + b, b * 4 + a)


ORDER = (1, 3, 2)


def proj_kernel(mix_ref, wh_ref, code_ref, emb_ref, gain_ref, wq_ref, cos_ref, sin_ref,
                own_ref, q_out, kv_out, attn_in, chunk, squares, qkv, s1, r1, s2, r2, s3, r3, sq, rq, loc):
    i = pl.program_id(0)
    dp, y, x, t = coords()
    ctx = y * 4 + x
    a, b = ab_of(dp, y, x)
    others = [{"context": (ctx + d) % 16} for d in range(1, 16)]
    barrier = pltpu.get_barrier_semaphore()

    @pl.when(i == 0)
    def _():
        squares[...] = jnp.zeros_like(squares)
        for where in others:
            pl.semaphore_signal(barrier, inc=1, device_id=where, device_id_type=MESH_ID)

    @pl.when(i < 8)
    def _():
        vals = jnp.dot(mix_ref[...], wh_ref[...], preferred_element_type=F32)
        vals = vals + jnp.dot(code_ref[...], emb_ref[...], preferred_element_type=F32)
        chunk[...] = vals
        part = jnp.sum(vals * vals, axis=1, keepdims=True)
        squares[...] += jnp.broadcast_to(part, squares.shape)
        attn_in[:, pl.ds(pl.multiple_of(i * 512, 512), 512)] = (vals * gain_ref[...]).astype(BF16)
        own_ref[...] = chunk[pl.ds(pl.multiple_of(t * 128, 128), 128), :]

    @pl.when(i >= 8)
    def _():
        k = i - 8
        j = (k // 2 + 1) % 3
        factor = lax.rsqrt(squares[...] / 4096.0 + EPS)
        factor = factor * jnp.where(j == 0, HD**-0.5 * math.log2(math.e), 1.0).astype(F32)
        rotated = j < 2
        cos = jnp.where(rotated, cos_ref[...], 1.0) * factor
        sin = jnp.where(rotated, sin_ref[...], 0.0) * factor
        vals = jnp.dot(attn_in[...], wq_ref[0], preferred_element_type=F32)
        for hh in range(2):
            head = vals[:, hh * 128 : (hh + 1) * 128]
            turned = head * cos + pltpu.roll(head, 64, 1) * sin
            qkv[2 * (k % 2) + hh, j] = turned.astype(BF16).reshape(2, 4, 64, 128)

    bp = {"context": ctx_of(dp, a, (b + 1) % 4)}
    bm = {"context": ctx_of(dp, a, (b + 3) % 4)}

    def held(part, k, off):
        return kv_out.at[ctx_of(dp, (a + 4 - k) % 4, (b + off) % 4), part]

    def to_head(part, d):
        h = (a + d) % 4
        return remote(qkv.at[h, 1 + part], kv_out.at[ctx, part], s1.at[3 * part + d - 1], r1.at[3 * part + d - 1],
                      {"context": ctx_of(dp, h, b)})

    def spread(part, side, k):
        src = qkv.at[a, 1 + part] if k == 0 else held(part, k, 0)
        at = 8 * part + 4 * side + k
        return remote(src, held(part, k, 0), s2.at[at], r2.at[at], (bp, bm)[side])

    def relay(part, k):
        ref = held(part, k, (3, 1)[part])
        return remote(ref, ref, s3.at[4 * part + k], r3.at[4 * part + k], (bp, bm)[part])

    def query(d):
        to = (ctx + d) % 16
        h, s = ab_of(dp, to // 4, to % 4)
        return remote(qkv.at[h, 0, :, s], q_out.at[ctx], sq.at[d - 1], rq.at[d - 1], others[d - 1])

    def landed(ref, recv):
        remote(ref, ref, s1.at[0], recv, bp).wait_recv()

    keeps = [
        pltpu.make_async_copy(qkv.at[a, 1], kv_out.at[ctx, 0], loc.at[0]),
        pltpu.make_async_copy(qkv.at[a, 2], kv_out.at[ctx, 1], loc.at[1]),
        pltpu.make_async_copy(qkv.at[a, 0, :, b], q_out.at[ctx], loc.at[2]),
    ]

    def leave(part):
        for d in ORDER:
            to_head(part, d).start()
        for side in range(2):
            spread(part, side, 0).start()
        keeps[part].start()

    def pass_on(part):
        for d in ORDER:
            landed(held(part, d, 0), r1.at[3 * part + d - 1])
            for side in range(2):
                spread(part, side, d).start()

    @pl.when(i == 9)
    def _():
        pl.semaphore_wait(barrier, 15)
        leave(0)

    @pl.when(i == 11)
    def _():
        leave(1)
        pass_on(0)

    @pl.when(i == 13)
    def _():
        pass_on(1)
        keeps[2].start()
        for d in range(1, 16):
            query(d).start()
        for part in range(2):
            for k in (0,) + ORDER:
                landed(held(part, k, (3, 1)[part]), r2.at[8 * part + 4 * part + k])
                relay(part, k).start()
        for part in range(2):
            for k in (0,) + ORDER:
                landed(held(part, k, (1, 3)[part]), r2.at[8 * part + 4 * (1 - part) + k])
        for d in range(1, 16):
            landed(q_out.at[(ctx + 16 - d) % 16], rq.at[d - 1])
        for part in range(2):
            for k in (0,) + ORDER:
                landed(held(part, k, 2), r3.at[4 * part + k])
        for part in range(2):
            for d in ORDER:
                to_head(part, d).wait_send()
            for k in range(4):
                for side in range(2):
                    spread(part, side, k).wait_send()
                relay(part, k).wait_send()
        for d in range(1, 16):
            query(d).wait_send()
        for c in keeps:
            c.wait()


def stream_qkv(mix, wh, code_hot, emb4, gain, wq, cos, sin):
    dma = pltpu.SemaphoreType.DMA

    def whi(i):
        return (0, jnp.minimum(i, 7))

    def wqi(i):
        k = jnp.maximum(i - 8, 0)
        return ((k // 2 + 1) % 3, 0, k % 2)

    def whole(*shape):
        return pl.BlockSpec(shape, lambda i: (0,) * len(shape))

    return pl.pallas_call(
        proj_kernel,
        out_shape=(
            jax.ShapeDtypeStruct((128, 4096), F32),
            jax.ShapeDtypeStruct((16, 2, 64, 128), BF16),
            jax.ShapeDtypeStruct((16, 2, 2, 4, 64, 128), BF16),
        ),
        grid=(14,),
        in_specs=[
            whole(512, 2048),
            pl.BlockSpec((2048, 512), whi),
            whole(512, 32),
            pl.BlockSpec((32, 512), whi),
            pl.BlockSpec((1, 512), whi),
            pl.BlockSpec((1, 4096, 256), wqi),
            whole(512, 128),
            whole(512, 128),
        ],
        out_specs=(pl.BlockSpec((128, 512), whi), ANY, ANY),
        scratch_shapes=[
            pltpu.VMEM((512, 4096), BF16),
            pltpu.VMEM((512, 512), F32),
            pltpu.VMEM((512, 128), F32),
            pltpu.VMEM((4, 3, 2, 4, 64, 128), BF16),
            dma((6,)), dma((6,)), dma((16,)), dma((16,)), dma((8,)), dma((8,)), dma((15,)), dma((15,)), dma((3,)),
        ],
        compiler_params=pltpu.CompilerParams(
            collective_id=1, has_side_effects=True, vmem_limit_bytes=48 * 2**20
        ),
        name="stream_qkv",
    )(mix, wh, code_hot, emb4, gain, wq, cos, sin)


def attend_kernel(slot_ref, q_ref, kv_ref, o_ref):
    b = slot_ref[32]

    def q_tile(tile):
        parts = []
        for p in range(4 * tile, 4 * tile + 4):
            slot = slot_ref[p]
            parts.append(q_ref[slot // 2, slot % 2])
        return jnp.concatenate(parts, axis=0)

    def step(queries, carries, block, masked):
        slots = [slot_ref[block + n] for n in range(4)]
        keys = [kv_ref[s // 2, 0, s % 2] for s in slots]
        vals = [kv_ref[s // 2, 1, s % 2] for s in slots]
        scores = [
            [lax.dot_general(q, k, (((1,), (1,)), ((), ())), preferred_element_type=F32) for k in keys] for q in queries
        ]
        done = []
        for (top, tot, acc), score in zip(carries, scores):
            if masked:
                for n in range(4):
                    r = lax.broadcasted_iota(jnp.int32, (256, 256), 0)
                    col = lax.broadcasted_iota(jnp.int32, (256, 256), 1) + n * 256
                    score[n] = jnp.where(col <= (r // 64) * 256 + b * 64 + r % 64, score[n], NEG_FILL)
            most = functools.reduce(jnp.maximum, score)
            new = jnp.maximum(top, jnp.max(most, axis=1, keepdims=True))
            shrink = jnp.exp2(top - new)
            weights = [jnp.exp2(s - new) for s in score]
            tot = tot * shrink + jnp.sum(functools.reduce(jnp.add, weights), axis=1, keepdims=True)
            for n, (w, v) in enumerate(zip(weights, vals)):
                part = jnp.dot(w.astype(BF16), v, preferred_element_type=F32)
                add = part if n == 0 else add + part
            done.append((new, tot, acc * shrink + add))
        return tuple(done)

    start = (jnp.full((256, 1), NEG_FILL, F32), jnp.zeros((256, 1), F32), jnp.zeros((256, 128), F32))
    for j in range(0, 8, 2):
        q0, q1 = q_tile(j), q_tile(j + 1)
        c0 = step([q0], [start], 4 * j, True)[0]
        c1 = step([q1], [start], 4 * j + 4, True)[0]
        c1 = step([q1], [c1], 4 * j, False)[0]
        carries = (c0, c1)
        if j:
            carries = lax.fori_loop(0, j, lambda n, c: step([q0, q1], c, 4 * n, False), carries, unroll=2)
        for tile in range(2):
            _, tot, acc = carries[tile]
            out = (acc / tot).astype(BF16)
            for n in range(4):
                o_ref[4 * (j + tile) + n] = out[n * 64 : (n + 1) * 64]


def attend_return_kernel(slot_ref, q_ref, kv_ref, att_out, o_pos, o_ref, send, recv, loc):
    dp, y, x, t = coords()
    ctx = y * 4 + x
    a, b = ab_of(dp, y, x)
    barrier = pltpu.get_barrier_semaphore()

    def source(n):
        st, sa, r = n // 8, (n // 2) % 4, n % 2
        return st, ctx_of(dp, sa, 2 * (t % 2) + r)

    def dest(n):
        return 2 * (n % 2) + b // 2, n // 2

    def hello(n, _):
        st, sc = source(n)

        @pl.when(jnp.logical_or(st != t, sc != ctx))
        def _():
            pl.semaphore_signal(barrier, inc=1, device_id={"context": sc, "tensor": st}, device_id_type=MESH_ID)

        return 0

    lax.fori_loop(0, 32, hello, 0)
    attend_kernel(slot_ref, q_ref, kv_ref, o_pos)
    for slot in range(32):
        o_ref[slot] = o_pos[slot_ref[33 + slot]]
    has_self = (b // 2 == t % 2).astype(jnp.int32)
    pl.semaphore_wait(barrier, 32 - has_self)
    mine = (t * 4 + a) * 2 + b % 2

    def out_copy(n):
        dt, dc = dest(n)
        return remote(o_ref.at[n], att_out.at[mine], send.at[n], recv.at[mine], {"context": dc, "tensor": dt}), dt, dc

    def start(k, _):
        n = (k + 2 * ctx) % 32
        copy, dt, dc = out_copy(n)
        self_copy = jnp.logical_and(dt == t, dc == ctx)

        @pl.when(jnp.logical_not(self_copy))
        def _():
            copy.start()

        @pl.when(self_copy)
        def _():
            pltpu.make_async_copy(o_ref.at[n], att_out.at[mine], loc).start()

        return 0

    lax.fori_loop(0, 32, start, 0)

    def finish(n, _):
        st, sc = source(n)

        @pl.when(jnp.logical_or(st != t, sc != ctx))
        def _():
            ref = att_out.at[n]
            remote(ref, ref, send.at[0], recv.at[n], {"dp": 1 - dp}).wait_recv()

        copy, dt, dc = out_copy(n)
        self_copy = jnp.logical_and(dt == t, dc == ctx)

        @pl.when(jnp.logical_not(self_copy))
        def _():
            copy.wait_send()

        @pl.when(self_copy)
        def _():
            pltpu.make_async_copy(o_ref.at[n], att_out.at[mine], loc).wait()

        return 0

    lax.fori_loop(0, 32, finish, 0)


def attend_return(slots, q_all, kv_all):
    dma = pltpu.SemaphoreType.DMA
    vmem = pl.BlockSpec(memory_space=pltpu.VMEM)
    return pl.pallas_call(
        attend_return_kernel,
        out_shape=jax.ShapeDtypeStruct((32, 64, 128), BF16),
        in_specs=[pl.BlockSpec(memory_space=pltpu.SMEM), vmem, vmem],
        out_specs=ANY,
        scratch_shapes=[
            pltpu.VMEM((32, 64, 128), BF16), pltpu.VMEM((32, 64, 128), BF16), dma((32,)), dma((32,)), dma
        ],
        compiler_params=pltpu.CompilerParams(
            collective_id=2, has_side_effects=True, vmem_limit_bytes=48 * 2**20
        ),
        name="attend_return",
    )(slots, q_all, kv_all)


def body(ids, block_order, embed, mix_gain, in_proj, short_filter, long_filter, conv_skip,
         hyena_out, attn_gain, qkv_proj, attn_out):
    dp, y, x, t = coords()
    ctx = y * 4 + x
    emb4 = jnp.concatenate([embed[c : c + 1] for c in CODES] + [jnp.zeros((28, embed.shape[1]), BF16)], axis=0)
    taps = jnp.concatenate(
        [jnp.zeros((32, 1), F32), long_filter[:, ::-1], jnp.zeros((32, 127), F32)], axis=1
    )
    slot_ids = jnp.arange(32, dtype=jnp.int32)
    pair = 2 * ctx + jnp.arange(2, dtype=jnp.int32)
    owned = jnp.sum(jnp.where(slot_ids[None] == pair[:, None], block_order[None], 0), axis=1)
    hit = (block_order[None, :] == owned[:, None] - 1).astype(jnp.int32).reshape(64)
    ids8 = jnp.broadcast_to(ids.reshape(1, 128), (8, 128))
    mix, code_hot, wh = hyena(
        ids8, hit, emb4, mix_gain.reshape(1, -1), in_proj, short_filter, taps, conv_skip.reshape(1, -1), hyena_out
    )
    wa = lax.all_gather(
        lax.dynamic_slice_in_dim(attn_out, (dp * 16 + ctx) * 16, 16, 0), ("tensor", "dp", "context"), axis=0, tiled=True
    )

    local_pos = (owned[:, None] * 256 + jnp.arange(256, dtype=jnp.int32)[None]).reshape(512)
    inverse_freq = THETA ** (-(2.0 * jnp.arange(64, dtype=F32)) / HD)
    angles = local_pos.astype(F32)[:, None] * inverse_freq[None, :]
    cos, sin = jnp.cos(angles), jnp.sin(angles)
    cos = jnp.concatenate([cos, cos], axis=1)
    sin = jnp.concatenate([-sin, sin], axis=1)
    stream_own, q_all, kv_all = stream_qkv(
        mix, wh, code_hot, emb4, attn_gain.reshape(1, -1), qkv_proj, cos, sin
    )
    slot_of = jnp.sum(jnp.where(block_order[None, :] == slot_ids[:, None], slot_ids[None, :], 0), axis=1)
    _, b = ab_of(dp, y, x)
    slots = jnp.concatenate([slot_of, b.astype(jnp.int32).reshape(1), block_order])
    att = attend_return(slots, q_all, kv_all.reshape(16, 2, 2, 256, 128))
    att = att.reshape(16, 128, 128).transpose(1, 0, 2).reshape(128, 2048)
    return stream_own + jnp.dot(att, wa, preferred_element_type=F32)


def solution(mesh):
    placed = (
        P(("dp", "context", "tensor")),
        P("dp"),
        P(),
        P(),
        P(None, None, "tensor"),
        P(None, None, "tensor"),
        P("tensor", None),
        P("tensor"),
        P("tensor", None),
        P(),
        P(None, None, "tensor"),
        P("tensor", None),
    )
    return jax.shard_map(
        body,
        mesh=mesh,
        in_specs=placed,
        out_specs=P(("dp", "context", "tensor"), None),
        check_vma=False,
    )
```

```python
import functools
import math

import jax
import jax.numpy as jnp
from jax import lax
from jax.experimental import pallas as pl
from jax.experimental.pallas import tpu as pltpu
from jax.sharding import PartitionSpec as P

HD = 128
EPS = 1e-06
THETA = 1000000.0
NEG_FILL = -1e30
CODES = (65, 67, 71, 84)
MESH_ID = pl.DeviceIdType.MESH
F32 = jnp.float32
BF16 = jnp.bfloat16
ANY = pl.BlockSpec(memory_space=pl.ANY)


def coords():
    dp = lax.axis_index("dp")
    ctx = lax.axis_index("context")
    t = lax.axis_index("tensor")
    return dp, ctx // 4, ctx % 4, t


def pick(dp, first, second):
    return first + dp * (second - first)


def remote(src, dst, send, recv, where):
    return pltpu.make_async_remote_copy(
        src_ref=src, dst_ref=dst, send_sem=send, recv_sem=recv, device_id=where, device_id_type=MESH_ID
    )


ZKINDS = ((3, 0), (3, 1), (1, 0), (1, 1), (2, 0), (2, 1))


class WeightGather:
    def __init__(self, w_in, w_out, send, recv, hold, local_sem):
        self.w_in, self.w_out, self.send, self.recv = w_in, w_out, send, recv
        self.hold, self.local_sem = hold, local_sem
        dp, y, x, t = coords()
        self.dp, self.t = dp, t
        u, w = pick(dp, x, y), pick(dp, y, x)
        self.q = (u + 2 * w) % 4
        self.sib_q = (w + 2 * u) % 4
        self.shard = w_in.shape[0]
        self.piece = self.shard // 16
        xp, xm, yp, ym = (x + 1) % 4, (x + 3) % 4, (y + 1) % 4, (y + 3) % 4
        self.up = {"context": pick(dp, y * 4 + xp, yp * 4 + x)}
        self.um = {"context": pick(dp, y * 4 + xm, ym * 4 + x)}
        self.wp = {"context": pick(dp, yp * 4 + x, y * 4 + xp)}
        self.wm = {"context": pick(dp, ym * 4 + x, y * 4 + xm)}
        self.zp = {"tensor": (t + 1) % 4}
        self.zm = {"tensor": (t + 3) % 4}
        self.sib = {"dp": 1 - dp}
        self.pending = []

    def unit(self, z, dp, q, h):
        start = z * self.shard + dp * (self.shard // 2) + q * (2 * self.piece) + h * self.piece
        return self.w_out.at[pl.ds(pl.multiple_of(start, self.piece), self.piece), :]

    def own(self, h):
        start = self.dp * (self.shard // 2) + self.q * (2 * self.piece) + h * self.piece
        return self.w_in.at[pl.ds(pl.multiple_of(start, self.piece), self.piece), :]

    def go(self, src, dst, recv_at, where):
        at = len(self.pending)
        copy = remote(src, dst, self.send.at[at], self.recv.at[recv_at], where)
        copy.start()
        self.pending.append(copy)

    def arrived(self, dst, recv_at):
        remote(dst, dst, self.send.at[0], self.recv.at[recv_at], self.sib).wait_recv()

    def start(self):
        self.load = pltpu.make_async_copy(self.w_in, self.hold, self.local_sem.at[0])
        self.load.start()
        for h in (0, 1):
            dst = self.unit(self.t, self.dp, self.q, h)
            first, second = ((self.zp, 0 + h), (self.zm, 2 + h))
            if h == 0:
                self.go(self.own(h), dst, first[1], first[0])
                self.go(self.own(1), self.unit(self.t, self.dp, self.q, 1), 3, self.zm)
            else:
                self.go(self.own(1), dst, 1, self.zp)
                self.go(self.own(0), self.unit(self.t, self.dp, self.q, 0), 2, self.zm)

    def keep(self):
        row = pl.multiple_of(self.t * self.shard, self.shard)
        self.load.wait()
        self.local = pltpu.make_async_copy(self.hold, self.w_out.at[pl.ds(row, self.shard), :], self.local_sem.at[1])
        self.local.start()

    def z_step(self, kind):
        zoff, h = ZKINDS[kind]
        ref = self.unit((self.t + zoff) % 4, self.dp, self.q, h)
        self.arrived(ref, kind)
        if kind == 0:
            self.go(ref, ref, 4, self.zp)
        if kind == 3:
            self.go(ref, ref, 5, self.zm)
        self.go(ref, ref, 6 + kind, self.up)
        self.go(ref, ref, 12 + kind, self.um)
        self.go(ref, ref, 18 + kind, self.wp if h == 0 else self.wm)
        self.go(ref, ref, 24 + kind, self.sib)

    def plane_ref(self, side, kind, dp, q):
        zoff, h = ZKINDS[kind]
        qoff = (3, 1, 2)[side]
        return self.unit((self.t + zoff) % 4, dp, (q + qoff) % 4, h)

    def plane_step(self, side, kind):
        at = 6 + 6 * side + kind
        ref = self.plane_ref(side, kind, self.dp, self.q)
        self.arrived(ref, at)
        self.go(ref, ref, 24 + at, self.sib)

    def finish(self):
        for kind in range(6):
            zoff, h = ZKINDS[kind]
            self.arrived(self.unit((self.t + zoff) % 4, 1 - self.dp, self.sib_q, h), 24 + kind)
            for side in range(3):
                self.arrived(self.plane_ref(side, kind, 1 - self.dp, self.sib_q), 30 + 6 * side + kind)
        for copy in self.pending:
            copy.wait_send()
        self.local.wait()


KIND_ORDER = (0, 3, 1, 2, 4, 5)
N_SENDS = 6 + 18 + 24


def code_rows(shape):
    k = lax.broadcasted_iota(jnp.int32, shape, 0) % 4
    return jnp.where(k < 2, jnp.where(k == 0, CODES[0], CODES[1]), jnp.where(k == 2, CODES[2], CODES[3]))


def hyena_kernel(ids_ref, order_ref, emb_ref, gain_hbm, proj_ref, short_hbm, taps_ref, skip_hbm, wh_ref,
                 mix_ref, hot_out, wh_out,
                 gain_ref, short_ref, skip_ref, ids_all, tab_all, taps_all, hots, proj_s, hold,
                 s_w, r_w, loc_w, s_ids, r_ids, s_tab, r_tab, s_taps, r_taps, p_sem, a_sem):
    dp, y, x, t = coords()
    ctx = y * 4 + x
    loads = [pltpu.make_async_copy(proj_ref.at[j], proj_s.at[j], p_sem.at[j]) for j in range(3)]
    small_loads = [
        pltpu.make_async_copy(gain_hbm, gain_ref, a_sem.at[0]),
        pltpu.make_async_copy(short_hbm, short_ref, a_sem.at[1]),
        pltpu.make_async_copy(skip_hbm, skip_ref, a_sem.at[2]),
    ]
    for c in small_loads + loads:
        c.start()
    barrier = pltpu.get_barrier_semaphore()
    zs = [{"tensor": (t + d) % 4} for d in (1, 2, 3)]
    xs = [{"context": y * 4 + (x + d) % 4} for d in (1, 2, 3)]
    ys = [{"context": ((y + d) % 4) * 4 + x} for d in (1, 2, 3)]
    partners = zs + xs + ys + [{"dp": 1 - dp}]
    for where in partners:
        pl.semaphore_signal(barrier, inc=1, device_id=where, device_id_type=MESH_ID)
    mine = ctx * 4 + t
    ids_all[mine] = jnp.broadcast_to(ids_ref[...], (8, 128))
    trow = pl.ds(pl.multiple_of(t * 32, 32), 32)
    taps_all[trow, :] = taps_ref[...]
    pl.semaphore_wait(barrier, len(partners))

    small = []

    def go(src, send, recv, where):
        c = remote(src, src, send, recv, where)
        c.start()
        small.append(c)

    def landed(ref, recv):
        remote(ref, ref, s_ids.at[0], recv, zs[0]).wait_recv()

    gh = WeightGather(wh_ref, wh_out, s_w, r_w, hold, loc_w)
    for d in (0, 1, 2):
        go(ids_all.at[pl.ds(mine, 1)], s_ids.at[d], r_ids.at[d], zs[d])
    gh.start()
    for d in (0, 1, 2):
        go(taps_all.at[trow, :], s_taps.at[d], r_taps.at[d], zs[d])

    for c in small_loads:
        c.wait()
    wide = emb_ref[...].astype(F32)
    square = jnp.sum(wide * wide, axis=1, keepdims=True)
    normed = (wide * lax.rsqrt(square / 4096.0 + EPS) * gain_ref[...]).astype(BF16)
    cols = pl.ds(pl.multiple_of(t * 512, 512), 512)
    for j in range(3):
        loads[j].wait()
        rows = jnp.dot(normed, proj_s[j], preferred_element_type=F32).astype(BF16).astype(F32)
        rows = jnp.concatenate([rows[c - 64 : c - 63] for c in CODES], axis=0)
        last = jnp.broadcast_to(skip_ref[...], (4, 512))
        tab_all[j, :, cols] = jnp.concatenate([short_ref[j, tap : tap + 1, :] * rows for tap in range(3)] + [last], axis=0)
    for d in (0, 1, 2):
        go(tab_all.at[:, :, cols], s_tab.at[d], r_tab.at[d], zs[d])
    for d in (0, 1, 2):
        landed(ids_all.at[pl.ds(ctx * 4 + (t + 3 - d) % 4, 1)], r_ids.at[d])
    for d in (0, 1, 2):
        go(ids_all.at[pl.ds(ctx * 4, 4)], s_ids.at[3 + d], r_ids.at[3 + d], xs[d])
    gh.z_step(0)
    gh.z_step(3)
    for d in (0, 1, 2):
        landed(ids_all.at[pl.ds((y * 4 + (x + 3 - d) % 4) * 4, 4)], r_ids.at[3 + d])
    for d in (0, 1, 2):
        go(ids_all.at[pl.ds(y * 16, 16)], s_ids.at[6 + d], r_ids.at[6 + d], ys[d])
    gh.z_step(1)
    gh.z_step(2)
    gh.keep()
    for d in (0, 1, 2):
        landed(ids_all.at[pl.ds(((y + 3 - d) % 4) * 16, 16)], r_ids.at[6 + d])
        zrow = pl.ds(pl.multiple_of(((t + 3 - d) % 4) * 32, 32), 32)
        landed(taps_all.at[zrow, :], r_taps.at[d])
        landed(tab_all.at[:, :, pl.ds(pl.multiple_of(((t + 3 - d) % 4) * 512, 512), 512)], r_tab.at[d])

    row8 = lax.broadcasted_iota(jnp.int32, (8, 384), 0)
    code8 = code_rows((8, 384))
    for b in range(2):
        prev = [jnp.zeros((8, 128), jnp.int32) for _ in range(2)]
        for slot in range(32):
            hit = (order_ref[slot] == order_ref[2 * ctx + b] - 1).astype(jnp.int32)
            for half in range(2):
                prev[half] = prev[half] + hit * ids_all[2 * slot + half]
        own = [ids_all[ctx * 4 + 2 * b + half] for half in range(2)]
        line = jnp.concatenate(prev + own, axis=1)
        back = [line[:, 128:]] + [pltpu.roll(line, tap, 1)[:, 128:] for tap in (1, 2)]
        top = jnp.where(jnp.where(row8 < 4, back[0], back[1]) == code8, 1.0, 0.0)
        low = jnp.where(row8 < 4, jnp.where(back[2] == code8, 1.0, 0.0), 0.0)
        hots[b * 384 : (b + 1) * 384, :] = jnp.concatenate([top, low, top, low], axis=0).T.astype(BF16)
        lines = jnp.concatenate([line[:, 256:]] * 4, axis=0)
        wanted = lax.broadcasted_iota(jnp.int32, (32, 256), 0) + 64
        hot_out[b * 256 : (b + 1) * 256, :] = jnp.where(lines == wanted, 1.0, 0.0).T.astype(BF16)

    def chunk(i, _):
        lanes = pl.ds(pl.multiple_of(i * 128, 128), 128)
        table = jnp.concatenate([tab_all[j, :, lanes] for j in range(3)], axis=1)
        high = table.astype(BF16)
        low = (table - high.astype(F32)).astype(BF16)
        both = jnp.concatenate([high, low], axis=0)
        filtered = jnp.dot(hots[...], both, preferred_element_type=F32)
        gated = filtered[:, 128:256] * filtered[:, 256:384]
        g16 = gated.astype(BF16)
        window = jnp.concatenate(
            [g16[b * 384 + s * 128 : b * 384 + s * 128 + 256] for b in range(2) for s in range(2)], axis=1
        )
        lane_group = (lax.broadcasted_iota(jnp.int32, window.shape, 1) % 128) // 16
        taps = taps_all[pl.ds(pl.multiple_of(i * 8, 8), 8), :]
        total = jnp.zeros((128, 512), F32)
        for g in range(8):
            base = jnp.broadcast_to(taps[g : g + 1, :], (128, 256))
            toep = pltpu.roll(base, 0, 1, stride=1, stride_axis=0).astype(BF16)
            masked = jnp.where(lane_group == g, window, jnp.zeros_like(window))
            total = total + jnp.dot(toep, masked, preferred_element_type=F32)
        skip = tab_all[0, 12:13, lanes]
        for b in range(2):
            for s in range(2):
                at = b * 384 + 128 + s * 128
                part = total[:, (2 * b + s) * 128 : (2 * b + s + 1) * 128]
                mixed = filtered[at : at + 128, 0:128] * (part + skip * gated[at : at + 128])
                mix_ref[b * 256 + s * 128 : b * 256 + (s + 1) * 128, lanes] = mixed.astype(BF16)
        return 0

    lax.fori_loop(0, 4, chunk, 0)
    gh.z_step(4)
    gh.z_step(5)
    for n, k in enumerate(KIND_ORDER):
        lax.fori_loop(4 + 2 * n, 6 + 2 * n, chunk, 0)
        for side in range(3):
            gh.plane_step(side, k)
    gh.finish()
    for c in small:
        c.wait_send()


def hyena(ids, order, emb, gain, in_proj, short, taps, skip, wh):
    dma = pltpu.SemaphoreType.DMA
    vmem = pl.BlockSpec(memory_space=pltpu.VMEM)
    return pl.pallas_call(
        hyena_kernel,
        out_shape=(
            jax.ShapeDtypeStruct((512, 2048), BF16),
            jax.ShapeDtypeStruct((512, 32), BF16),
            jax.ShapeDtypeStruct((2048, 4096), BF16),
        ),
        in_specs=[vmem, pl.BlockSpec(memory_space=pltpu.SMEM), vmem, ANY, ANY, ANY, vmem, ANY, ANY],
        out_specs=(vmem, vmem, ANY),
        scratch_shapes=[
            pltpu.VMEM(gain.shape, F32),
            pltpu.VMEM(short.shape, F32),
            pltpu.VMEM(skip.shape, F32),
            pltpu.VMEM((64, 8, 128), jnp.int32),
            pltpu.VMEM((3, 16, 2048), F32),
            pltpu.VMEM((128, 256), F32),
            pltpu.VMEM((768, 32), BF16),
            pltpu.VMEM(in_proj.shape, BF16),
            pltpu.VMEM(wh.shape, BF16),
            dma((N_SENDS,)), dma((48,)), dma((2,)),
            dma((9,)), dma((9,)), dma((3,)), dma((3,)), dma((3,)), dma((3,)), dma((3,)), dma((3,)),
        ],
        compiler_params=pltpu.CompilerParams(
            collective_id=0, has_side_effects=True, vmem_limit_bytes=48 * 2**20
        ),
        name="hyena",
    )(ids, order, emb, gain, in_proj, short, taps, skip, wh)


def ab_of(dp, y, x):
    return pick(dp, y, x), pick(dp, x, y)


def ctx_of(dp, a, b):
    return pick(dp, a * 4 + b, b * 4 + a)


ORDER = (1, 3, 2)


def proj_kernel(mix_ref, wh_ref, code_ref, emb_ref, gain_ref, wq_ref, cos_ref, sin_ref,
                own_ref, q_out, kv_out, attn_in, chunk, squares, qkv, s1, r1, s2, r2, s3, r3, sq, rq, loc):
    i = pl.program_id(0)
    dp, y, x, t = coords()
    ctx = y * 4 + x
    a, b = ab_of(dp, y, x)
    others = [{"context": (ctx + d) % 16} for d in range(1, 16)]
    barrier = pltpu.get_barrier_semaphore()

    @pl.when(i == 0)
    def _():
        squares[...] = jnp.zeros_like(squares)
        for where in others:
            pl.semaphore_signal(barrier, inc=1, device_id=where, device_id_type=MESH_ID)

    @pl.when(i < 8)
    def _():
        vals = jnp.dot(mix_ref[...], wh_ref[...], preferred_element_type=F32)
        vals = vals + jnp.dot(code_ref[...], emb_ref[...], preferred_element_type=F32)
        chunk[...] = vals
        part = jnp.sum(vals * vals, axis=1, keepdims=True)
        squares[...] += jnp.broadcast_to(part, squares.shape)
        attn_in[:, pl.ds(pl.multiple_of(i * 512, 512), 512)] = (vals * gain_ref[...]).astype(BF16)
        own_ref[...] = chunk[pl.ds(pl.multiple_of(t * 128, 128), 128), :]

    @pl.when(i >= 8)
    def _():
        k = i - 8
        j = (k // 2 + 1) % 3
        factor = lax.rsqrt(squares[...] / 4096.0 + EPS)
        factor = factor * jnp.where(j == 0, HD**-0.5 * math.log2(math.e), 1.0).astype(F32)
        rotated = j < 2
        cos = jnp.where(rotated, cos_ref[...], 1.0) * factor
        sin = jnp.where(rotated, sin_ref[...], 0.0) * factor
        vals = jnp.dot(attn_in[...], wq_ref[0], preferred_element_type=F32)
        for hh in range(2):
            head = vals[:, hh * 128 : (hh + 1) * 128]
            turned = head * cos + pltpu.roll(head, 64, 1) * sin
            qkv[2 * (k % 2) + hh, j] = turned.astype(BF16).reshape(2, 4, 64, 128)

    bp = {"context": ctx_of(dp, a, (b + 1) % 4)}
    bm = {"context": ctx_of(dp, a, (b + 3) % 4)}

    def held(part, k, off):
        return kv_out.at[ctx_of(dp, (a + 4 - k) % 4, (b + off) % 4), part]

    def to_head(part, d):
        h = (a + d) % 4
        return remote(qkv.at[h, 1 + part], kv_out.at[ctx, part], s1.at[3 * part + d - 1], r1.at[3 * part + d - 1],
                      {"context": ctx_of(dp, h, b)})

    def spread(part, side, k):
        src = qkv.at[a, 1 + part] if k == 0 else held(part, k, 0)
        at = 8 * part + 4 * side + k
        return remote(src, held(part, k, 0), s2.at[at], r2.at[at], (bp, bm)[side])

    def relay(part, k):
        ref = held(part, k, (3, 1)[part])
        return remote(ref, ref, s3.at[4 * part + k], r3.at[4 * part + k], (bp, bm)[part])

    def query(d):
        to = (ctx + d) % 16
        h, s = ab_of(dp, to // 4, to % 4)
        return remote(qkv.at[h, 0, :, s], q_out.at[ctx], sq.at[d - 1], rq.at[d - 1], others[d - 1])

    def landed(ref, recv):
        remote(ref, ref, s1.at[0], recv, bp).wait_recv()

    keeps = [
        pltpu.make_async_copy(qkv.at[a, 1], kv_out.at[ctx, 0], loc.at[0]),
        pltpu.make_async_copy(qkv.at[a, 2], kv_out.at[ctx, 1], loc.at[1]),
        pltpu.make_async_copy(qkv.at[a, 0, :, b], q_out.at[ctx], loc.at[2]),
    ]

    def leave(part):
        for d in ORDER:
            to_head(part, d).start()
        for side in range(2):
            spread(part, side, 0).start()
        keeps[part].start()

    def pass_on(part):
        for d in ORDER:
            landed(held(part, d, 0), r1.at[3 * part + d - 1])
            for side in range(2):
                spread(part, side, d).start()

    @pl.when(i == 9)
    def _():
        pl.semaphore_wait(barrier, 15)
        leave(0)

    @pl.when(i == 11)
    def _():
        leave(1)
        pass_on(0)

    @pl.when(i == 13)
    def _():
        pass_on(1)
        keeps[2].start()
        for d in range(1, 16):
            query(d).start()
        for part in range(2):
            for k in (0,) + ORDER:
                landed(held(part, k, (3, 1)[part]), r2.at[8 * part + 4 * part + k])
                relay(part, k).start()
        for part in range(2):
            for k in (0,) + ORDER:
                landed(held(part, k, (1, 3)[part]), r2.at[8 * part + 4 * (1 - part) + k])
        for d in range(1, 16):
            landed(q_out.at[(ctx + 16 - d) % 16], rq.at[d - 1])
        for part in range(2):
            for k in (0,) + ORDER:
                landed(held(part, k, 2), r3.at[4 * part + k])
        for part in range(2):
            for d in ORDER:
                to_head(part, d).wait_send()
            for k in range(4):
                for side in range(2):
                    spread(part, side, k).wait_send()
                relay(part, k).wait_send()
        for d in range(1, 16):
            query(d).wait_send()
        for c in keeps:
            c.wait()


def stream_qkv(mix, wh, code_hot, emb4, gain, wq, cos, sin):
    dma = pltpu.SemaphoreType.DMA

    def whi(i):
        return (0, jnp.minimum(i, 7))

    def wqi(i):
        k = jnp.maximum(i - 8, 0)
        return ((k // 2 + 1) % 3, 0, k % 2)

    def whole(*shape):
        return pl.BlockSpec(shape, lambda i: (0,) * len(shape))

    return pl.pallas_call(
        proj_kernel,
        out_shape=(
            jax.ShapeDtypeStruct((128, 4096), F32),
            jax.ShapeDtypeStruct((16, 2, 64, 128), BF16),
            jax.ShapeDtypeStruct((16, 2, 2, 4, 64, 128), BF16),
        ),
        grid=(14,),
        in_specs=[
            whole(512, 2048),
            pl.BlockSpec((2048, 512), whi),
            whole(512, 32),
            pl.BlockSpec((32, 512), whi),
            pl.BlockSpec((1, 512), whi),
            pl.BlockSpec((1, 4096, 256), wqi),
            whole(512, 128),
            whole(512, 128),
        ],
        out_specs=(pl.BlockSpec((128, 512), whi), ANY, ANY),
        scratch_shapes=[
            pltpu.VMEM((512, 4096), BF16),
            pltpu.VMEM((512, 512), F32),
            pltpu.VMEM((512, 128), F32),
            pltpu.VMEM((4, 3, 2, 4, 64, 128), BF16),
            dma((6,)), dma((6,)), dma((16,)), dma((16,)), dma((8,)), dma((8,)), dma((15,)), dma((15,)), dma((3,)),
        ],
        compiler_params=pltpu.CompilerParams(
            collective_id=1, has_side_effects=True, vmem_limit_bytes=48 * 2**20
        ),
        name="stream_qkv",
    )(mix, wh, code_hot, emb4, gain, wq, cos, sin)


def attend_kernel(slot_ref, q_ref, kv_ref, o_ref):
    b = slot_ref[32]

    def q_tile(tile):
        parts = []
        for p in range(4 * tile, 4 * tile + 4):
            slot = slot_ref[p]
            parts.append(q_ref[slot // 2, slot % 2])
        return jnp.concatenate(parts, axis=0)

    def step(queries, carries, block, masked):
        slots = [slot_ref[block + n] for n in range(4)]
        keys = [kv_ref[s // 2, 0, s % 2] for s in slots]
        vals = [kv_ref[s // 2, 1, s % 2] for s in slots]
        scores = [
            [lax.dot_general(q, k, (((1,), (1,)), ((), ())), preferred_element_type=F32) for k in keys] for q in queries
        ]
        done = []
        for (top, tot, acc), score in zip(carries, scores):
            if masked:
                for n in range(4):
                    r = lax.broadcasted_iota(jnp.int32, (256, 256), 0)
                    col = lax.broadcasted_iota(jnp.int32, (256, 256), 1) + n * 256
                    score[n] = jnp.where(col <= (r // 64) * 256 + b * 64 + r % 64, score[n], NEG_FILL)
            most = functools.reduce(jnp.maximum, score)
            new = jnp.maximum(top, jnp.max(most, axis=1, keepdims=True))
            shrink = jnp.exp2(top - new)
            weights = [jnp.exp2(s - new) for s in score]
            tot = tot * shrink + jnp.sum(functools.reduce(jnp.add, weights), axis=1, keepdims=True)
            for n, (w, v) in enumerate(zip(weights, vals)):
                part = jnp.dot(w.astype(BF16), v, preferred_element_type=F32)
                add = part if n == 0 else add + part
            done.append((new, tot, acc * shrink + add))
        return tuple(done)

    start = (jnp.full((256, 1), NEG_FILL, F32), jnp.zeros((256, 1), F32), jnp.zeros((256, 128), F32))
    for j in range(0, 8, 2):
        q0, q1 = q_tile(j), q_tile(j + 1)
        c0 = step([q0], [start], 4 * j, True)[0]
        c1 = step([q1], [start], 4 * j + 4, True)[0]
        c1 = step([q1], [c1], 4 * j, False)[0]
        carries = (c0, c1)
        if j:
            carries = lax.fori_loop(0, j, lambda n, c: step([q0, q1], c, 4 * n, False), carries, unroll=2)
        for tile in range(2):
            _, tot, acc = carries[tile]
            out = (acc / tot).astype(BF16)
            for n in range(4):
                o_ref[4 * (j + tile) + n] = out[n * 64 : (n + 1) * 64]


def attend_return_kernel(slot_ref, q_hbm, kv_hbm, att_out, q_ref, kv_ref, o_pos, o_ref, send, recv, loc, kv_sem):
    dp, y, x, t = coords()
    ctx = y * 4 + x
    a, b = ab_of(dp, y, x)
    barrier = pltpu.get_barrier_semaphore()

    loads = [
        pltpu.make_async_copy(kv_hbm, kv_ref, kv_sem.at[0]),
        pltpu.make_async_copy(q_hbm, q_ref, kv_sem.at[1]),
    ]
    for c in loads:
        c.start()

    def source(n):
        st, sa, r = n // 8, (n // 2) % 4, n % 2
        return st, ctx_of(dp, sa, 2 * (t % 2) + r)

    def dest(n):
        return 2 * (n % 2) + b // 2, n // 2

    def hello(n, _):
        st, sc = source(n)

        @pl.when(jnp.logical_or(st != t, sc != ctx))
        def _():
            pl.semaphore_signal(barrier, inc=1, device_id={"context": sc, "tensor": st}, device_id_type=MESH_ID)

        return 0

    lax.fori_loop(0, 32, hello, 0)
    for c in loads:
        c.wait()
    attend_kernel(slot_ref, q_ref, kv_ref, o_pos)
    for slot in range(32):
        o_ref[slot] = o_pos[slot_ref[33 + slot]]
    has_self = (b // 2 == t % 2).astype(jnp.int32)
    pl.semaphore_wait(barrier, 32 - has_self)
    mine = (t * 4 + a) * 2 + b % 2

    def out_copy(n):
        dt, dc = dest(n)
        return remote(o_ref.at[n], att_out.at[mine], send.at[n], recv.at[mine], {"context": dc, "tensor": dt}), dt, dc

    def start(k, _):
        n = (k + 2 * ctx) % 32
        copy, dt, dc = out_copy(n)
        self_copy = jnp.logical_and(dt == t, dc == ctx)

        @pl.when(jnp.logical_not(self_copy))
        def _():
            copy.start()

        @pl.when(self_copy)
        def _():
            pltpu.make_async_copy(o_ref.at[n], att_out.at[mine], loc).start()

        return 0

    lax.fori_loop(0, 32, start, 0)

    def finish(n, _):
        st, sc = source(n)

        @pl.when(jnp.logical_or(st != t, sc != ctx))
        def _():
            ref = att_out.at[n]
            remote(ref, ref, send.at[0], recv.at[n], {"dp": 1 - dp}).wait_recv()

        copy, dt, dc = out_copy(n)
        self_copy = jnp.logical_and(dt == t, dc == ctx)

        @pl.when(jnp.logical_not(self_copy))
        def _():
            copy.wait_send()

        @pl.when(self_copy)
        def _():
            pltpu.make_async_copy(o_ref.at[n], att_out.at[mine], loc).wait()

        return 0

    lax.fori_loop(0, 32, finish, 0)


def attend_return(slots, q_all, kv_all):
    dma = pltpu.SemaphoreType.DMA
    return pl.pallas_call(
        attend_return_kernel,
        out_shape=jax.ShapeDtypeStruct((32, 64, 128), BF16),
        in_specs=[pl.BlockSpec(memory_space=pltpu.SMEM), ANY, ANY],
        out_specs=ANY,
        scratch_shapes=[
            pltpu.VMEM(q_all.shape, BF16), pltpu.VMEM(kv_all.shape, BF16),
            pltpu.VMEM((32, 64, 128), BF16), pltpu.VMEM((32, 64, 128), BF16), dma((32,)), dma((32,)), dma, dma((2,))
        ],
        compiler_params=pltpu.CompilerParams(
            collective_id=2, has_side_effects=True, vmem_limit_bytes=58 * 2**20
        ),
        name="attend_return",
    )(slots, q_all, kv_all)


def final_kernel(att_ref, wa_ref, own_ref, out_ref):
    rows = jnp.concatenate([att_ref[0], att_ref[1]], axis=1)

    @pl.when(pl.program_id(0) == 0)
    def _():
        out_ref[...] = own_ref[...]

    out_ref[...] += jnp.dot(rows, wa_ref[...], preferred_element_type=F32)


def final(att, wa, own):
    return pl.pallas_call(
        final_kernel,
        out_shape=jax.ShapeDtypeStruct((128, 4096), F32),
        grid=(8,),
        in_specs=[
            pl.BlockSpec((2, 128, 128), lambda i: (i, 0, 0)),
            pl.BlockSpec((256, 4096), lambda i: (i, 0)),
            pl.BlockSpec((128, 4096), lambda i: (0, 0)),
        ],
        out_specs=pl.BlockSpec((128, 4096), lambda i: (0, 0)),
        compiler_params=pltpu.CompilerParams(vmem_limit_bytes=58 * 2**20),
        name="final",
    )(att, wa, own)


def body(ids, block_order, embed, mix_gain, in_proj, short_filter, long_filter, conv_skip,
         hyena_out, attn_gain, qkv_proj, attn_out):
    dp, y, x, t = coords()
    ctx = y * 4 + x
    emb32 = lax.slice_in_dim(embed, 64, 96, axis=0)
    taps = jnp.concatenate(
        [jnp.zeros((32, 1), F32), long_filter[:, ::-1], jnp.zeros((32, 127), F32)], axis=1
    )
    slot_ids = jnp.arange(32, dtype=jnp.int32)
    pair = 2 * ctx + jnp.arange(2, dtype=jnp.int32)
    owned = jnp.sum(jnp.where(slot_ids[None] == pair[:, None], block_order[None], 0), axis=1)
    mix, code_hot, wh = hyena(
        ids.reshape(1, 128), block_order, emb32, mix_gain.reshape(1, -1), in_proj, short_filter, taps,
        conv_skip.reshape(1, -1), hyena_out
    )
    wa = lax.all_gather(
        lax.dynamic_slice_in_dim(attn_out, (dp * 16 + ctx) * 16, 16, 0), ("tensor", "dp", "context"), axis=0, tiled=True
    )

    local_pos = (owned[:, None] * 256 + jnp.arange(256, dtype=jnp.int32)[None]).reshape(512)
    inverse_freq = THETA ** (-(2.0 * jnp.arange(64, dtype=F32)) / HD)
    angles = local_pos.astype(F32)[:, None] * inverse_freq[None, :]
    cos, sin = jnp.cos(angles), jnp.sin(angles)
    cos = jnp.concatenate([cos, cos], axis=1)
    sin = jnp.concatenate([-sin, sin], axis=1)
    stream_own, q_all, kv_all = stream_qkv(
        mix, wh, code_hot, emb32, attn_gain.reshape(1, -1), qkv_proj, cos, sin
    )
    slot_of = jnp.sum(jnp.where(block_order[None, :] == slot_ids[:, None], slot_ids[None, :], 0), axis=1)
    _, b = ab_of(dp, y, x)
    slots = jnp.concatenate([slot_of, b.astype(jnp.int32).reshape(1), block_order])
    att = attend_return(slots, q_all, kv_all.reshape(16, 2, 2, 256, 128))
    return final(att.reshape(16, 128, 128), wa, stream_own)


def solution(mesh):
    placed = (
        P(("dp", "context", "tensor")),
        P("dp"),
        P(),
        P(),
        P(None, None, "tensor"),
        P(None, None, "tensor"),
        P("tensor", None),
        P("tensor"),
        P("tensor", None),
        P(),
        P(None, None, "tensor"),
        P("tensor", None),
    )
    return jax.shard_map(
        body,
        mesh=mesh,
        in_specs=placed,
        out_specs=P(("dp", "context", "tensor"), None),
        check_vma=False,
    )
```

```python
import functools
import math

import jax
import jax.numpy as jnp
from jax import lax
from jax.experimental import pallas as pl
from jax.experimental.pallas import tpu as pltpu
from jax.sharding import PartitionSpec as P

HD = 128
EPS = 1e-06
THETA = 1000000.0
NEG_FILL = -1e30
CODES = (65, 67, 71, 84)
MESH_ID = pl.DeviceIdType.MESH
F32 = jnp.float32
BF16 = jnp.bfloat16
ANY = pl.BlockSpec(memory_space=pl.ANY)


def coords():
    dp = lax.axis_index("dp")
    ctx = lax.axis_index("context")
    t = lax.axis_index("tensor")
    return dp, ctx // 4, ctx % 4, t


def pick(dp, first, second):
    return first + dp * (second - first)


def remote(src, dst, send, recv, where):
    return pltpu.make_async_remote_copy(
        src_ref=src, dst_ref=dst, send_sem=send, recv_sem=recv, device_id=where, device_id_type=MESH_ID
    )


ZKINDS = ((3, 0), (3, 1), (1, 0), (1, 1), (2, 0), (2, 1))


class WeightGather:
    def __init__(self, w_in, w_out, send, recv, hold, local_sem):
        self.w_in, self.w_out, self.send, self.recv = w_in, w_out, send, recv
        self.hold, self.local_sem = hold, local_sem
        dp, y, x, t = coords()
        self.dp, self.t = dp, t
        u, w = pick(dp, x, y), pick(dp, y, x)
        self.q = (u + 2 * w) % 4
        self.sib_q = (w + 2 * u) % 4
        self.shard = w_in.shape[0]
        self.piece = self.shard // 16
        xp, xm, yp, ym = (x + 1) % 4, (x + 3) % 4, (y + 1) % 4, (y + 3) % 4
        self.up = {"context": pick(dp, y * 4 + xp, yp * 4 + x)}
        self.um = {"context": pick(dp, y * 4 + xm, ym * 4 + x)}
        self.wp = {"context": pick(dp, yp * 4 + x, y * 4 + xp)}
        self.wm = {"context": pick(dp, ym * 4 + x, y * 4 + xm)}
        self.zp = {"tensor": (t + 1) % 4}
        self.zm = {"tensor": (t + 3) % 4}
        self.sib = {"dp": 1 - dp}
        self.pending = []

    def unit(self, z, dp, q, h):
        start = z * self.shard + dp * (self.shard // 2) + q * (2 * self.piece) + h * self.piece
        return self.w_out.at[pl.ds(pl.multiple_of(start, self.piece), self.piece), :]

    def own(self, h):
        start = self.dp * (self.shard // 2) + self.q * (2 * self.piece) + h * self.piece
        return self.w_in.at[pl.ds(pl.multiple_of(start, self.piece), self.piece), :]

    def go(self, src, dst, recv_at, where):
        at = len(self.pending)
        copy = remote(src, dst, self.send.at[at], self.recv.at[recv_at], where)
        copy.start()
        self.pending.append(copy)

    def arrived(self, dst, recv_at):
        remote(dst, dst, self.send.at[0], self.recv.at[recv_at], self.sib).wait_recv()

    def start(self):
        self.load = pltpu.make_async_copy(self.w_in, self.hold, self.local_sem.at[0])
        self.load.start()
        for h in (0, 1):
            dst = self.unit(self.t, self.dp, self.q, h)
            first, second = ((self.zp, 0 + h), (self.zm, 2 + h))
            if h == 0:
                self.go(self.own(h), dst, first[1], first[0])
                self.go(self.own(1), self.unit(self.t, self.dp, self.q, 1), 3, self.zm)
            else:
                self.go(self.own(1), dst, 1, self.zp)
                self.go(self.own(0), self.unit(self.t, self.dp, self.q, 0), 2, self.zm)

    def keep(self):
        row = pl.multiple_of(self.t * self.shard, self.shard)
        self.load.wait()
        self.local = pltpu.make_async_copy(self.hold, self.w_out.at[pl.ds(row, self.shard), :], self.local_sem.at[1])
        self.local.start()

    def z_step(self, kind):
        zoff, h = ZKINDS[kind]
        ref = self.unit((self.t + zoff) % 4, self.dp, self.q, h)
        self.arrived(ref, kind)
        if kind == 0:
            self.go(ref, ref, 4, self.zp)
        if kind == 3:
            self.go(ref, ref, 5, self.zm)
        self.go(ref, ref, 6 + kind, self.up)
        self.go(ref, ref, 12 + kind, self.um)
        self.go(ref, ref, 18 + kind, self.wp if h == 0 else self.wm)
        self.go(ref, ref, 24 + kind, self.sib)

    def plane_ref(self, side, kind, dp, q):
        zoff, h = ZKINDS[kind]
        qoff = (3, 1, 2)[side]
        return self.unit((self.t + zoff) % 4, dp, (q + qoff) % 4, h)

    def plane_step(self, side, kind):
        at = 6 + 6 * side + kind
        ref = self.plane_ref(side, kind, self.dp, self.q)
        self.arrived(ref, at)
        self.go(ref, ref, 24 + at, self.sib)

    def finish(self):
        for kind in range(6):
            zoff, h = ZKINDS[kind]
            self.arrived(self.unit((self.t + zoff) % 4, 1 - self.dp, self.sib_q, h), 24 + kind)
            for side in range(3):
                self.arrived(self.plane_ref(side, kind, 1 - self.dp, self.sib_q), 30 + 6 * side + kind)
        for copy in self.pending:
            copy.wait_send()
        self.local.wait()


KIND_ORDER = (0, 3, 1, 2, 4, 5)
N_SENDS = 6 + 18 + 24


def code_rows(shape):
    k = lax.broadcasted_iota(jnp.int32, shape, 0) % 4
    return jnp.where(k < 2, jnp.where(k == 0, CODES[0], CODES[1]), jnp.where(k == 2, CODES[2], CODES[3]))


def hyena_kernel(ids_ref, order_ref, emb_ref, gain_hbm, proj_ref, short_hbm, taps_ref, skip_hbm, wh_ref,
                 mix_ref, hot_out, wh_out,
                 gain_ref, short_ref, skip_ref, ids_all, tab_all, taps_all, hots, proj_s, hold,
                 s_w, r_w, loc_w, s_ids, r_ids, s_tab, r_tab, s_taps, r_taps, p_sem, a_sem):
    dp, y, x, t = coords()
    ctx = y * 4 + x
    loads = [pltpu.make_async_copy(proj_ref.at[j], proj_s.at[j], p_sem.at[j]) for j in range(3)]
    small_loads = [
        pltpu.make_async_copy(gain_hbm, gain_ref, a_sem.at[0]),
        pltpu.make_async_copy(short_hbm, short_ref, a_sem.at[1]),
        pltpu.make_async_copy(skip_hbm, skip_ref, a_sem.at[2]),
    ]
    for c in small_loads + loads:
        c.start()
    barrier = pltpu.get_barrier_semaphore()
    zs = [{"tensor": (t + d) % 4} for d in (1, 2, 3)]
    xs = [{"context": y * 4 + (x + d) % 4} for d in (1, 2, 3)]
    ys = [{"context": ((y + d) % 4) * 4 + x} for d in (1, 2, 3)]
    partners = zs + xs + ys + [{"dp": 1 - dp}]
    for where in partners:
        pl.semaphore_signal(barrier, inc=1, device_id=where, device_id_type=MESH_ID)
    mine = ctx * 4 + t
    ids_all[mine] = jnp.broadcast_to(ids_ref[...], (8, 128))
    trow = pl.ds(pl.multiple_of(t * 32, 32), 32)
    taps_all[trow, :] = taps_ref[...]
    pl.semaphore_wait(barrier, len(partners))

    small = []

    def go(src, send, recv, where):
        c = remote(src, src, send, recv, where)
        c.start()
        small.append(c)

    def landed(ref, recv):
        remote(ref, ref, s_ids.at[0], recv, zs[0]).wait_recv()

    gh = WeightGather(wh_ref, wh_out, s_w, r_w, hold, loc_w)
    for d in (0, 1, 2):
        go(ids_all.at[pl.ds(mine, 1)], s_ids.at[d], r_ids.at[d], zs[d])
    gh.start()
    for d in (0, 1, 2):
        go(taps_all.at[trow, :], s_taps.at[d], r_taps.at[d], zs[d])

    for c in small_loads:
        c.wait()
    wide = emb_ref[...].astype(F32)
    square = jnp.sum(wide * wide, axis=1, keepdims=True)
    normed = (wide * lax.rsqrt(square / 4096.0 + EPS) * gain_ref[...]).astype(BF16)
    cols = pl.ds(pl.multiple_of(t * 512, 512), 512)
    for j in range(3):
        loads[j].wait()
        rows = jnp.dot(normed, proj_s[j], preferred_element_type=F32).astype(BF16).astype(F32)
        rows = jnp.concatenate([rows[c - 64 : c - 63] for c in CODES], axis=0)
        last = jnp.broadcast_to(skip_ref[...], (4, 512))
        tab_all[j, :, cols] = jnp.concatenate([short_ref[j, tap : tap + 1, :] * rows for tap in range(3)] + [last], axis=0)
    for d in (0, 1, 2):
        go(tab_all.at[:, :, cols], s_tab.at[d], r_tab.at[d], zs[d])
    for d in (0, 1, 2):
        landed(ids_all.at[pl.ds(ctx * 4 + (t + 3 - d) % 4, 1)], r_ids.at[d])
    for d in (0, 1, 2):
        go(ids_all.at[pl.ds(ctx * 4, 4)], s_ids.at[3 + d], r_ids.at[3 + d], xs[d])
    gh.z_step(0)
    gh.z_step(3)
    for d in (0, 1, 2):
        landed(ids_all.at[pl.ds((y * 4 + (x + 3 - d) % 4) * 4, 4)], r_ids.at[3 + d])
    for d in (0, 1, 2):
        go(ids_all.at[pl.ds(y * 16, 16)], s_ids.at[6 + d], r_ids.at[6 + d], ys[d])
    gh.z_step(1)
    gh.z_step(2)
    gh.keep()
    for d in (0, 1, 2):
        landed(ids_all.at[pl.ds(((y + 3 - d) % 4) * 16, 16)], r_ids.at[6 + d])
        zrow = pl.ds(pl.multiple_of(((t + 3 - d) % 4) * 32, 32), 32)
        landed(taps_all.at[zrow, :], r_taps.at[d])
        landed(tab_all.at[:, :, pl.ds(pl.multiple_of(((t + 3 - d) % 4) * 512, 512), 512)], r_tab.at[d])

    row8 = lax.broadcasted_iota(jnp.int32, (8, 384), 0)
    code8 = code_rows((8, 384))
    for b in range(2):
        prev = [jnp.zeros((8, 128), jnp.int32) for _ in range(2)]
        for slot in range(32):
            hit = (order_ref[slot] == order_ref[2 * ctx + b] - 1).astype(jnp.int32)
            for half in range(2):
                prev[half] = prev[half] + hit * ids_all[2 * slot + half]
        own = [ids_all[ctx * 4 + 2 * b + half] for half in range(2)]
        line = jnp.concatenate(prev + own, axis=1)
        back = [line[:, 128:]] + [pltpu.roll(line, tap, 1)[:, 128:] for tap in (1, 2)]
        top = jnp.where(jnp.where(row8 < 4, back[0], back[1]) == code8, 1.0, 0.0)
        low = jnp.where(row8 < 4, jnp.where(back[2] == code8, 1.0, 0.0), 0.0)
        hots[b * 384 : (b + 1) * 384, :] = jnp.concatenate([top, low, top, low], axis=0).T.astype(BF16)
        lines = jnp.concatenate([line[:, 256:]] * 4, axis=0)
        wanted = lax.broadcasted_iota(jnp.int32, (32, 256), 0) + 64
        hot_out[b * 256 : (b + 1) * 256, :] = jnp.where(lines == wanted, 1.0, 0.0).T.astype(BF16)

    def chunk(i, _):
        lanes = pl.ds(pl.multiple_of(i * 128, 128), 128)
        table = jnp.concatenate([tab_all[j, :, lanes] for j in range(3)], axis=1)
        high = table.astype(BF16)
        low = (table - high.astype(F32)).astype(BF16)
        both = jnp.concatenate([high, low], axis=0)
        filtered = jnp.dot(hots[...], both, preferred_element_type=F32)
        gated = filtered[:, 128:256] * filtered[:, 256:384]
        g16 = gated.astype(BF16)
        window = jnp.concatenate(
            [g16[b * 384 + s * 128 : b * 384 + s * 128 + 256] for b in range(2) for s in range(2)], axis=1
        )
        lane_group = (lax.broadcasted_iota(jnp.int32, window.shape, 1) % 128) // 16
        taps = taps_all[pl.ds(pl.multiple_of(i * 8, 8), 8), :]
        total = jnp.zeros((128, 512), F32)
        for g in range(8):
            base = jnp.broadcast_to(taps[g : g + 1, :], (128, 256))
            toep = pltpu.roll(base, 0, 1, stride=1, stride_axis=0).astype(BF16)
            masked = jnp.where(lane_group == g, window, jnp.zeros_like(window))
            total = total + jnp.dot(toep, masked, preferred_element_type=F32)
        skip = tab_all[0, 12:13, lanes]
        for b in range(2):
            for s in range(2):
                at = b * 384 + 128 + s * 128
                part = total[:, (2 * b + s) * 128 : (2 * b + s + 1) * 128]
                mixed = filtered[at : at + 128, 0:128] * (part + skip * gated[at : at + 128])
                mix_ref[b * 256 + s * 128 : b * 256 + (s + 1) * 128, lanes] = mixed.astype(BF16)
        return 0

    lax.fori_loop(0, 4, chunk, 0)
    gh.z_step(4)
    gh.z_step(5)
    for n, k in enumerate(KIND_ORDER):
        lax.fori_loop(4 + 2 * n, 6 + 2 * n, chunk, 0)
        for side in range(3):
            gh.plane_step(side, k)
    gh.finish()
    for c in small:
        c.wait_send()


def hyena(ids, order, emb, gain, in_proj, short, taps, skip, wh):
    dma = pltpu.SemaphoreType.DMA
    vmem = pl.BlockSpec(memory_space=pltpu.VMEM)
    return pl.pallas_call(
        hyena_kernel,
        out_shape=(
            jax.ShapeDtypeStruct((512, 2048), BF16),
            jax.ShapeDtypeStruct((512, 32), BF16),
            jax.ShapeDtypeStruct((2048, 4096), BF16),
        ),
        in_specs=[vmem, pl.BlockSpec(memory_space=pltpu.SMEM), vmem, ANY, ANY, ANY, vmem, ANY, ANY],
        out_specs=(vmem, vmem, ANY),
        scratch_shapes=[
            pltpu.VMEM(gain.shape, F32),
            pltpu.VMEM(short.shape, F32),
            pltpu.VMEM(skip.shape, F32),
            pltpu.VMEM((64, 8, 128), jnp.int32),
            pltpu.VMEM((3, 16, 2048), F32),
            pltpu.VMEM((128, 256), F32),
            pltpu.VMEM((768, 32), BF16),
            pltpu.VMEM(in_proj.shape, BF16),
            pltpu.VMEM(wh.shape, BF16),
            dma((N_SENDS,)), dma((48,)), dma((2,)),
            dma((9,)), dma((9,)), dma((3,)), dma((3,)), dma((3,)), dma((3,)), dma((3,)), dma((3,)),
        ],
        compiler_params=pltpu.CompilerParams(
            collective_id=0, has_side_effects=True, vmem_limit_bytes=48 * 2**20
        ),
        name="hyena",
    )(ids, order, emb, gain, in_proj, short, taps, skip, wh)


def ab_of(dp, y, x):
    return pick(dp, y, x), pick(dp, x, y)


def ctx_of(dp, a, b):
    return pick(dp, a * 4 + b, b * 4 + a)


ORDER = (1, 3, 2)


def proj_kernel(mix_ref, wh_ref, code_ref, emb_ref, gain_ref, wq_ref, cos_ref, sin_ref,
                own_ref, q_out, kv_out, attn_in, chunk, squares, qkv, s1, r1, s2, r2, s3, r3, sq, rq, loc):
    i = pl.program_id(0)
    dp, y, x, t = coords()
    ctx = y * 4 + x
    a, b = ab_of(dp, y, x)
    others = [{"context": (ctx + d) % 16} for d in range(1, 16)]
    barrier = pltpu.get_barrier_semaphore()

    @pl.when(i == 0)
    def _():
        squares[...] = jnp.zeros_like(squares)
        for where in others:
            pl.semaphore_signal(barrier, inc=1, device_id=where, device_id_type=MESH_ID)

    @pl.when(i < 8)
    def _():
        vals = jnp.dot(mix_ref[...], wh_ref[...], preferred_element_type=F32)
        vals = vals + jnp.dot(code_ref[...], emb_ref[...], preferred_element_type=F32)
        chunk[...] = vals
        part = jnp.sum(vals * vals, axis=1, keepdims=True)
        squares[...] += jnp.broadcast_to(part, squares.shape)
        attn_in[:, pl.ds(pl.multiple_of(i * 512, 512), 512)] = (vals * gain_ref[...]).astype(BF16)
        own_ref[...] = chunk[pl.ds(pl.multiple_of(t * 128, 128), 128), :]

    @pl.when(i >= 8)
    def _():
        k = i - 8
        j = (k // 2 + 1) % 3
        factor = lax.rsqrt(squares[...] / 4096.0 + EPS)
        factor = factor * jnp.where(j == 0, HD**-0.5 * math.log2(math.e), 1.0).astype(F32)
        rotated = j < 2
        cos = jnp.where(rotated, cos_ref[...], 1.0) * factor
        sin = jnp.where(rotated, sin_ref[...], 0.0) * factor
        vals = jnp.dot(attn_in[...], wq_ref[0], preferred_element_type=F32)
        for hh in range(2):
            head = vals[:, hh * 128 : (hh + 1) * 128]
            turned = head * cos + pltpu.roll(head, 64, 1) * sin
            qkv[2 * (k % 2) + hh, j] = turned.astype(BF16).reshape(2, 4, 64, 128)

    bp = {"context": ctx_of(dp, a, (b + 1) % 4)}
    bm = {"context": ctx_of(dp, a, (b + 3) % 4)}

    def held(part, k, off):
        return kv_out.at[ctx_of(dp, (a + 4 - k) % 4, (b + off) % 4), part]

    def to_head(part, d):
        h = (a + d) % 4
        return remote(qkv.at[h, 1 + part], kv_out.at[ctx, part], s1.at[3 * part + d - 1], r1.at[3 * part + d - 1],
                      {"context": ctx_of(dp, h, b)})

    def spread(part, side, k):
        src = qkv.at[a, 1 + part] if k == 0 else held(part, k, 0)
        at = 8 * part + 4 * side + k
        return remote(src, held(part, k, 0), s2.at[at], r2.at[at], (bp, bm)[side])

    def relay(part, k):
        ref = held(part, k, (3, 1)[part])
        return remote(ref, ref, s3.at[4 * part + k], r3.at[4 * part + k], (bp, bm)[part])

    def query(d):
        to = (ctx + d) % 16
        h, s = ab_of(dp, to // 4, to % 4)
        return remote(qkv.at[h, 0, :, s], q_out.at[ctx], sq.at[d - 1], rq.at[d - 1], others[d - 1])

    def landed(ref, recv):
        remote(ref, ref, s1.at[0], recv, bp).wait_recv()

    keeps = [
        pltpu.make_async_copy(qkv.at[a, 1], kv_out.at[ctx, 0], loc.at[0]),
        pltpu.make_async_copy(qkv.at[a, 2], kv_out.at[ctx, 1], loc.at[1]),
        pltpu.make_async_copy(qkv.at[a, 0, :, b], q_out.at[ctx], loc.at[2]),
    ]

    def leave(part):
        for d in ORDER:
            to_head(part, d).start()
        for side in range(2):
            spread(part, side, 0).start()
        keeps[part].start()

    def pass_on(part):
        for d in ORDER:
            landed(held(part, d, 0), r1.at[3 * part + d - 1])
            for side in range(2):
                spread(part, side, d).start()

    @pl.when(i == 9)
    def _():
        pl.semaphore_wait(barrier, 15)
        leave(0)

    @pl.when(i == 11)
    def _():
        leave(1)
        pass_on(0)

    @pl.when(i == 13)
    def _():
        pass_on(1)
        keeps[2].start()
        for d in range(1, 16):
            query(d).start()
        for part in range(2):
            for k in (0,) + ORDER:
                landed(held(part, k, (3, 1)[part]), r2.at[8 * part + 4 * part + k])
                relay(part, k).start()
        for part in range(2):
            for k in (0,) + ORDER:
                landed(held(part, k, (1, 3)[part]), r2.at[8 * part + 4 * (1 - part) + k])
        for d in range(1, 16):
            landed(q_out.at[(ctx + 16 - d) % 16], rq.at[d - 1])
        for part in range(2):
            for k in (0,) + ORDER:
                landed(held(part, k, 2), r3.at[4 * part + k])
        for part in range(2):
            for d in ORDER:
                to_head(part, d).wait_send()
            for k in range(4):
                for side in range(2):
                    spread(part, side, k).wait_send()
                relay(part, k).wait_send()
        for d in range(1, 16):
            query(d).wait_send()
        for c in keeps:
            c.wait()


def stream_qkv(mix, wh, code_hot, emb4, gain, wq, cos, sin):
    dma = pltpu.SemaphoreType.DMA

    def whi(i):
        return (0, jnp.minimum(i, 7))

    def wqi(i):
        k = jnp.maximum(i - 8, 0)
        return ((k // 2 + 1) % 3, 0, k % 2)

    def whole(*shape):
        return pl.BlockSpec(shape, lambda i: (0,) * len(shape))

    return pl.pallas_call(
        proj_kernel,
        out_shape=(
            jax.ShapeDtypeStruct((128, 4096), F32),
            jax.ShapeDtypeStruct((16, 2, 64, 128), BF16),
            jax.ShapeDtypeStruct((16, 2, 2, 4, 64, 128), BF16),
        ),
        grid=(14,),
        in_specs=[
            whole(512, 2048),
            pl.BlockSpec((2048, 512), whi),
            whole(512, 32),
            pl.BlockSpec((32, 512), whi),
            pl.BlockSpec((1, 512), whi),
            pl.BlockSpec((1, 4096, 256), wqi),
            whole(512, 128),
            whole(512, 128),
        ],
        out_specs=(pl.BlockSpec((128, 512), whi), ANY, ANY),
        scratch_shapes=[
            pltpu.VMEM((512, 4096), BF16),
            pltpu.VMEM((512, 512), F32),
            pltpu.VMEM((512, 128), F32),
            pltpu.VMEM((4, 3, 2, 4, 64, 128), BF16),
            dma((6,)), dma((6,)), dma((16,)), dma((16,)), dma((8,)), dma((8,)), dma((15,)), dma((15,)), dma((3,)),
        ],
        compiler_params=pltpu.CompilerParams(
            collective_id=1, has_side_effects=True, vmem_limit_bytes=48 * 2**20
        ),
        name="stream_qkv",
    )(mix, wh, code_hot, emb4, gain, wq, cos, sin)


def attend_kernel(slot_ref, q_ref, kv_ref, o_ref):
    b = slot_ref[32]

    def q_tile(tile):
        parts = []
        for p in range(4 * tile, 4 * tile + 4):
            slot = slot_ref[p]
            parts.append(q_ref[slot // 2, slot % 2])
        return jnp.concatenate(parts, axis=0)

    def step(queries, carries, block, masked):
        slots = [slot_ref[block + n] for n in range(4)]
        keys = [kv_ref[s // 2, 0, s % 2] for s in slots]
        vals = [kv_ref[s // 2, 1, s % 2] for s in slots]
        scores = [
            [lax.dot_general(q, k, (((1,), (1,)), ((), ())), preferred_element_type=F32) for k in keys] for q in queries
        ]
        done = []
        for (top, tot, acc), score in zip(carries, scores):
            if masked:
                for n in range(4):
                    r = lax.broadcasted_iota(jnp.int32, (256, 256), 0)
                    col = lax.broadcasted_iota(jnp.int32, (256, 256), 1) + n * 256
                    score[n] = jnp.where(col <= (r // 64) * 256 + b * 64 + r % 64, score[n], NEG_FILL)
            most = functools.reduce(jnp.maximum, score)
            new = jnp.maximum(top, jnp.max(most, axis=1, keepdims=True))
            shrink = jnp.exp2(top - new)
            weights = [jnp.exp2(s - new) for s in score]
            tot = tot * shrink + jnp.sum(functools.reduce(jnp.add, weights), axis=1, keepdims=True)
            for n, (w, v) in enumerate(zip(weights, vals)):
                part = jnp.dot(w.astype(BF16), v, preferred_element_type=F32)
                add = part if n == 0 else add + part
            done.append((new, tot, acc * shrink + add))
        return tuple(done)

    start = (jnp.full((256, 1), NEG_FILL, F32), jnp.zeros((256, 1), F32), jnp.zeros((256, 128), F32))
    for j in range(0, 8, 2):
        q0, q1 = q_tile(j), q_tile(j + 1)
        c0 = step([q0], [start], 4 * j, True)[0]
        c1 = step([q1], [start], 4 * j + 4, True)[0]
        c1 = step([q1], [c1], 4 * j, False)[0]
        carries = (c0, c1)
        if j:
            carries = lax.fori_loop(0, j, lambda n, c: step([q0, q1], c, 4 * n, False), carries, unroll=2)
        for tile in range(2):
            _, tot, acc = carries[tile]
            out = (acc / tot).astype(BF16)
            for n in range(4):
                o_ref[4 * (j + tile) + n] = out[n * 64 : (n + 1) * 64]


def attend_return_kernel(slot_ref, q_ref, kv_ref, wa_hbm, own_ref, out_ref, att_out, wa_ref, rows_ref, o_pos, o_ref,
                         send, recv, loc, wa_sem):
    dp, y, x, t = coords()
    ctx = y * 4 + x
    a, b = ab_of(dp, y, x)
    barrier = pltpu.get_barrier_semaphore()

    wa_load = pltpu.make_async_copy(wa_hbm, wa_ref, wa_sem)
    wa_load.start()

    def source(n):
        st, sa, r = n // 8, (n // 2) % 4, n % 2
        return st, ctx_of(dp, sa, 2 * (t % 2) + r)

    def dest(n):
        return 2 * (n % 2) + b // 2, n // 2

    def hello(n, _):
        st, sc = source(n)

        @pl.when(jnp.logical_or(st != t, sc != ctx))
        def _():
            pl.semaphore_signal(barrier, inc=1, device_id={"context": sc, "tensor": st}, device_id_type=MESH_ID)

        return 0

    lax.fori_loop(0, 32, hello, 0)
    attend_kernel(slot_ref, q_ref, kv_ref, o_pos)
    for slot in range(32):
        o_ref[slot] = o_pos[slot_ref[33 + slot]]
    has_self = (b // 2 == t % 2).astype(jnp.int32)
    pl.semaphore_wait(barrier, 32 - has_self)
    mine = (t * 4 + a) * 2 + b % 2

    def out_copy(n):
        dt, dc = dest(n)
        return remote(o_ref.at[n], att_out.at[mine], send.at[n], recv.at[mine], {"context": dc, "tensor": dt}), dt, dc

    def start(k, _):
        n = (k + 2 * ctx) % 32
        copy, dt, dc = out_copy(n)
        self_copy = jnp.logical_and(dt == t, dc == ctx)

        @pl.when(jnp.logical_not(self_copy))
        def _():
            copy.start()

        @pl.when(self_copy)
        def _():
            pltpu.make_async_copy(o_ref.at[n], att_out.at[mine], loc).start()

        return 0

    lax.fori_loop(0, 32, start, 0)

    def finish(n, _):
        st, sc = source(n)

        @pl.when(jnp.logical_or(st != t, sc != ctx))
        def _():
            ref = att_out.at[n]
            remote(ref, ref, send.at[0], recv.at[n], {"dp": 1 - dp}).wait_recv()

        copy, dt, dc = out_copy(n)
        self_copy = jnp.logical_and(dt == t, dc == ctx)

        @pl.when(jnp.logical_not(self_copy))
        def _():
            copy.wait_send()

        @pl.when(self_copy)
        def _():
            pltpu.make_async_copy(o_ref.at[n], att_out.at[mine], loc).wait()

        return 0

    lax.fori_loop(0, 32, finish, 0)
    wa_load.wait()
    for head in range(16):
        for r in range(2):
            rows_ref[r * 64 : (r + 1) * 64, head * 128 : (head + 1) * 128] = att_out[2 * head + r]

    def tile(n, _):
        lanes = pl.ds(pl.multiple_of(n * 512, 512), 512)
        out_ref[:, lanes] = own_ref[:, lanes] + jnp.dot(rows_ref[...], wa_ref[:, lanes], preferred_element_type=F32)
        return 0

    lax.fori_loop(0, 8, tile, 0)


def attend_return(slots, q_all, kv_all, wa, own):
    dma = pltpu.SemaphoreType.DMA
    vmem = pl.BlockSpec(memory_space=pltpu.VMEM)
    return pl.pallas_call(
        attend_return_kernel,
        out_shape=jax.ShapeDtypeStruct((128, 4096), F32),
        in_specs=[pl.BlockSpec(memory_space=pltpu.SMEM), vmem, vmem, ANY, vmem],
        out_specs=vmem,
        scratch_shapes=[
            pltpu.VMEM((32, 64, 128), BF16), pltpu.VMEM(wa.shape, BF16), pltpu.VMEM((128, 2048), BF16),
            pltpu.VMEM((32, 64, 128), BF16), pltpu.VMEM((32, 64, 128), BF16), dma((32,)), dma((32,)), dma, dma
        ],
        compiler_params=pltpu.CompilerParams(
            collective_id=2, has_side_effects=True, vmem_limit_bytes=48 * 2**20
        ),
        name="attend_return",
    )(slots, q_all, kv_all, wa, own)


def body(ids, block_order, embed, mix_gain, in_proj, short_filter, long_filter, conv_skip,
         hyena_out, attn_gain, qkv_proj, attn_out):
    dp, y, x, t = coords()
    ctx = y * 4 + x
    emb32 = lax.slice_in_dim(embed, 64, 96, axis=0)
    taps = jnp.concatenate(
        [jnp.zeros((32, 1), F32), long_filter[:, ::-1], jnp.zeros((32, 127), F32)], axis=1
    )
    slot_ids = jnp.arange(32, dtype=jnp.int32)
    pair = 2 * ctx + jnp.arange(2, dtype=jnp.int32)
    owned = jnp.sum(jnp.where(slot_ids[None] == pair[:, None], block_order[None], 0), axis=1)
    mix, code_hot, wh = hyena(
        ids.reshape(1, 128), block_order, emb32, mix_gain.reshape(1, -1), in_proj, short_filter, taps,
        conv_skip.reshape(1, -1), hyena_out
    )
    wa = lax.all_gather(
        lax.dynamic_slice_in_dim(attn_out, (dp * 16 + ctx) * 16, 16, 0), ("tensor", "dp", "context"), axis=0, tiled=True
    )

    local_pos = (owned[:, None] * 256 + jnp.arange(256, dtype=jnp.int32)[None]).reshape(512)
    inverse_freq = THETA ** (-(2.0 * jnp.arange(64, dtype=F32)) / HD)
    angles = local_pos.astype(F32)[:, None] * inverse_freq[None, :]
    cos, sin = jnp.cos(angles), jnp.sin(angles)
    cos = jnp.concatenate([cos, cos], axis=1)
    sin = jnp.concatenate([-sin, sin], axis=1)
    stream_own, q_all, kv_all = stream_qkv(
        mix, wh, code_hot, emb32, attn_gain.reshape(1, -1), qkv_proj, cos, sin
    )
    wa, kv_all = lax.optimization_barrier((wa, kv_all))
    slot_of = jnp.sum(jnp.where(block_order[None, :] == slot_ids[:, None], slot_ids[None, :], 0), axis=1)
    _, b = ab_of(dp, y, x)
    slots = jnp.concatenate([slot_of, b.astype(jnp.int32).reshape(1), block_order])
    return attend_return(slots, q_all, kv_all.reshape(16, 2, 2, 256, 128), wa, stream_own)


def solution(mesh):
    placed = (
        P(("dp", "context", "tensor")),
        P("dp"),
        P(),
        P(),
        P(None, None, "tensor"),
        P(None, None, "tensor"),
        P("tensor", None),
        P("tensor"),
        P("tensor", None),
        P(),
        P(None, None, "tensor"),
        P("tensor", None),
    )
    return jax.shard_map(
        body,
        mesh=mesh,
        in_specs=placed,
        out_specs=P(("dp", "context", "tensor"), None),
        check_vma=False,
    )
```
